256 devices in a mesh: gz: 64 (over z, x, core), gy: 4 (over y).
Axes of the slice: x: 4, y: 4, z: 8, core: 2. Of those that a mesh axis runs over, the one named last changes fastest.
Arguments:
- pressure: float32 [512, 256, 256], P('gz', 'gy'), may hold values from -6 to 6
- velocity: float32 [3, 512, 256, 256], P(None, 'gz', 'gy'), may hold values from -6 to 6
- bulk: float32 [512, 256, 256], P('gz', 'gy'), may hold values from 0.15 to 0.6
- buoyancy: float32 [512, 256, 256], P('gz', 'gy'), may hold values from 0.15 to 0.6
- tiles: bfloat16 [2048, 16, 32, 32], P(('gz', 'gy')), may hold values from -3 to 3
- tile_corner: int32 [2048, 3], replicated, may hold values from 0 to 511, as said below
- live_count: int32 [256], replicated, may hold values from 1 to 8, 1024 in all
Outputs:
- new_pressure: float32 [512, 256, 256], P('gz', 'gy')
- new_velocity: float32 [3, 512, 256, 256], P(None, 'gz', 'gy')
The draws below stay inside these ranges and needn't reach their ends.
Inputs may be any that keep to these rules, and one draw needn't show every extreme that they name: `tile_corner`: row s belongs to slot s % 8 of device s // 8, devices numbered with gz major and gy minor. Its z0 lies in that device's own slab of 8 planes, its y0 in that device's own block of 64 rows; x0 is any column. `live_count`: entry d counts the live slots of device d (the first ones); later slots of that device are ignored.
All inputs are finite; a program needn't handle non-finite values.
Results may differ from the reference program's by a relative error of at most 0.0015.
Values may be sent and summed in bfloat16 or wider, within the bound.
No kernel may reach another device: no remote copies, remote signals or barrier semaphores. Data moves between devices by JAX's collectives and lax.ppermute only.
A program may use at most 64 MiB of HBM per device.

```python
import math
import jax
import jax.numpy as jnp
import numpy as np
from jax import lax

NX = 256
NY = 256
CZ = 8
TZ = 16
TY = 32
TX = 32
E_CAP = 8
ELEMENTS = 1024
SLOTS = 2048
NZ = 512
NY_DEV = 64
DEVICES = 256


def draw_tile_corner(key, part):
    key = jax.random.fold_in(key, 7)
    key_z, key_y, key_x = jax.random.split(key, 3)
    slot_index = jnp.arange(SLOTS, dtype=jnp.int32)
    device = slot_index // E_CAP
    devices_y = NY // NY_DEV
    slab_index = device // devices_y
    row_block = device % devices_y
    plane_offset = jax.random.randint(key_z, (SLOTS,), 0, CZ, dtype=jnp.int32)
    row_offset = jax.random.randint(key_y, (SLOTS,), 0, NY_DEV, dtype=jnp.int32)
    column = jax.random.randint(key_x, (SLOTS,), 0, NX, dtype=jnp.int32)
    final_slot = slot_index == SLOTS - 1
    plane_offset = jnp.where(final_slot, CZ - 1, plane_offset)
    row_offset = jnp.where(final_slot, NY_DEV - 1, row_offset)
    column = jnp.where(final_slot, NX - 1, column)
    first_plane = slab_index * CZ + plane_offset
    first_row = row_block * NY_DEV + row_offset
    return jnp.stack([first_plane, first_row, column], axis=1).astype(jnp.int32)


def shard_levels(own_key, shape, pieces, least, largest):
    def one(axis_at, parts):
        draws = jax.random.uniform(jax.random.fold_in(jax.random.fold_in(own_key, 6), axis_at), (parts,), jnp.float32, least / len(pieces), largest / len(pieces))
        return jnp.repeat(jnp.exp(draws), shape[axis_at] // parts).reshape((-1,) + (1,) * (len(shape) - axis_at - 1))

    loudness = one(*pieces[0])
    for cut in pieces[1:]:
        loudness = loudness * one(*cut)
    return loudness


def length_profile(number_of, total, most, skew):
    portions = [(1 << 20) // math.isqrt(grade ** skew) + 1 for grade in range(2, number_of + 1)]
    surplus, given = total - most - (number_of - 1), [1] * (number_of - 1)
    while surplus > 0:
        candidates = [i for i in range(number_of - 1) if given[i] < most]
        whole, budget = sum([portions[i] for i in candidates]), surplus
        for i in candidates:
            more = min(most - given[i], max(1, budget * portions[i] // whole), surplus)
            given[i] = given[i] + more
            surplus = surplus - more
    return np.array([most] + given)


def ragged(own_key, count, total, limit, skew):
    if count == 2:
        one = jax.random.randint(own_key, (), max(1, total - limit), min(limit, total - 1) + 1)
        return jnp.stack([one, total - one])
    lengths = jnp.asarray(length_profile(count, total, limit, skew), jnp.int32)
    couples = (count - 1) // 2
    donor, sink = lengths[1:1 + 2 * couples:2], lengths[2:2 + 2 * couples:2]
    slack = jnp.minimum(donor - 1, limit - sink)
    passed = jax.random.randint(jax.random.fold_in(own_key, 1), (couples,), 0, 1 << 20) % (slack + 1)
    lengths = lengths.at[1:1 + 2 * couples:2].set(donor - passed).at[2:2 + 2 * couples:2].set(sink + passed)
    return lengths[jax.random.permutation(jax.random.fold_in(own_key, 2), count)]


def scatter_about(stream_key, extent, spread, limit, cuts=(), kind=jnp.bfloat16):
    factor_of = shard_levels(stream_key, extent, cuts, -0.22, 0.18) if cuts else 1.0
    values = jax.random.normal(stream_key, extent, jnp.float32) * spread * factor_of
    return jnp.minimum(jnp.maximum(values, -limit), limit).astype(kind)


def setup_inputs(seed: int = 0) -> dict:
    seeds = jax.random.split(jax.random.key(seed), 8)
    pressure = scatter_about(seeds[0], (NZ, NY, NX), 1.0, 6.0, ((0, 64), (1, 4)), jnp.float32)
    velocity = scatter_about(seeds[1], (3, NZ, NY, NX), 1.0, 6.0, ((1, 64), (2, 4)), jnp.float32)
    bulk = jnp.clip(jnp.exp(math.log(0.6) - 1.3862944 * jax.random.uniform(seeds[2], (NZ, NY, NX), jnp.float32) ** shard_levels(seeds[2], (NZ, NY, NX), ((0, 64), (1, 4)), -0.2, 0.2)), 0.15, 0.6)
    buoyancy = jnp.clip(jnp.exp(math.log(0.6) - 1.3862944 * jax.random.uniform(seeds[3], (NZ, NY, NX), jnp.float32) ** shard_levels(seeds[3], (NZ, NY, NX), ((0, 64), (1, 4)), -0.2, 0.2)), 0.15, 0.6)
    tiles = scatter_about(seeds[4], (SLOTS, TZ, TY, TX), 0.5, 3.0, ((0, 256),))
    tile_corner = draw_tile_corner(jax.random.fold_in(seeds[7], 71), 0)
    live_count = ragged(seeds[6], DEVICES, ELEMENTS, E_CAP, 2).astype(jnp.int32)
    return {"pressure": pressure, "velocity": velocity, "bulk": bulk, "buoyancy": buoyancy, "tiles": tiles, "tile_corner": tile_corner, "live_count": live_count}


kappa_courant = 0.3

def wavenumber(length):
    position = jnp.arange(length)
    signed = jnp.where(position < length // 2, position, position - length)
    return signed.astype(jnp.float32) * (2.0 * math.pi / length)

def staggered(wave, orientation):
    return 1j * wave * jnp.exp(orientation * 0.5j * wave)

def build_source(tiles, tile_corner, live_count, grid_z, grid_y, grid_x):
    slot_total = tiles.shape[0]
    tile_z, tile_y, tile_x = (tiles.shape[1], tiles.shape[2], tiles.shape[3])
    padded = jnp.zeros((grid_z + tile_z, grid_y + tile_y, grid_x + tile_x), jnp.float32)

    def add_tile(slot_index, buffer):
        slot_index = jnp.asarray(slot_index).astype(jnp.int32)
        device = slot_index // E_CAP
        live_mask = (slot_index % E_CAP < live_count[device]).astype(jnp.float32)
        corner = tile_corner[slot_index].astype(jnp.int32)
        anchor = (corner[0], corner[1], corner[2])
        current = lax.dynamic_slice(buffer, anchor, (tile_z, tile_y, tile_x))
        placed = current + tiles[slot_index].astype(jnp.float32) * live_mask
        return lax.dynamic_update_slice(buffer, placed, anchor)
    padded = lax.fori_loop(0, slot_total, add_tile, padded)
    folded = padded[:grid_z].at[:tile_z].add(padded[grid_z:])
    folded = folded[:, :grid_y].at[:, :tile_y].add(folded[:, grid_y:])
    folded = folded[:, :, :grid_x].at[:, :, :tile_x].add(folded[:, :, grid_x:])
    return folded

def reference(pressure, velocity, bulk, buoyancy, tiles, tile_corner, live_count):
    grid_z, grid_y, grid_x = pressure.shape
    wave_z = wavenumber(grid_z)[:, None, None]
    wave_y = wavenumber(grid_y)[None, :, None]
    wave_x = wavenumber(grid_x)[None, None, :]
    magnitude = jnp.sqrt(wave_x * wave_x + wave_y * wave_y + wave_z * wave_z)
    kappa_factor = jnp.sinc(kappa_courant * magnitude / (2.0 * math.pi))
    keep_x = (jnp.arange(grid_x) != grid_x // 2).astype(jnp.float32)[None, None, :]
    base = kappa_factor * keep_x
    waves = (wave_x, wave_y, wave_z)
    pressure_spectrum = jnp.fft.fftn(pressure)
    components = []
    for direction in range(3):
        slope = jnp.real(jnp.fft.ifftn(staggered(waves[direction], 1.0) * base * pressure_spectrum))
        components.append(velocity[direction] - buoyancy * slope)
    new_velocity = jnp.stack(components)
    divergence_spectrum = staggered(waves[0], -1.0) * base * jnp.fft.fftn(new_velocity[0])
    for direction in range(1, 3):
        divergence_spectrum = divergence_spectrum + staggered(waves[direction], -1.0) * base * jnp.fft.fftn(new_velocity[direction])
    divergence = jnp.real(jnp.fft.ifftn(divergence_spectrum))
    source = build_source(tiles, tile_corner, live_count, grid_z, grid_y, grid_x)
    new_pressure = pressure - bulk * divergence + source
    return (new_pressure.astype(jnp.float32), new_velocity.astype(jnp.float32))
```

```python
import functools
import math

import jax
import jax.numpy as jnp
import ml_dtypes
import numpy as np
from jax import lax
from jax.experimental import pallas as pl
from jax.experimental.pallas import tpu as pltpu
from jax.sharding import PartitionSpec as P

NX = 256
NY = 256
NZ = 512
HALF = 128
ROWS = 64
PEERS_Y = 4
kappa_courant = 0.3
f32 = jnp.float32
bf16 = jnp.bfloat16
f16 = jnp.float16

SPECTRUM_SCALE = 1.0 / 256.0
SLOPE_LINK = 0.25
MIDDLE_LINK = 1.0 / 16.0
DIVERGENCE_LINK = 1.0 / 32.0


def split_table(table):
    high = table.astype(ml_dtypes.bfloat16)
    low = (table - high.astype(np.float64)).astype(ml_dtypes.bfloat16)
    return high, low


def make_tables():
    index = np.arange(256)
    angle = 2.0 * np.pi / 256 * (np.outer(index, index) % 256)
    cos_high, cos_low = split_table(np.cos(angle))
    sin_high, sin_low = split_table(np.sin(angle))
    rows = np.concatenate(
        [
            np.concatenate([cos_high, cos_high, cos_low], axis=1),
            np.concatenate([sin_high, sin_high, sin_low], axis=1),
        ],
        axis=0,
    )
    wave_x = 2.0 * np.pi / NX * np.arange(HALF)
    angle_x = 2.0 * np.pi / NX * (np.outer(index, np.arange(HALF)) % NX)

    def stacked(table):
        high, low = split_table(table)
        return np.concatenate([high, high, low], axis=0)

    def forward_x(factor):
        spectrum = np.exp(-1j * angle_x) * factor[None, :]
        return stacked(np.concatenate([spectrum.real, spectrum.imag], axis=1))

    def inverse_x(factor):
        weight = np.where(np.arange(HALF) == 0, 1.0, 2.0) * factor
        wave = np.exp(1j * angle_x.T) * weight[:, None]
        return stacked(np.concatenate([wave.real, -wave.imag], axis=0))

    ahead = 1j * wave_x * np.exp(0.5j * wave_x)
    behind = 1j * wave_x * np.exp(-0.5j * wave_x)
    plain = np.ones(HALF)
    wave_z = 2.0 * np.pi / NZ * np.where(np.arange(NZ) < NZ // 2, np.arange(NZ), np.arange(NZ) - NZ)
    wave_y = 2.0 * np.pi / NY * np.where(np.arange(NY) < NY // 2, np.arange(NY), np.arange(NY) - NY)

    def lanes(column):
        return np.broadcast_to(column[:, None], (column.shape[0], HALF)).astype(np.float32)

    def derivative(wave):
        return np.stack([lanes(-wave * np.sin(0.5 * wave)), lanes(wave * np.cos(0.5 * wave))])

    turn = np.exp(-2j * np.pi / NZ * index)
    return {
        "rows": rows,
        "x_forward": forward_x(plain),
        "x_forward_behind": forward_x(behind),
        "x_inverse": inverse_x(plain),
        "x_inverse_ahead": inverse_x(ahead),
        "wave_z": derivative(wave_z),
        "wave_y": derivative(wave_y),
        "turn": np.stack([lanes(turn.real), lanes(turn.imag)]),
    }


TABLES = make_tables()


def pieces(x, axis):
    high = x.astype(bf16)
    low = (x - high.astype(f32)).astype(bf16)
    return jnp.concatenate([high, low, high], axis=axis)


def rows_transform(rows_ref, fields):
    stacked = pieces(jnp.concatenate(fields, axis=1), 0)
    both = jnp.dot(rows_ref[...], stacked, preferred_element_type=f32)
    cosine = [both[:256, HALF * i : HALF * (i + 1)] for i in range(len(fields))]
    sine = [both[256:, HALF * i : HALF * (i + 1)] for i in range(len(fields))]
    return cosine, sine


def forward_rows(rows_ref, fields):
    cosine, sine = rows_transform(rows_ref, fields)
    out = []
    for i in range(0, len(fields), 2):
        out += [cosine[i] + sine[i + 1], cosine[i + 1] - sine[i]]
    return out


def inverse_rows(rows_ref, fields):
    cosine, sine = rows_transform(rows_ref, fields)
    out = []
    for i in range(0, len(fields), 2):
        out += [cosine[i] - sine[i + 1], cosine[i + 1] + sine[i]]
    return out


def times(real, imag, factor_real, factor_imag):
    return real * factor_real - imag * factor_imag, real * factor_imag + imag * factor_real


def columns_transform(x, table_ref):
    return jnp.dot(pieces(x, 1), table_ref[...], preferred_element_type=f32)


def kappa_rows(first, ky, signed_start):
    kz = lax.broadcasted_iota(jnp.int32, (256, HALF), 0) + signed_start
    kx = lax.broadcasted_iota(jnp.int32, (256, HALF), 1)
    ky = jnp.where(ky < NY // 2, ky, ky - NY)
    wave_z = kz.astype(f32) * (2.0 * math.pi / NZ)
    wave_x = kx.astype(f32) * (2.0 * math.pi / NX)
    wave_y = ky.astype(f32) * (2.0 * math.pi / NY)
    square = (kappa_courant / 2.0) ** 2 * (wave_x * wave_x + wave_z * wave_z + wave_y * wave_y)
    total = jnp.full((256, HALF), 1.0 / math.factorial(15), f32)
    for order in range(6, -1, -1):
        total = 1.0 / math.factorial(2 * order + 1) - square * total
    return total


def place_rows(scratch, position, blocks):
    for back, block in enumerate(blocks):
        start = pl.multiple_of(((position + PEERS_Y - back) % PEERS_Y) * ROWS, ROWS)
        scratch[..., pl.ds(start, ROWS), :] = block[...].astype(f32)


def forward_plane_kernel(where, b0, b1, b2, b3, rows_ref, x_ref, out, planes):
    place_rows(planes, where[0], (b0, b1, b2, b3))
    spectrum = columns_transform(planes[...].reshape(512, NX), x_ref) * SPECTRUM_SCALE
    fields = []
    for r in range(2):
        part = spectrum[256 * r : 256 * (r + 1)]
        fields += [part[:, :HALF], part[:, HALF:]]
    for i, field in enumerate(forward_rows(rows_ref, fields)):
        out[pl.ds(i, 256, stride=4), :] = field


def forward_z(rows_ref, turn_ref, even, odd):
    out = forward_rows(rows_ref, even + odd)
    count = len(even)
    low, high = [], []
    for i in range(0, count, 2):
        real, imag = times(out[count + i], out[count + i + 1], turn_ref[0], turn_ref[1])
        low += [out[i] + real, out[i + 1] + imag]
        high += [out[i] - real, out[i + 1] - imag]
    return low, high


def inverse_z(rows_ref, turn_ref, low, high):
    even, odd = [], []
    for i in range(0, len(low), 2):
        even += [low[i] + high[i], low[i + 1] + high[i + 1]]
        odd += times(low[i] - high[i], low[i + 1] - high[i + 1], turn_ref[0], -turn_ref[1])
    out = inverse_rows(rows_ref, even + odd)
    return out[: len(low)], out[len(low) :]


def slope_columns_kernel(where, data, rows_ref, turn_ref, wave_ref, out):
    even = [data[pl.ds(i, 256, stride=4), :] for i in (0, 1)]
    odd = [data[pl.ds(i, 256, stride=4), :] for i in (2, 3)]
    spectra = forward_z(rows_ref, turn_ref, even, odd)
    filtered = []
    for half in range(2):
        kappa = kappa_rows(half, where[0], -256 * half) * (SLOPE_LINK / NZ)
        real, imag = spectra[half][0] * kappa, spectra[half][1] * kappa
        span = pl.ds(256 * half, 256)
        filtered.append([real, imag, *times(real, imag, wave_ref[0, span], wave_ref[1, span])])
    even, odd = inverse_z(rows_ref, turn_ref, filtered[0], filtered[1])
    for r, fields in enumerate((even, odd)):
        for i, field in enumerate(fields):
            out[pl.ds(4 * r + i, 256, stride=8), :] = field


def middle_kernel(
    where, data, f0, f1, f2, f3, rows_ref, xi_ref, xia_ref, xf_ref, xfb_ref, wave_ref, slopes, out, planes
):
    place_rows(planes, where[0], (f0, f1, f2, f3))
    for r in range(2):
        q_real, q_imag, g_real, g_imag = [
            data[pl.ds(4 * r + i, 256, stride=8), :] for i in range(4)
        ]
        along = times(q_real, q_imag, wave_ref[0], wave_ref[1])
        mixed = inverse_rows(rows_ref, [q_real, q_imag, *along, g_real, g_imag])
        turned = []
        for d, table in enumerate((xia_ref, xi_ref, xi_ref)):
            pair = jnp.concatenate(mixed[2 * d : 2 * d + 2], axis=1)
            slope = columns_transform(pair, table) * SPECTRUM_SCALE
            slopes[d, r] = slope
            velocity = planes[d, r] - planes[3, r] * (slope * (1.0 / SLOPE_LINK))
            spectrum = columns_transform(velocity, (xfb_ref, xf_ref, xf_ref)[d])
            spectrum = spectrum * (SPECTRUM_SCALE * MIDDLE_LINK)
            turned += [spectrum[:, :HALF], spectrum[:, HALF:]]
        x_real, x_imag, y_real, y_imag, z_real, z_imag = forward_rows(rows_ref, turned)
        y_real, y_imag = times(y_real, y_imag, -wave_ref[0], wave_ref[1])
        fields = (x_real + y_real, x_imag + y_imag, z_real, z_imag)
        for i, field in enumerate(fields):
            out[pl.ds(4 * r + i, 256, stride=8), :] = field


def divergence_columns_kernel(where, data, rows_ref, turn_ref, wave_ref, out):
    even = [data[pl.ds(i, 256, stride=8), :] for i in range(4)]
    odd = [data[pl.ds(4 + i, 256, stride=8), :] for i in range(4)]
    spectra = forward_z(rows_ref, turn_ref, even, odd)
    summed = []
    for half in range(2):
        kappa = kappa_rows(half, where[0], -256 * half) * (DIVERGENCE_LINK / MIDDLE_LINK / NZ)
        span = pl.ds(256 * half, 256)
        a_real, a_imag, z_real, z_imag = spectra[half]
        real, imag = times(z_real, z_imag, -wave_ref[0, span], wave_ref[1, span])
        summed.append([(a_real + real) * kappa, (a_imag + imag) * kappa])
    even, odd = inverse_z(rows_ref, turn_ref, summed[0], summed[1])
    for i, field in enumerate(even + odd):
        out[pl.ds(i, 256, stride=4), :] = field


def inverse_plane_kernel(where, data, rows_ref, x_ref, o0, o1, o2, o3, planes):
    fields = [data[pl.ds(i, 256, stride=4), :] for i in range(4)]
    mixed = inverse_rows(rows_ref, fields)
    for r in range(2):
        pair = jnp.concatenate(mixed[2 * r : 2 * r + 2], axis=1)
        planes[r] = columns_transform(pair, x_ref) * SPECTRUM_SCALE
    for ahead, out in enumerate((o0, o1, o2, o3)):
        start = pl.multiple_of(((where[0] + ahead) % PEERS_Y) * ROWS, ROWS)
        out[...] = planes[:, pl.ds(start, ROWS), :]


VMEM = pl.BlockSpec(memory_space=pltpu.VMEM)
SMEM = pl.BlockSpec(memory_space=pltpu.SMEM)


def call(kernel, where, arrays, shapes, scratch=(), name=None, limit=24, flops=4e8):
    return pl.pallas_call(
        kernel,
        out_shape=[jax.ShapeDtypeStruct(shape, f32) for shape in shapes],
        in_specs=[SMEM] + [VMEM] * len(arrays),
        out_specs=[VMEM] * len(shapes),
        scratch_shapes=[pltpu.VMEM(shape, f32) for shape in scratch],
        compiler_params=pltpu.CompilerParams(vmem_limit_bytes=limit << 20),
        cost_estimate=pl.CostEstimate(flops=int(flops), bytes_accessed=1 << 20, transcendentals=0),
        name=name,
    )(where, *arrays)


def from_behind(x, axis, by):
    peers = lax.axis_size(axis)
    return lax.ppermute(x, axis, [(i, (i + by) % peers) for i in range(peers)])


def to_planes(fields, row_block):
    axis = fields.ndim - 3

    def planes_of(device):
        return lax.dynamic_slice_in_dim(fields, 2 * device, 2, axis).astype(f16)

    blocks = [planes_of(row_block)]
    for ahead in range(1, PEERS_Y):
        blocks.append(from_behind(planes_of((row_block + ahead) % PEERS_Y), "gy", ahead))
    return blocks


def to_rows(blocks, row_block, axis):
    arrived = [blocks[0]] + [
        from_behind(blocks[ahead].astype(f16), "gy", ahead).astype(f32)
        for ahead in range(1, PEERS_Y)
    ]
    ordered = []
    for device in range(PEERS_Y):
        back = (row_block - device) % PEERS_Y
        ordered.append(lax.select_n(back, *arrived))
    return jnp.concatenate(ordered, axis)


def exchange(columns, rows):
    blocks = columns.astype(f16).reshape(256, rows, HALF)
    moved = lax.all_to_all(blocks, ("gz", "gy"), 0, 0, tiled=True)
    return moved.reshape(256 * rows, HALF).astype(f32)


def one_hot_place(extent, start, span):
    target = jnp.arange(extent, dtype=jnp.int32)[None, :, None]
    wanted = start[:, None, None] + jnp.arange(span, dtype=jnp.int32)[None, None, :]
    return (target == wanted).astype(jnp.bfloat16)


def place_tiles(buffer, blocks, plane_start, row_start, column_start):
    planes, rows, columns = buffer.shape
    tile_z, tile_y, tile_x = (blocks.shape[1], blocks.shape[2], blocks.shape[3])
    column_hot = one_hot_place(columns, column_start, tile_x)
    across = jnp.einsum(
        "sabc,sxc->sabx", blocks, column_hot, preferred_element_type=jnp.float32
    ).astype(jnp.bfloat16)
    plane_hot = one_hot_place(planes, plane_start, tile_z)
    lifted = jnp.einsum(
        "sAa,sabx->sAbx", plane_hot, across, preferred_element_type=jnp.float32
    ).astype(jnp.bfloat16)
    row_hot = one_hot_place(rows, row_start, tile_y)
    return buffer + jnp.einsum("sAbx,srb->Arx", lifted, row_hot, preferred_element_type=jnp.float32)


def fold_columns(buffer, grid_x, tile_x):
    return buffer[..., :grid_x].at[..., :tile_x].add(buffer[..., grid_x:])


def source_of(tiles, tile_corner, live_count, slab_index, row_block):
    slabs_z = lax.axis_size("gz")
    rows_y = lax.axis_size("gy")
    slab_planes, row_count, grid_x = NZ // slabs_z, ROWS, NX
    slot_count, tile_z, tile_y, tile_x = tiles.shape
    slab_reach = (slab_planes + tile_z - 2) // slab_planes + 1
    own_device = slab_index * rows_y + row_block
    own_corners = lax.dynamic_slice_in_dim(tile_corner, own_device * slot_count, slot_count, 0)
    live_mask = (jnp.arange(slot_count, dtype=jnp.int32) < live_count[own_device]).astype(
        jnp.bfloat16
    )
    masked = tiles * live_mask[:, None, None, None]
    plane_offset = own_corners[:, 0] - slab_index * slab_planes
    padded = jnp.pad(masked, ((0, 0), (slab_planes, slab_planes), (0, 0), (0, 0)))
    window = jnp.zeros((slab_planes, 2 * row_count, grid_x + tile_x), jnp.float32)
    zero_start = jnp.zeros((slot_count,), jnp.int32)
    for step_index in range(slab_reach):
        first_plane = step_index * slab_planes - plane_offset + slab_planes
        blocks = jax.vmap(
            lambda tile_block, first_index: lax.dynamic_slice_in_dim(
                tile_block, first_index, slab_planes, 0
            )
        )(padded, first_plane)
        corners = own_corners
        if step_index > 0:
            blocks = from_behind(blocks, "gz", step_index)
            sender = (slab_index - step_index) % slabs_z * rows_y + row_block
            corners = lax.dynamic_slice_in_dim(tile_corner, sender * slot_count, slot_count, 0)
        window = place_tiles(
            window, blocks, zero_start, corners[:, 1] - row_block * row_count, corners[:, 2]
        )
    window = fold_columns(window, grid_x, tile_x)
    return window[:, :row_count] + from_behind(
        window[:, row_count:].astype(jnp.bfloat16), "gy", 1
    ).astype(jnp.float32)


def local(pressure, velocity, bulk, buoyancy, tiles, tile_corner, live_count):
    slab_index = lax.axis_index("gz")
    row_block = lax.axis_index("gy")
    here = row_block.reshape(1).astype(jnp.int32)
    device = (slab_index * PEERS_Y + row_block).reshape(1).astype(jnp.int32)
    table = {key: jnp.asarray(value) for key, value in TABLES.items()}
    rows, turn, wave_z, wave_y = (table[key] for key in ("rows", "turn", "wave_z", "wave_y"))

    blocks = to_planes(pressure, row_block)
    (spectrum,) = call(
        forward_plane_kernel,
        here,
        [*blocks_f32(blocks), rows, table["x_forward"]],
        [(1024, HALF)],
        [(2, NY, NX)],
        name="forward_plane",
    )
    velocity, buoyancy_after, spectrum = lax.optimization_barrier((velocity, buoyancy, spectrum))
    fields = jnp.concatenate([velocity, buoyancy_after[None]])
    field_blocks = to_planes(fields, row_block)

    columns = exchange(spectrum, 4)
    (slope_columns,) = call(
        slope_columns_kernel,
        device,
        [columns, rows, turn, wave_z],
        [(2048, HALF)],
        name="slope_columns",
    )
    slope_columns = exchange(slope_columns, 8)
    slopes, middle = call(
        middle_kernel,
        here,
        [
            slope_columns,
            *blocks_f32(field_blocks),
            rows,
            table["x_inverse"],
            table["x_inverse_ahead"],
            table["x_forward"],
            table["x_forward_behind"],
            wave_y,
        ],
        [(3, 2, NY, NX), (2048, HALF)],
        [(4, 2, NY, NX)],
        name="middle",
        limit=40,
    )
    slope_blocks = [
        lax.dynamic_slice_in_dim(slopes, ROWS * ((row_block + ahead) % PEERS_Y), ROWS, 2)
        for ahead in range(PEERS_Y)
    ]
    slopes_here = to_rows(slope_blocks, row_block, 1)
    new_velocity = velocity - buoyancy[None] * (slopes_here * (1.0 / SLOPE_LINK))

    middle = exchange(middle, 8)
    (divergence_columns,) = call(
        divergence_columns_kernel,
        device,
        [middle, rows, turn, wave_z],
        [(1024, HALF)],
        name="divergence_columns",
    )
    divergence_columns = exchange(divergence_columns, 4)
    divergence_blocks = call(
        inverse_plane_kernel,
        here,
        [divergence_columns, rows, table["x_inverse"]],
        [(2, ROWS, NX)] * PEERS_Y,
        [(2, NY, NX)],
        name="inverse_plane",
    )
    source = source_of(tiles, tile_corner, live_count, slab_index, row_block)
    divergence = to_rows(divergence_blocks, row_block, 0)
    new_pressure = pressure - bulk * (divergence * (1.0 / DIVERGENCE_LINK)) + source
    return (new_pressure, new_velocity)


def blocks_f32(blocks):
    return [block.astype(f32) for block in blocks]


def solution(mesh):
    in_specs = (
        P("gz", "gy", None),
        P(None, "gz", "gy", None),
        P("gz", "gy", None),
        P("gz", "gy", None),
        P(("gz", "gy"), None, None, None),
        P(),
        P(),
    )
    out_specs = (P("gz", "gy", None), P(None, "gz", "gy", None))
    return jax.shard_map(local, mesh=mesh, in_specs=in_specs, out_specs=out_specs, check_vma=False)
```

```python
import math

import jax
import jax.numpy as jnp
import ml_dtypes
import numpy as np
from jax import lax
from jax.experimental import pallas as pl
from jax.experimental.pallas import tpu as pltpu
from jax.sharding import PartitionSpec as P

NX = 256
NY = 256
NZ = 512
HALF = 128
ROWS = 64
SLAB = 8
SLOTS_HERE = 8
TILE = 32
PEERS_Y = 4
PEERS_Z = 64
kappa_courant = 0.3
f32 = jnp.float32
bf16 = jnp.bfloat16
f16 = jnp.float16

X_SCALE = 1.0 / 16.0
SLOPE_LINK = 0.25
MIDDLE_LINK = 1.0 / 16.0
DIVERGENCE_LINK = 1.0 / 32.0


def split_table(table):
    high = table.astype(ml_dtypes.bfloat16)
    low = (table - high.astype(np.float64)).astype(ml_dtypes.bfloat16)
    return high, low


def left_table(table):
    high, low = split_table(table)
    return np.concatenate([high, high, low], axis=1)


def right_table(table):
    return np.ascontiguousarray(left_table(table.T).T)


def signed_waves(length):
    index = np.arange(length)
    return 2.0 * np.pi / length * np.where(index < length // 2, index, index - length)


def derivative_matrix(length, orientation):
    wave = signed_waves(length)
    kernel = np.fft.ifft(1j * wave * np.exp(orientation * 0.5j * wave)).real
    index = np.arange(length)
    return kernel[(index[:, None] - index[None, :]) % length]


def cas(rows, columns, length):
    angle = 2.0 * np.pi / length * (np.outer(rows, columns) % length)
    return np.cos(angle) + np.sin(angle)


def make_tables():
    index = np.arange(256)
    wave_x = 2.0 * np.pi / NX * np.arange(HALF)
    angle_x = 2.0 * np.pi / NX * (np.outer(np.arange(HALF), index) % NX)

    def forward_x(factor):
        spectrum = np.exp(-1j * angle_x) * factor[:, None]
        return left_table(np.concatenate([spectrum.real, spectrum.imag], axis=0))

    def inverse_x(factor):
        weight = np.where(np.arange(HALF) == 0, 1.0, 2.0) * factor
        wave = np.exp(1j * angle_x) * weight[:, None]
        return np.concatenate([wave.real, -wave.imag], axis=0)

    ahead = 1j * wave_x * np.exp(0.5j * wave_x)
    behind = 1j * wave_x * np.exp(-0.5j * wave_x)
    plain = np.ones(HALF)
    waves = np.arange(NZ)
    pair_order = (2 * np.arange(256)[None, :] + np.arange(2)[:, None]).reshape(-1)
    slab_order = (
        8 * np.arange(64)[None, None, :]
        + 2 * np.arange(4)[None, :, None]
        + np.arange(2)[:, None, None]
    ).reshape(-1)
    natural = cas(waves, waves, NZ)
    ahead_z = derivative_matrix(NZ, 1.0)
    behind_z = derivative_matrix(NZ, -1.0)
    return {
        "x_forward": forward_x(plain),
        "x_forward_behind": forward_x(behind),
        "x_inverse": right_table(inverse_x(plain)),
        "x_inverse_both": right_table(
            np.concatenate([inverse_x(ahead), inverse_x(plain)], axis=1)
        ),
        "y_ahead": left_table(derivative_matrix(NY, 1.0)),
        "y_behind": left_table(derivative_matrix(NY, -1.0)),
        "y_waves": right_table(cas(index, index, NY)),
        "z_from_slabs": left_table(natural[:, slab_order]),
        "z_to_pairs": left_table(
            np.concatenate([natural[pair_order], (ahead_z @ natural)[pair_order]], axis=0)
        ),
        "z_from_pairs": np.concatenate(
            [left_table(natural[:, pair_order]), left_table((natural @ behind_z)[:, pair_order])],
            axis=1,
        ),
        "z_to_slabs": left_table(natural[slab_order]),
    }


TABLES = make_tables()


def pieces(x, axis):
    high = x.astype(bf16)
    low = (x - high.astype(f32)).astype(bf16)
    return jnp.concatenate([high, low, high], axis=axis)


def contract(a, b, a_dim, b_dim):
    return lax.dot_general(a, b, (((a_dim,), (b_dim,)), ((), ())), preferred_element_type=f32)


def left(table_ref, x):
    return contract(table_ref[...], pieces(x, 0), 1, 0)


def right(x, table_ref):
    return contract(pieces(x, 1), table_ref[...], 1, 0)


def to_components(table_ref, lines):
    return contract(table_ref[...], pieces(lines, 1), 1, 1)


def to_lines(components, table_ref):
    return contract(pieces(components, 0), table_ref[...], 0, 0)


def kappa_plane(kx):
    kz = lax.broadcasted_iota(jnp.int32, (NZ, NY), 0)
    ky = lax.broadcasted_iota(jnp.int32, (NZ, NY), 1)
    wave_z = jnp.where(kz < NZ // 2, kz, kz - NZ).astype(f32) * (2.0 * math.pi / NZ)
    wave_y = jnp.where(ky < NY // 2, ky, ky - NY).astype(f32) * (2.0 * math.pi / NY)
    wave_x = jnp.full((NZ, NY), kx, jnp.int32).astype(f32) * (2.0 * math.pi / NX)
    square = (kappa_courant / 2.0) ** 2 * (wave_x * wave_x + wave_z * wave_z + wave_y * wave_y)
    total = jnp.full((NZ, NY), 1.0 / math.factorial(15), f32)
    for order in range(6, -1, -1):
        total = 1.0 / math.factorial(2 * order + 1) - square * total
    return total


def first_half():
    return lax.broadcasted_iota(jnp.int32, (64, HALF), 1) < ROWS


def forward_lines_kernel(pressure, x_ref, out):
    components = to_components(x_ref, pressure[...].reshape(512, NX)) * X_SCALE
    for i in range(4):
        out[pl.ds(i, 256, stride=4), :] = components[:, HALF * i : HALF * (i + 1)]


def filter_out_kernel(where, data, y_ref, z_from_ref, z_to_ref, out, plane):
    early = first_half()
    for pair in range(4):
        for side in range(2):
            a = data[pl.ds(8 * side + pair, 64, stride=16), :]
            b = data[pl.ds(8 * side + 4 + pair, 64, stride=16), :]
            span = pl.ds(HALF * side, HALF)
            plane[pl.ds(64 * pair, 64), span] = jnp.where(early, a, pltpu.roll(b, ROWS, 1))
            plane[pl.ds(256 + 64 * pair, 64), span] = jnp.where(early, pltpu.roll(a, ROWS, 1), b)
    waves = left(z_from_ref, right(plane[...], y_ref))
    waves = waves * (kappa_plane(where[0] % HALF) * (SLOPE_LINK / (NZ * NY)))
    planes = left(z_to_ref, right(waves, y_ref))
    for field in range(2):
        for r in range(2):
            for side in range(2):
                start = 512 * field + 256 * r
                out[pl.ds(4 * r + 2 * field + side, 256, stride=8), :] = planes[
                    start : start + 256, HALF * side : HALF * (side + 1)
                ]


def middle_kernel(
    where, data, f0, f1, f2, f3, xi_ref, xib_ref, xf_ref, xfb_ref, ya_ref, yb_ref, slopes, out, fields
):
    for back, block in enumerate((f0, f1, f2, f3)):
        start = pl.multiple_of(((where[0] + PEERS_Y - back) % PEERS_Y) * ROWS, ROWS)
        fields[:, :, pl.ds(start, ROWS), :] = block[...].astype(f32)
    for r in range(2):
        q, g = [
            jnp.concatenate(
                [data[pl.ds(4 * r + 2 * field + side, 256, stride=8), :] for side in range(2)], axis=1
            )
            for field in range(2)
        ]
        both = to_lines(q, xib_ref) * X_SCALE
        along = (both[:, :NX], left(ya_ref, both[:, NX:]), to_lines(g, xi_ref) * X_SCALE)
        moved = []
        for d, slope in enumerate(along):
            slopes[d, r] = slope
            moved.append(fields[d, r] - fields[3, r] * (slope * (1.0 / SLOPE_LINK)))
        scale = X_SCALE * MIDDLE_LINK
        summed = to_components(xfb_ref, moved[0]) + to_components(xf_ref, left(yb_ref, moved[1]))
        for field, components in enumerate((summed * scale, to_components(xf_ref, moved[2]) * scale)):
            for side in range(2):
                out[pl.ds(4 * r + 2 * field + side, 256, stride=8), :] = components[
                    :, HALF * side : HALF * (side + 1)
                ]


def filter_back_kernel(where, data, y_ref, z_from_ref, z_to_ref, out):
    arrived = []
    for field in range(2):
        whole = jnp.concatenate(
            [
                jnp.concatenate(
                    [data[pl.ds(4 * r + 2 * field + side, 256, stride=8), :] for side in range(2)],
                    axis=1,
                )
                for r in range(2)
            ],
            axis=0,
        )
        arrived.append(pieces(whole, 0))
    waves = contract(z_from_ref[...], jnp.concatenate(arrived, axis=0), 1, 0)
    scale = DIVERGENCE_LINK / MIDDLE_LINK / (NZ * NY)
    waves = right(waves, y_ref) * (kappa_plane(where[0] % HALF) * scale)
    plane = left(z_to_ref, right(waves, y_ref))
    early = first_half()
    for pair in range(4):
        for side in range(2):
            span = slice(HALF * side, HALF * (side + 1))
            even = plane[64 * pair : 64 * (pair + 1), span]
            odd = plane[256 + 64 * pair : 256 + 64 * (pair + 1), span]
            out[pl.ds(8 * side + pair, 64, stride=16), :] = jnp.where(
                early, even, pltpu.roll(odd, ROWS, 1)
            )
            out[pl.ds(8 * side + 4 + pair, 64, stride=16), :] = jnp.where(
                early, pltpu.roll(even, ROWS, 1), odd
            )


def new_pressure_kernel(data, x_ref, pressure, bulk, own, passed, out):
    components = jnp.concatenate([data[pl.ds(i, 256, stride=4), :] for i in range(4)], axis=1)
    lines = to_lines(components, x_ref) * (X_SCALE / DIVERGENCE_LINK)
    out[...] = pressure[...] - bulk[...] * lines.reshape(SLAB, ROWS, NX) + own[...]
    out[:, :TILE, :] += passed[...].astype(f32)


def source_kernel(offset, column, starts, t0, t1, t2, own, passed, l0, l1, l2):
    blank = jnp.zeros((SLAB, 256, NX), bf16)
    l0[:SLAB] = blank
    l2[SLAB:] = blank

    def place(slot, carry):
        rows = pl.ds(pl.multiple_of(slot * TILE, TILE), TILE)
        lane = lax.broadcasted_iota(jnp.int32, (TILE, NX), 1)
        line = lax.broadcasted_iota(jnp.int32, (TILE, NX), 0)
        for reach, (tiles, placed) in enumerate(((t0, l0), (t1, l1), (t2, l2))):
            hot = ((lane - line - column[reach, slot]) & (NX - 1)) == 0
            hot = jnp.where(hot, 1.0, 0.0).astype(bf16)
            first = SLAB - offset[reach, slot] if reach == 1 else 0
            to = 0 if reach == 1 else offset[reach, slot]
            block = tiles[slot, pl.ds(first, SLAB)].reshape(SLAB * TILE, TILE)
            across = jnp.dot(block, hot, preferred_element_type=f32).astype(bf16)
            placed[pl.ds(to, SLAB), rows, :] = across.reshape(SLAB, TILE, NX)
        return carry

    lax.fori_loop(0, SLOTS_HERE, place, 0)
    line = lax.broadcasted_iota(jnp.int32, (ROWS + TILE, 256), 0)
    hots = [
        jnp.where(line == starts[0:1, 256 * reach : 256 * (reach + 1)], 1.0, 0.0).astype(bf16)
        for reach in range(3)
    ]
    for z in range(SLAB):
        window = jnp.dot(hots[0], l0[z], preferred_element_type=f32)
        window += jnp.dot(hots[1], l1[z], preferred_element_type=f32)
        window += jnp.dot(hots[2], l2[SLAB + z], preferred_element_type=f32)
        own[z] = window[:ROWS]
        passed[z] = window[ROWS:].astype(bf16)


VMEM = pl.BlockSpec(memory_space=pltpu.VMEM)
SMEM = pl.BlockSpec(memory_space=pltpu.SMEM)


def call(kernel, scalars, arrays, shapes, scratch=(), name=None, limit=24, flops=4e8):
    return pl.pallas_call(
        kernel,
        out_shape=[jax.ShapeDtypeStruct(shape, kind) for shape, kind in shapes],
        in_specs=[SMEM] * len(scalars) + [VMEM] * len(arrays),
        out_specs=[VMEM] * len(shapes),
        scratch_shapes=[pltpu.VMEM(shape, kind) for shape, kind in scratch],
        compiler_params=pltpu.CompilerParams(vmem_limit_bytes=limit << 20),
        cost_estimate=pl.CostEstimate(flops=int(flops), bytes_accessed=1 << 20, transcendentals=0),
        name=name,
    )(*scalars, *arrays)


def from_behind(x, axis, by):
    peers = lax.axis_size(axis)
    return lax.ppermute(x, axis, [(i, (i + by) % peers) for i in range(peers)])


def to_planes(fields, row_block):
    axis = fields.ndim - 3

    def planes_of(device):
        return lax.dynamic_slice_in_dim(fields, 2 * device, 2, axis).astype(f16)

    blocks = [planes_of(row_block)]
    for ahead in range(1, PEERS_Y):
        blocks.append(from_behind(planes_of((row_block + ahead) % PEERS_Y), "gy", ahead))
    return [block.astype(f32) for block in blocks]


def to_rows(blocks, row_block, axis):
    arrived = [blocks[0]] + [
        from_behind(blocks[ahead].astype(f16), "gy", ahead).astype(f32)
        for ahead in range(1, PEERS_Y)
    ]
    ordered = []
    for device in range(PEERS_Y):
        back = (row_block - device) % PEERS_Y
        ordered.append(lax.select_n(back, *arrived))
    return jnp.concatenate(ordered, axis)


def exchange(columns, rows):
    blocks = columns.astype(f16).reshape(256, rows, HALF)
    moved = lax.all_to_all(blocks, ("gz", "gy"), 0, 0, tiled=True)
    return moved.reshape(256 * rows, HALF).astype(f32)


def source_of(tiles, tile_corner, live_count, slab_index, row_block):
    corners, lives = [], []
    for reach in range(3):
        sender = (slab_index - reach) % PEERS_Z * PEERS_Y + row_block
        corners.append(lax.dynamic_slice_in_dim(tile_corner, sender * SLOTS_HERE, SLOTS_HERE, 0))
        lives.append(live_count[sender])
    corners = jnp.stack(corners)
    live = jnp.arange(SLOTS_HERE, dtype=jnp.int32)[None, :] < jnp.stack(lives)[:, None]
    offset = corners[:, :, 0] % SLAB
    first_row = jnp.where(live, corners[:, :, 1] - row_block * ROWS, -2 * TILE)
    starts = first_row[:, :, None] + jnp.arange(TILE, dtype=jnp.int32)[None, None, :]
    packed = tiles.reshape(SLOTS_HERE, 2 * SLAB, 8, HALF)
    before = from_behind(packed, "gz", 1).reshape(SLOTS_HERE, 2 * SLAB, TILE, TILE)
    second = from_behind(packed[:, SLAB:], "gz", 2).reshape(SLOTS_HERE, SLAB, TILE, TILE)
    own, passed = call(
        source_kernel,
        [offset, corners[:, :, 2]],
        [starts.reshape(1, 3 * 256), tiles, before, second],
        [((SLAB, ROWS, NX), f32), ((SLAB, TILE, NX), bf16)],
        [((2 * SLAB, 256, NX), bf16), ((SLAB, 256, NX), bf16), ((2 * SLAB, 256, NX), bf16)],
        name="source",
    )
    return own, from_behind(passed, "gy", 1)


def local(pressure, velocity, bulk, buoyancy, tiles, tile_corner, live_count):
    slab_index = lax.axis_index("gz")
    row_block = lax.axis_index("gy")
    here = row_block.reshape(1).astype(jnp.int32)
    device = (slab_index * PEERS_Y + row_block).reshape(1).astype(jnp.int32)
    table = {key: jnp.asarray(value) for key, value in TABLES.items()}

    (components,) = call(
        forward_lines_kernel,
        [],
        [pressure, table["x_forward"]],
        [((1024, HALF), f32)],
        name="forward_lines",
    )
    velocity, buoyancy, tiles, tile_corner, components = lax.optimization_barrier(
        (velocity, buoyancy, tiles, tile_corner, components)
    )
    field_blocks = to_planes(jnp.concatenate([velocity, buoyancy[None]]), row_block)
    (filtered,) = call(
        filter_out_kernel,
        [device],
        [exchange(components, 4), table["y_waves"], table["z_from_slabs"], table["z_to_pairs"]],
        [((2048, HALF), f32)],
        [((NZ, NY), f32)],
        name="filter_out",
    )
    slopes, middle = call(
        middle_kernel,
        [here],
        [
            exchange(filtered, 8),
            *field_blocks,
            table["x_inverse"],
            table["x_inverse_both"],
            table["x_forward"],
            table["x_forward_behind"],
            table["y_ahead"],
            table["y_behind"],
        ],
        [((3, 2, NY, NX), f32), ((2048, HALF), f32)],
        [((4, 2, NY, NX), f32)],
        name="middle",
        limit=32,
    )
    slope_blocks = [
        lax.dynamic_slice_in_dim(slopes, ROWS * ((row_block + ahead) % PEERS_Y), ROWS, 2)
        for ahead in range(PEERS_Y)
    ]
    slopes_here = to_rows(slope_blocks, row_block, 1)
    new_velocity = velocity - buoyancy[None] * (slopes_here * (1.0 / SLOPE_LINK))
    (filtered_back,) = call(
        filter_back_kernel,
        [device],
        [exchange(middle, 8), table["y_waves"], table["z_from_pairs"], table["z_to_slabs"]],
        [((1024, HALF), f32)],
        name="filter_back",
    )
    own, passed = source_of(tiles, tile_corner, live_count, slab_index, row_block)
    divergence = exchange(filtered_back, 4)
    divergence, new_velocity = lax.optimization_barrier((divergence, new_velocity))
    (new_pressure,) = call(
        new_pressure_kernel,
        [],
        [divergence, table["x_inverse"], pressure, bulk, own, passed],
        [((SLAB, ROWS, NX), f32)],
        name="new_pressure",
    )
    return (new_pressure, new_velocity)


def solution(mesh):
    in_specs = (
        P("gz", "gy", None),
        P(None, "gz", "gy", None),
        P("gz", "gy", None),
        P("gz", "gy", None),
        P(("gz", "gy"), None, None, None),
        P(),
        P(),
    )
    out_specs = (P("gz", "gy", None), P(None, "gz", "gy", None))
    return jax.shard_map(local, mesh=mesh, in_specs=in_specs, out_specs=out_specs, check_vma=False)
```

```python
import math

import jax
import jax.numpy as jnp
import ml_dtypes
import numpy as np
from jax import lax
from jax.experimental import pallas as pl
from jax.experimental.pallas import tpu as pltpu
from jax.sharding import PartitionSpec as P

NX = 256
NY = 256
NZ = 512
HALF = 128
ROWS = 64
SLAB = 8
SLOTS_HERE = 8
TILE = 32
PEERS_Y = 4
PEERS_Z = 64
kappa_courant = 0.3
f32 = jnp.float32
bf16 = jnp.bfloat16
f16 = jnp.float16

X_SCALE = 1.0 / 16.0
SLOPE_LINK = 0.25
MIDDLE_LINK = 1.0 / 16.0
DIVERGENCE_LINK = 1.0 / 32.0


def split_table(table):
    high = table.astype(ml_dtypes.bfloat16)
    low = (table - high.astype(np.float64)).astype(ml_dtypes.bfloat16)
    return high, low


def left_table(table):
    high, low = split_table(table)
    return np.concatenate([high, high, low], axis=1)


def right_table(table):
    return np.ascontiguousarray(left_table(table.T).T)


def signed_waves(length):
    index = np.arange(length)
    return 2.0 * np.pi / length * np.where(index < length // 2, index, index - length)


def derivative_matrix(length, orientation):
    wave = signed_waves(length)
    kernel = np.fft.ifft(1j * wave * np.exp(orientation * 0.5j * wave)).real
    index = np.arange(length)
    return kernel[(index[:, None] - index[None, :]) % length]


def make_tables():
    index = np.arange(256)
    angle = 2.0 * np.pi / 256 * (np.outer(index, index) % 256)
    wave_x = 2.0 * np.pi / NX * np.arange(HALF)

    def forward_x(factor):
        spectrum = np.exp(-1j * angle[:HALF]) * factor[:, None]
        return left_table(np.concatenate([spectrum.real, spectrum.imag], axis=0))

    def inverse_x(factor):
        weight = np.where(np.arange(HALF) == 0, 1.0, 2.0) * factor
        wave = np.exp(1j * angle[:HALF]) * weight[:, None]
        return np.concatenate([wave.real, -wave.imag], axis=0)

    ahead = 1j * wave_x * np.exp(0.5j * wave_x)
    behind = 1j * wave_x * np.exp(-0.5j * wave_x)
    plain = np.ones(HALF)
    forward_z = np.concatenate([np.cos(angle[:HALF]), -np.sin(angle[:HALF])], axis=0)
    forward_z[HALF] = np.cos(angle[HALF])
    inverse_z = 2.0 * forward_z.T
    inverse_z[:, 0] = forward_z[0]
    inverse_z[:, HALF] = forward_z[HALF]
    slab_order = (4 * np.arange(64)[None, :] + np.arange(4)[:, None]).reshape(-1)
    low = np.arange(HALF)
    high = low - 256
    coefficients = np.zeros((HALF, HALF), np.float32)
    coefficients[:, 0] = np.cos(2.0 * np.pi / NZ * low)
    coefficients[:, 1] = np.sin(2.0 * np.pi / NZ * low)

    def derivative(number, orientation):
        wave = 2.0 * np.pi / NZ * number
        return -orientation * wave * np.sin(0.5 * wave), wave * np.cos(0.5 * wave)

    for first, orientation in ((2, 1.0), (9, -1.0)):
        middle_real, middle_imag = derivative(128, orientation)
        for at, number in ((first, low), (first + 3, high)):
            real, imag = derivative(number, orientation)
            coefficients[:, at] = real
            coefficients[:, at + 1] = np.where((low == 0), 0.0, imag)
            coefficients[:, at + 2] = np.where((low == 0), middle_real, real)
        coefficients[:, first + 6] = np.where((low == 0), middle_imag, 0.0)
    return {
        "x_forward": forward_x(plain),
        "x_forward_behind": forward_x(behind),
        "x_inverse": right_table(inverse_x(plain)),
        "x_inverse_both": right_table(
            np.concatenate([inverse_x(ahead), inverse_x(plain)], axis=1)
        ),
        "y_ahead": left_table(derivative_matrix(NY, 1.0)),
        "y_behind": left_table(derivative_matrix(NY, -1.0)),
        "y_waves": right_table(np.cos(angle) + np.sin(angle)),
        "z_from_slabs": left_table(forward_z[:, slab_order]),
        "z_to_pairs": left_table(inverse_z),
        "z_from_pairs": left_table(forward_z),
        "z_to_slabs": left_table(inverse_z[slab_order]),
        "z_coefficients": coefficients,
    }


TABLES = make_tables()


def pieces(x, axis):
    high = x.astype(bf16)
    low = (x - high.astype(f32)).astype(bf16)
    return jnp.concatenate([high, low, high], axis=axis)


def contract(a, b, a_dim, b_dim):
    return lax.dot_general(a, b, (((a_dim,), (b_dim,)), ((), ())), preferred_element_type=f32)


def left(table_ref, x):
    return contract(table_ref[...], pieces(x, 0), 1, 0)


def right(x, table_ref):
    return contract(pieces(x, 1), table_ref[...], 1, 0)


def to_components(table_ref, lines):
    return contract(table_ref[...], pieces(lines, 1), 1, 1)


def to_lines(components, table_ref):
    return right(components.T, table_ref)


class Fetch:
    def __init__(self, sources, targets, semaphores):
        self.targets = targets
        self.copies = [
            pltpu.make_async_copy(source, target, semaphores.at[i])
            for i, (source, target) in enumerate(zip(sources, targets))
        ]
        for copy in self.copies:
            copy.start()

    def __getitem__(self, i):
        if self.copies[i] is not None:
            self.copies[i].wait()
            self.copies[i] = None
        return self.targets[i]


def kappa_rows(kx, part):
    kz = lax.broadcasted_iota(jnp.int32, (HALF, NY), 0)
    ky = lax.broadcasted_iota(jnp.int32, (HALF, NY), 1)
    number = kz - 256 * (part // 2)
    if part % 2:
        number = jnp.where(kz == 0, 128, number)
    wave_z = number.astype(f32) * (2.0 * math.pi / NZ)
    wave_y = jnp.where(ky < NY // 2, ky, ky - NY).astype(f32) * (2.0 * math.pi / NY)
    wave_x = jnp.full((HALF, NY), kx, jnp.int32).astype(f32) * (2.0 * math.pi / NX)
    square = (kappa_courant / 2.0) ** 2 * (wave_x * wave_x + wave_z * wave_z + wave_y * wave_y)
    total = jnp.full((HALF, NY), 1.0 / math.factorial(15), f32)
    for order in range(6, -1, -1):
        total = 1.0 / math.factorial(2 * order + 1) - square * total
    return total


def forward_z(table_ref, coefficient, fields):
    sides = [side for field in fields for side in (field[:256], field[256:])]
    sums = left(table_ref, jnp.concatenate(sides, axis=1))
    cosine, sine = coefficient(0), coefficient(1)
    spectra = []
    for i in range(0, len(sides), 2):
        even = sums[:, NY * i : NY * (i + 1)]
        odd = sums[:, NY * (i + 1) : NY * (i + 2)]
        real = cosine * odd[:HALF] + sine * odd[HALF:]
        imag = cosine * odd[HALF:] - sine * odd[:HALF]
        spectra.append(
            [even[:HALF] + real, even[HALF:] + imag, even[:HALF] - real, even[HALF:] - imag]
        )
    return spectra


def inverse_z(table_ref, coefficient, spectra):
    cosine, sine = coefficient(0), coefficient(1)
    sides = []
    for a, b, c, d in spectra:
        real, imag = a - c, b - d
        sides.append(jnp.concatenate([a + c, b + d], axis=0))
        sides.append(jnp.concatenate([cosine * real - sine * imag, cosine * imag + sine * real], axis=0))
    return left(table_ref, jnp.concatenate(sides, axis=1))


def derivative_z(coefficient, first, spectrum):
    a, b, c, d = spectrum
    mixed = coefficient(first + 6)
    return [
        coefficient(first) * a - coefficient(first + 1) * b,
        coefficient(first + 2) * b + coefficient(first + 1) * a - mixed * d,
        coefficient(first + 3) * c - coefficient(first + 4) * d,
        coefficient(first + 5) * d + coefficient(first + 4) * c + mixed * b,
    ]


def blocks_of(x):
    return [x[HALF * i : HALF * (i + 1)] for i in range(4)]


def first_half():
    return lax.broadcasted_iota(jnp.int32, (64, HALF), 1) < ROWS


def forward_lines_kernel(pressure, x_table, out, *scratch):
    *targets, semaphores = scratch
    sources = [x_table] + [pressure.at[pl.ds(2 * i, 2)] for i in range(4)]
    fetch = Fetch(sources, targets, semaphores)
    x_ref = fetch[0]
    for i in range(4):
        lines = fetch[i + 1][...].reshape(HALF, NX)
        out[pl.ds(i, 256, stride=4), :] = to_components(x_ref, lines) * X_SCALE


def filter_out_kernel(where, data, y, z_from, z_to, z_numbers, out, plane, *scratch):
    *targets, semaphores = scratch
    fetch = Fetch((y, z_from, z_numbers, z_to), targets, semaphores)
    early = first_half()
    for pair in range(4):
        for side in range(2):
            a = data[pl.ds(8 * side + pair, 64, stride=16), :]
            b = data[pl.ds(8 * side + 4 + pair, 64, stride=16), :]
            span = pl.ds(HALF * side, HALF)
            plane[pl.ds(64 * pair, 64), span] = jnp.where(early, a, pltpu.roll(b, ROWS, 1))
            plane[pl.ds(256 + 64 * pair, 64), span] = jnp.where(early, pltpu.roll(a, ROWS, 1), b)
    mixed = right(plane[...], fetch[0])
    z_from_ref, numbers = fetch[1], fetch[2]

    def coefficient(i):
        return numbers[:, i : i + 1]

    (spectrum,) = forward_z(z_from_ref, coefficient, [mixed])
    scale = SLOPE_LINK / (NZ * NY)
    waves = [x * (kappa_rows(where[0] % HALF, part) * scale) for part, x in enumerate(spectrum)]
    waves = blocks_of(right(jnp.concatenate(waves, axis=0), fetch[0]))
    planes = inverse_z(fetch[3], coefficient, [waves, derivative_z(coefficient, 2, waves)])
    for field in range(2):
        for r in range(2):
            for side in range(2):
                start = NY * (2 * field + r) + HALF * side
                out[pl.ds(4 * r + 2 * field + side, 256, stride=8), :] = planes[
                    :, start : start + HALF
                ]


def middle_kernel(
    where, data, f0, f1, f2, f3, xib, xi, ya, yb, xfb, xf, slopes, out, fields, held, *scratch
):
    *targets, semaphores = scratch
    fetch = Fetch((xib, xi, ya, yb, xfb, xf), targets, semaphores)
    for back, block in enumerate((f0, f1, f2, f3)):
        start = pl.multiple_of(((where[0] + PEERS_Y - back) % PEERS_Y) * ROWS, ROWS)
        fields[:, :, pl.ds(start, ROWS), :] = block[...]
    returned = []
    for r in range(2):
        q, g = [
            jnp.concatenate(
                [data[pl.ds(4 * r + 2 * field + side, 256, stride=8), :] for side in range(2)], axis=1
            )
            for field in range(2)
        ]
        both = to_lines(q, fetch[0]) * X_SCALE
        along = (both[:, :NX], left(fetch[2], both[:, NX:]), to_lines(g, fetch[1]) * X_SCALE)
        moved = []
        for d, slope in enumerate(along):
            held[r, d] = slope
            moved.append(fields[d, r] - fields[3, r] * (slope * (1.0 / SLOPE_LINK)))
        returned.append(pltpu.make_async_copy(held.at[r], slopes.at[r], semaphores.at[6 + r]))
        returned[r].start()
        scale = X_SCALE * MIDDLE_LINK
        along_y = left(fetch[3], moved[1])
        summed = to_components(fetch[4], moved[0]) + to_components(fetch[5], along_y)
        for field, components in enumerate(
            (summed * scale, to_components(fetch[5], moved[2]) * scale)
        ):
            for side in range(2):
                out[pl.ds(4 * r + 2 * field + side, 256, stride=8), :] = components[
                    :, HALF * side : HALF * (side + 1)
                ]
    for copy in returned:
        copy.wait()


def filter_back_kernel(where, data, y, z_from, z_to, z_numbers, out, *scratch):
    *targets, semaphores = scratch
    fetch = Fetch((z_from, z_numbers, y, z_to), targets, semaphores)
    arrived = [
        jnp.concatenate(
            [
                jnp.concatenate(
                    [data[pl.ds(4 * r + 2 * field + side, 256, stride=8), :] for side in range(2)],
                    axis=1,
                )
                for r in range(2)
            ],
            axis=0,
        )
        for field in range(2)
    ]
    z_from_ref, numbers = fetch[0], fetch[1]

    def coefficient(i):
        return numbers[:, i : i + 1]

    across, along = forward_z(z_from_ref, coefficient, arrived)
    waves = [x + z for x, z in zip(across, derivative_z(coefficient, 9, along))]
    waves = blocks_of(right(jnp.concatenate(waves, axis=0), fetch[2]))
    scale = DIVERGENCE_LINK / MIDDLE_LINK / (NZ * NY)
    waves = [x * (kappa_rows(where[0] % HALF, part) * scale) for part, x in enumerate(waves)]
    waves = blocks_of(right(jnp.concatenate(waves, axis=0), fetch[2]))
    plane = inverse_z(fetch[3], coefficient, [waves])
    early = first_half()
    for pair in range(4):
        for side in range(2):
            rows = slice(64 * pair, 64 * (pair + 1))
            even = plane[rows, HALF * side : HALF * (side + 1)]
            odd = plane[rows, NY + HALF * side : NY + HALF * (side + 1)]
            out[pl.ds(8 * side + pair, 64, stride=16), :] = jnp.where(
                early, even, pltpu.roll(odd, ROWS, 1)
            )
            out[pl.ds(8 * side + 4 + pair, 64, stride=16), :] = jnp.where(
                early, pltpu.roll(even, ROWS, 1), odd
            )


def new_pressure_kernel(data, x_table, pressure, bulk, own, passed, out, held, x_ref, semaphores):
    fetch = Fetch((x_table,), (x_ref,), semaphores)
    sent = []
    for i in range(4):
        planes = pl.ds(2 * i, 2)
        components = data[pl.ds(i, 256, stride=4), :]
        lines = to_lines(components, fetch[0]) * (X_SCALE / DIVERGENCE_LINK)
        held[planes] = pressure[planes] - bulk[planes] * lines.reshape(2, ROWS, NX) + own[planes]
        held[planes, :TILE, :] += passed[planes].astype(f32)
        sent.append(pltpu.make_async_copy(held.at[planes], out.at[planes], semaphores.at[1 + i]))
        sent[i].start()
    for copy in sent:
        copy.wait()


def source_kernel(where, lives, c0, c1, c2, t0, t1, t2, own, passed, l0, l1, l2):
    blank = jnp.zeros((SLAB, 256, NX), bf16)
    l0[:SLAB] = blank
    l2[SLAB:] = blank
    corners = (c0, c1, c2)

    def place(slot, carry):
        rows = pl.ds(pl.multiple_of(slot * TILE, TILE), TILE)
        lane = lax.broadcasted_iota(jnp.int32, (TILE, NX), 1)
        line = lax.broadcasted_iota(jnp.int32, (TILE, NX), 0)
        for reach, (tiles, placed) in enumerate(((t0, l0), (t1, l1), (t2, l2))):
            offset = corners[reach][slot, 0] & (SLAB - 1)
            hot = ((lane - line - corners[reach][slot, 2]) & (NX - 1)) == 0
            hot = jnp.where(hot, 1.0, 0.0).astype(bf16)
            first = SLAB - offset if reach == 1 else 0
            to = 0 if reach == 1 else offset
            block = tiles[slot, pl.ds(first, SLAB)].reshape(SLAB * TILE, TILE)
            across = jnp.dot(block, hot, preferred_element_type=f32).astype(bf16)
            placed[pl.ds(to, SLAB), rows, :] = across.reshape(SLAB, TILE, NX)
        return carry

    lax.fori_loop(0, SLOTS_HERE, place, 0)
    line = lax.broadcasted_iota(jnp.int32, (ROWS + TILE, 256), 0)
    lane = lax.broadcasted_iota(jnp.int32, (ROWS + TILE, 256), 1)
    hots = []
    for reach in range(3):
        sender = ((where[0] + PEERS_Z - reach) % PEERS_Z) * PEERS_Y + where[1]
        start = jnp.full((ROWS + TILE, 256), -2 * TILE, jnp.int32)
        for slot in range(SLOTS_HERE):
            row = corners[reach][slot, 1] - where[1] * ROWS - slot * TILE
            row = jnp.where(slot < lives[sender], row, -NX)
            start = jnp.where(lane // TILE == slot, lane + row, start)
        hots.append(jnp.where(line == start, 1.0, 0.0).astype(bf16))
    for z in range(SLAB):
        window = jnp.dot(hots[0], l0[z], preferred_element_type=f32)
        window += jnp.dot(hots[1], l1[z], preferred_element_type=f32)
        window += jnp.dot(hots[2], l2[SLAB + z], preferred_element_type=f32)
        own[z] = window[:ROWS]
        passed[z] = window[ROWS:].astype(bf16)


VMEM = pl.BlockSpec(memory_space=pltpu.VMEM)
SMEM = pl.BlockSpec(memory_space=pltpu.SMEM)
ANY = pl.BlockSpec(memory_space=pl.ANY)


def call(
    kernel, name, scalars, arrays, far, shapes, scratch=(), far_out=0, targets=None, extra=0, limit=16
):
    if targets is None:
        targets = [(x.shape, x.dtype) for x in far]
    scratch = [pltpu.VMEM(shape, kind) for shape, kind in (*scratch, *targets)]
    if far:
        scratch.append(pltpu.SemaphoreType.DMA((len(targets) + extra,)))
    return pl.pallas_call(
        kernel,
        out_shape=[jax.ShapeDtypeStruct(shape, kind) for shape, kind in shapes],
        in_specs=[SMEM] * len(scalars) + [VMEM] * len(arrays) + [ANY] * len(far),
        out_specs=[ANY] * far_out + [VMEM] * (len(shapes) - far_out),
        scratch_shapes=scratch,
        compiler_params=pltpu.CompilerParams(vmem_limit_bytes=limit << 20),
        cost_estimate=pl.CostEstimate(flops=int(4e8), bytes_accessed=1 << 20, transcendentals=0),
        name=name,
    )(*scalars, *arrays, *far)


def from_behind(x, axis, by):
    peers = lax.axis_size(axis)
    return lax.ppermute(x, axis, [(i, (i + by) % peers) for i in range(peers)])


def to_planes(fields, row_block):
    axis = fields.ndim - 3

    def planes_of(device):
        return lax.dynamic_slice_in_dim(fields, 2 * device, 2, axis)

    blocks = [planes_of(row_block)]
    for ahead in range(1, PEERS_Y):
        sent = planes_of((row_block + ahead) % PEERS_Y).astype(f16)
        blocks.append(from_behind(sent, "gy", ahead))
    return blocks


def to_rows(blocks, row_block, axis):
    arrived = [blocks[0]] + [
        from_behind(blocks[ahead].astype(f16), "gy", ahead).astype(f32)
        for ahead in range(1, PEERS_Y)
    ]
    ordered = []
    for device in range(PEERS_Y):
        back = (row_block - device) % PEERS_Y
        ordered.append(lax.select_n(back, *arrived))
    return jnp.concatenate(ordered, axis)


def exchange(columns, rows):
    blocks = columns.astype(f16).reshape(256, rows, HALF)
    return lax.all_to_all(blocks, ("gz", "gy"), 0, 0, tiled=True)


def arrived(moved):
    return moved.reshape(-1, HALF).astype(f32)


def local(pressure, velocity, bulk, buoyancy, tiles, tile_corner, live_count):
    slab_index = lax.axis_index("gz")
    row_block = lax.axis_index("gy")
    here = row_block.reshape(1).astype(jnp.int32)
    device = (slab_index * PEERS_Y + row_block).reshape(1).astype(jnp.int32)
    place = jnp.stack([slab_index, row_block]).astype(jnp.int32)
    table = {key: jnp.asarray(value) for key, value in TABLES.items()}

    (components,) = call(
        forward_lines_kernel,
        "forward_lines",
        [],
        [],
        [pressure, table["x_forward"]],
        [((1024, HALF), f32)],
        targets=[((256, 768), bf16)] + [((2, ROWS, NX), f32)] * 4,
    )
    velocity, buoyancy, tiles, tile_corner, components = lax.optimization_barrier(
        (velocity, buoyancy, tiles, tile_corner, components)
    )
    field_blocks = to_planes(jnp.concatenate([velocity, buoyancy[None]]), row_block)
    packed = tiles.reshape(SLOTS_HERE, 2 * SLAB, 8, HALF)
    tiles_before = from_behind(packed, "gz", 1)
    tiles_second = from_behind(packed[:, SLAB:], "gz", 2)
    moved, *field_blocks = lax.optimization_barrier((exchange(components, 4), *field_blocks))
    (filtered,) = call(
        filter_out_kernel,
        "filter_out",
        [device],
        [arrived(moved)],
        [table["y_waves"], table["z_from_slabs"], table["z_to_pairs"], table["z_coefficients"]],
        [((2048, HALF), f32)],
        [((NZ, NY), f32)],
        targets=[((768, 256), bf16), ((256, 768), bf16), ((HALF, HALF), f32), ((256, 768), bf16)],
    )
    moved, tiles_before, tiles_second = lax.optimization_barrier(
        (exchange(filtered, 8), tiles_before, tiles_second)
    )
    slopes, middle = call(
        middle_kernel,
        "middle",
        [here],
        [arrived(moved), *[block.astype(f32) for block in field_blocks]],
        [
            table[key]
            for key in (
                "x_inverse_both", "x_inverse", "y_ahead", "y_behind", "x_forward_behind", "x_forward"
            )
        ],
        [((2, 3, NY, NX), f32), ((2048, HALF), f32)],
        [((4, 2, NY, NX), f32), ((2, 3, NY, NX), f32)],
        far_out=1,
        extra=2,
        limit=24,
    )
    slope_blocks = [
        lax.dynamic_slice_in_dim(slopes, ROWS * ((row_block + ahead) % PEERS_Y), ROWS, 2)
        for ahead in range(PEERS_Y)
    ]
    slopes_here = jnp.swapaxes(to_rows(slope_blocks, row_block, 0), 0, 1)
    new_velocity = velocity - buoyancy[None] * (slopes_here * (1.0 / SLOPE_LINK))

    corners = [
        lax.dynamic_slice_in_dim(
            tile_corner,
            ((slab_index - reach) % PEERS_Z * PEERS_Y + row_block) * SLOTS_HERE,
            SLOTS_HERE,
            0,
        )
        for reach in range(3)
    ]
    own, passed = call(
        source_kernel,
        "source",
        [place, live_count, *corners],
        [
            tiles,
            tiles_before.reshape(SLOTS_HERE, 2 * SLAB, TILE, TILE),
            tiles_second.reshape(SLOTS_HERE, SLAB, TILE, TILE),
        ],
        [],
        [((SLAB, ROWS, NX), f32), ((SLAB, TILE, NX), bf16)],
        [((2 * SLAB, 256, NX), bf16), ((SLAB, 256, NX), bf16), ((2 * SLAB, 256, NX), bf16)],
    )
    moved, own, passed = lax.optimization_barrier((exchange(middle, 8), own, passed))
    passed = from_behind(passed, "gy", 1)
    (filtered_back,) = call(
        filter_back_kernel,
        "filter_back",
        [device],
        [arrived(moved)],
        [table["y_waves"], table["z_from_pairs"], table["z_to_slabs"], table["z_coefficients"]],
        [((1024, HALF), f32)],
        targets=[((256, 768), bf16), ((HALF, HALF), f32), ((768, 256), bf16), ((256, 768), bf16)],
    )
    moved, new_velocity, passed = lax.optimization_barrier(
        (exchange(filtered_back, 4), new_velocity, passed)
    )
    (new_pressure,) = pl.pallas_call(
        new_pressure_kernel,
        out_shape=[jax.ShapeDtypeStruct((SLAB, ROWS, NX), f32)],
        in_specs=[VMEM, ANY, VMEM, VMEM, VMEM, VMEM],
        out_specs=[ANY],
        scratch_shapes=[
            pltpu.VMEM((SLAB, ROWS, NX), f32),
            pltpu.VMEM((768, 256), bf16),
            pltpu.SemaphoreType.DMA((5,)),
        ],
        compiler_params=pltpu.CompilerParams(vmem_limit_bytes=16 << 20),
        name="new_pressure",
    )(arrived(moved), table["x_inverse"], pressure, bulk, own, passed)
    return (new_pressure, new_velocity)


def solution(mesh):
    in_specs = (
        P("gz", "gy", None),
        P(None, "gz", "gy", None),
        P("gz", "gy", None),
        P("gz", "gy", None),
        P(("gz", "gy"), None, None, None),
        P(),
        P(),
    )
    out_specs = (P("gz", "gy", None), P(None, "gz", "gy", None))
    return jax.shard_map(local, mesh=mesh, in_specs=in_specs, out_specs=out_specs, check_vma=False)
```

```python
import math

import jax
import jax.numpy as jnp
import ml_dtypes
import numpy as np
from jax import lax
from jax.experimental import pallas as pl
from jax.experimental.pallas import tpu as pltpu
from jax.sharding import PartitionSpec as P

NX = 256
NY = 256
NZ = 512
HALF = 128
ROWS = 64
SLAB = 8
SLOTS_HERE = 8
TILE = 32
PEERS_Y = 4
PEERS_Z = 64
kappa_courant = 0.3
f32 = jnp.float32
bf16 = jnp.bfloat16
f16 = jnp.float16

X_SCALE = 1.0 / 16.0
SLOPE_LINK = 0.25
MIDDLE_LINK = 1.0 / 16.0
DIVERGENCE_LINK = 1.0 / 32.0


def split_table(table):
    high = table.astype(ml_dtypes.bfloat16)
    low = (table - high.astype(np.float64)).astype(ml_dtypes.bfloat16)
    return high, low


def left_table(table):
    high, low = split_table(table)
    return np.concatenate([high, high, low], axis=1)


def right_table(table):
    return np.ascontiguousarray(left_table(table.T).T)


def signed_waves(length):
    index = np.arange(length)
    return 2.0 * np.pi / length * np.where(index < length // 2, index, index - length)


def derivative_matrix(length, orientation):
    wave = signed_waves(length)
    kernel = np.fft.ifft(1j * wave * np.exp(orientation * 0.5j * wave)).real
    index = np.arange(length)
    return kernel[(index[:, None] - index[None, :]) % length]


def make_tables():
    index = np.arange(256)
    angle = 2.0 * np.pi / 256 * (np.outer(index, index) % 256)
    wave_x = 2.0 * np.pi / NX * np.arange(HALF)

    def forward_x(factor):
        spectrum = np.exp(-1j * angle[:HALF]) * factor[:, None]
        return left_table(np.concatenate([spectrum.real, spectrum.imag], axis=0))

    def inverse_x(factor):
        weight = np.where(np.arange(HALF) == 0, 1.0, 2.0) * factor
        wave = np.exp(1j * angle[:HALF]) * weight[:, None]
        return np.concatenate([wave.real, -wave.imag], axis=0)

    ahead = 1j * wave_x * np.exp(0.5j * wave_x)
    behind = 1j * wave_x * np.exp(-0.5j * wave_x)
    plain = np.ones(HALF)
    forward_z = np.concatenate([np.cos(angle[:HALF]), -np.sin(angle[:HALF])], axis=0)
    forward_z[HALF] = np.cos(angle[HALF])
    inverse_z = 2.0 * forward_z.T
    inverse_z[:, 0] = forward_z[0]
    inverse_z[:, HALF] = forward_z[HALF]
    slab_order = (4 * np.arange(64)[None, :] + np.arange(4)[:, None]).reshape(-1)
    low = np.arange(HALF)
    high = low - 256
    coefficients = np.zeros((HALF, HALF), np.float32)
    coefficients[:, 0] = np.cos(2.0 * np.pi / NZ * low)
    coefficients[:, 1] = np.sin(2.0 * np.pi / NZ * low)

    def derivative(number, orientation):
        wave = 2.0 * np.pi / NZ * number
        return -orientation * wave * np.sin(0.5 * wave), wave * np.cos(0.5 * wave)

    for first, orientation in ((2, 1.0), (9, -1.0)):
        middle_real, middle_imag = derivative(128, orientation)
        for at, number in ((first, low), (first + 3, high)):
            real, imag = derivative(number, orientation)
            coefficients[:, at] = real
            coefficients[:, at + 1] = np.where((low == 0), 0.0, imag)
            coefficients[:, at + 2] = np.where((low == 0), middle_real, real)
        coefficients[:, first + 6] = np.where((low == 0), middle_imag, 0.0)
    return {
        "x_forward": forward_x(plain),
        "x_forward_behind": forward_x(behind),
        "x_inverse": right_table(inverse_x(plain)),
        "x_inverse_both": right_table(
            np.concatenate([inverse_x(ahead), inverse_x(plain)], axis=1)
        ),
        "y_ahead": left_table(derivative_matrix(NY, 1.0)),
        "y_behind": left_table(derivative_matrix(NY, -1.0)),
        "y_waves": right_table(np.cos(angle) + np.sin(angle)),
        "z_from_slabs": left_table(forward_z[:, slab_order]),
        "z_to_pairs": left_table(inverse_z),
        "z_from_pairs": left_table(forward_z),
        "z_to_slabs": left_table(inverse_z[slab_order]),
        "z_coefficients": coefficients,
    }


TABLES = make_tables()


def pieces(x, axis):
    high = x.astype(bf16)
    low = (x - high.astype(f32)).astype(bf16)
    return jnp.concatenate([high, low, high], axis=axis)


def contract(a, b, a_dim, b_dim):
    return lax.dot_general(a, b, (((a_dim,), (b_dim,)), ((), ())), preferred_element_type=f32)


def left(table_ref, x):
    return contract(table_ref[...], pieces(x, 0), 1, 0)


def right(x, table_ref):
    return contract(pieces(x, 1), table_ref[...], 1, 0)


def to_components(table_ref, lines):
    return contract(table_ref[...], pieces(lines, 1), 1, 1)


def to_lines(components, table_ref):
    return right(components.T, table_ref)


class Fetch:
    def __init__(self, sources, targets, semaphores):
        self.targets = targets
        self.copies = [
            pltpu.make_async_copy(source, target, semaphores.at[i])
            for i, (source, target) in enumerate(zip(sources, targets))
        ]
        for copy in self.copies:
            copy.start()

    def __getitem__(self, i):
        if self.copies[i] is not None:
            self.copies[i].wait()
            self.copies[i] = None
        return self.targets[i]


def kappa_rows(kx, part):
    kz = lax.broadcasted_iota(jnp.int32, (HALF, NY), 0)
    ky = lax.broadcasted_iota(jnp.int32, (HALF, NY), 1)
    number = kz - 256 * (part // 2)
    if part % 2:
        number = jnp.where(kz == 0, 128, number)
    wave_z = number.astype(f32) * (2.0 * math.pi / NZ)
    wave_y = jnp.where(ky < NY // 2, ky, ky - NY).astype(f32) * (2.0 * math.pi / NY)
    wave_x = jnp.full((HALF, NY), kx, jnp.int32).astype(f32) * (2.0 * math.pi / NX)
    square = (kappa_courant / 2.0) ** 2 * (wave_x * wave_x + wave_z * wave_z + wave_y * wave_y)
    total = jnp.full((HALF, NY), 1.0 / math.factorial(15), f32)
    for order in range(6, -1, -1):
        total = 1.0 / math.factorial(2 * order + 1) - square * total
    return total


def forward_z(table_ref, coefficient, fields):
    sides = [side for field in fields for side in (field[:256], field[256:])]
    sums = left(table_ref, jnp.concatenate(sides, axis=1))
    cosine, sine = coefficient(0), coefficient(1)
    spectra = []
    for i in range(0, len(sides), 2):
        even = sums[:, NY * i : NY * (i + 1)]
        odd = sums[:, NY * (i + 1) : NY * (i + 2)]
        real = cosine * odd[:HALF] + sine * odd[HALF:]
        imag = cosine * odd[HALF:] - sine * odd[:HALF]
        spectra.append(
            [even[:HALF] + real, even[HALF:] + imag, even[:HALF] - real, even[HALF:] - imag]
        )
    return spectra


def inverse_z(table_ref, coefficient, spectra):
    cosine, sine = coefficient(0), coefficient(1)
    sides = []
    for a, b, c, d in spectra:
        real, imag = a - c, b - d
        sides.append(jnp.concatenate([a + c, b + d], axis=0))
        sides.append(jnp.concatenate([cosine * real - sine * imag, cosine * imag + sine * real], axis=0))
    return left(table_ref, jnp.concatenate(sides, axis=1))


def derivative_z(coefficient, first, spectrum):
    a, b, c, d = spectrum
    mixed = coefficient(first + 6)
    return [
        coefficient(first) * a - coefficient(first + 1) * b,
        coefficient(first + 2) * b + coefficient(first + 1) * a - mixed * d,
        coefficient(first + 3) * c - coefficient(first + 4) * d,
        coefficient(first + 5) * d + coefficient(first + 4) * c + mixed * b,
    ]


def blocks_of(x):
    return [x[HALF * i : HALF * (i + 1)] for i in range(4)]


def first_half():
    return lax.broadcasted_iota(jnp.int32, (64, HALF), 1) < ROWS


def forward_lines_kernel(pressure, x_table, out, *scratch):
    *targets, semaphores = scratch
    sources = [x_table] + [pressure.at[pl.ds(2 * i, 2)] for i in range(4)]
    fetch = Fetch(sources, targets, semaphores)
    x_ref = fetch[0]
    for i in range(4):
        lines = fetch[i + 1][...].reshape(HALF, NX)
        out[pl.ds(i, 256, stride=4), :] = to_components(x_ref, lines) * X_SCALE


def filter_out_kernel(where, data, y, z_from, z_to, z_numbers, out, plane, *scratch):
    *targets, semaphores = scratch
    fetch = Fetch((y, z_from, z_numbers, z_to), targets, semaphores)
    early = first_half()
    for pair in range(4):
        for side in range(2):
            a = data[pl.ds(8 * side + pair, 64, stride=16), :]
            b = data[pl.ds(8 * side + 4 + pair, 64, stride=16), :]
            span = pl.ds(HALF * side, HALF)
            plane[pl.ds(64 * pair, 64), span] = jnp.where(early, a, pltpu.roll(b, ROWS, 1))
            plane[pl.ds(256 + 64 * pair, 64), span] = jnp.where(early, pltpu.roll(a, ROWS, 1), b)
    mixed = right(plane[...], fetch[0])
    z_from_ref, numbers = fetch[1], fetch[2]

    def coefficient(i):
        return numbers[:, i : i + 1]

    (spectrum,) = forward_z(z_from_ref, coefficient, [mixed])
    scale = SLOPE_LINK / (NZ * NY)
    waves = [x * (kappa_rows(where[0] % HALF, part) * scale) for part, x in enumerate(spectrum)]
    waves = blocks_of(right(jnp.concatenate(waves, axis=0), fetch[0]))
    planes = inverse_z(fetch[3], coefficient, [waves, derivative_z(coefficient, 2, waves)])
    for field in range(2):
        for r in range(2):
            for side in range(2):
                start = NY * (2 * field + r) + HALF * side
                out[pl.ds(4 * r + 2 * field + side, 256, stride=8), :] = planes[
                    :, start : start + HALF
                ]


def middle_kernel(
    where, data, xib, xi, ya, yb, xfb, xf, velocity, buoyancy, near, f2, slopes, out, held, *scratch
):
    *targets, fields, semaphores = scratch
    own = pl.ds(2 * where[0], 2)
    starts = [
        pl.ds(pl.multiple_of(((where[0] + PEERS_Y - back) % PEERS_Y) * ROWS, ROWS), ROWS)
        for back in range(PEERS_Y)
    ]
    blocks = Fetch(
        (velocity.at[:, own], buoyancy.at[own], near.at[0], f2, near.at[1]),
        (
            fields.at[pl.ds(0, 3), :, starts[0]],
            fields.at[3, :, starts[0]],
            *[fields.at[:, :, starts[back]] for back in (1, 2, 3)],
        ),
        semaphores.at[pl.ds(8, 5)],
    )
    fetch = Fetch((xib, xi, ya, yb, xfb, xf), targets, semaphores)
    returned = []
    for r in range(2):
        q, g = [
            jnp.concatenate(
                [data[pl.ds(4 * r + 2 * field + side, 256, stride=8), :] for side in range(2)], axis=1
            )
            for field in range(2)
        ]
        both = to_lines(q, fetch[0]) * X_SCALE
        along = (both[:, :NX], left(fetch[2], both[:, NX:]), to_lines(g, fetch[1]) * X_SCALE)
        if r == 0:
            for i in range(5):
                blocks[i]
        moved = []
        for d, slope in enumerate(along):
            held[r, d] = slope
            moved.append(fields[d, r] - fields[3, r] * (slope * (1.0 / SLOPE_LINK)))
        returned.append(pltpu.make_async_copy(held.at[r], slopes.at[:, r], semaphores.at[6 + r]))
        returned[r].start()
        scale = X_SCALE * MIDDLE_LINK
        along_y = left(fetch[3], moved[1])
        summed = to_components(fetch[4], moved[0]) + to_components(fetch[5], along_y)
        for field, components in enumerate(
            (summed * scale, to_components(fetch[5], moved[2]) * scale)
        ):
            for side in range(2):
                out[pl.ds(4 * r + 2 * field + side, 256, stride=8), :] = components[
                    :, HALF * side : HALF * (side + 1)
                ]
    for copy in returned:
        copy.wait()


def filter_back_kernel(where, data, y, z_from, z_to, z_numbers, out, *scratch):
    *targets, semaphores = scratch
    fetch = Fetch((z_from, z_numbers, y, z_to), targets, semaphores)
    arrived = [
        jnp.concatenate(
            [
                jnp.concatenate(
                    [data[pl.ds(4 * r + 2 * field + side, 256, stride=8), :] for side in range(2)],
                    axis=1,
                )
                for r in range(2)
            ],
            axis=0,
        )
        for field in range(2)
    ]
    z_from_ref, numbers = fetch[0], fetch[1]

    def coefficient(i):
        return numbers[:, i : i + 1]

    across, along = forward_z(z_from_ref, coefficient, arrived)
    waves = [x + z for x, z in zip(across, derivative_z(coefficient, 9, along))]
    waves = blocks_of(right(jnp.concatenate(waves, axis=0), fetch[2]))
    scale = DIVERGENCE_LINK / MIDDLE_LINK / (NZ * NY)
    waves = [x * (kappa_rows(where[0] % HALF, part) * scale) for part, x in enumerate(waves)]
    waves = blocks_of(right(jnp.concatenate(waves, axis=0), fetch[2]))
    plane = inverse_z(fetch[3], coefficient, [waves])
    early = first_half()
    for pair in range(4):
        for side in range(2):
            rows = slice(64 * pair, 64 * (pair + 1))
            even = plane[rows, HALF * side : HALF * (side + 1)]
            odd = plane[rows, NY + HALF * side : NY + HALF * (side + 1)]
            out[pl.ds(8 * side + pair, 64, stride=16), :] = jnp.where(
                early, even, pltpu.roll(odd, ROWS, 1)
            )
            out[pl.ds(8 * side + 4 + pair, 64, stride=16), :] = jnp.where(
                early, pltpu.roll(even, ROWS, 1), odd
            )


def new_pressure_kernel(data, x_table, *rest):
    out, held, x_ref, semaphores = rest[5:6] + rest[-3:]
    near = rest[6:11]
    fetch = Fetch((x_table, *rest[:5]), (x_ref, *near), semaphores.at[pl.ds(4, 6)])
    sent = []
    for i in range(4):
        planes = pl.ds(2 * i, 2)
        components = data[pl.ds(i, 256, stride=4), :]
        lines = to_lines(components, fetch[0]) * (X_SCALE / DIVERGENCE_LINK)
        pressure, bulk, *source = [fetch[1 + j][planes].astype(f32) for j in range(5)]
        held[planes] = (
            pressure - bulk * lines.reshape(2, ROWS, NX) + (source[0] + source[1] + source[2])
        )
        sent.append(pltpu.make_async_copy(held.at[planes], out.at[planes], semaphores.at[i]))
        sent[i].start()
    for copy in sent:
        copy.wait()


def source_kernel(where, lives, corner, tiles, own, passed, lifted):
    lifted[:SLAB] = jnp.zeros((SLAB, 256, NX), bf16)
    lifted[2 * SLAB :] = jnp.zeros((SLAB, 256, NX), bf16)

    def place(slot, carry):
        rows = pl.ds(pl.multiple_of(slot * TILE, TILE), TILE)
        lane = lax.broadcasted_iota(jnp.int32, (TILE, NX), 1)
        line = lax.broadcasted_iota(jnp.int32, (TILE, NX), 0)
        hot = ((lane - line - corner[slot, 2]) & (NX - 1)) == 0
        hot = jnp.where(hot, 1.0, 0.0).astype(bf16)
        block = tiles[slot].reshape(2 * SLAB * TILE, TILE)
        across = jnp.dot(block, hot, preferred_element_type=f32).astype(bf16)
        planes = pl.ds(corner[slot, 0] & (SLAB - 1), 2 * SLAB)
        lifted[planes, rows, :] = across.reshape(2 * SLAB, TILE, NX)
        return carry

    lax.fori_loop(0, SLOTS_HERE, place, 0)
    line = lax.broadcasted_iota(jnp.int32, (ROWS + TILE, 256), 0)
    lane = lax.broadcasted_iota(jnp.int32, (ROWS + TILE, 256), 1)
    start = jnp.full((ROWS + TILE, 256), -2 * TILE, jnp.int32)
    for slot in range(SLOTS_HERE):
        row = corner[slot, 1] - where[1] * ROWS - slot * TILE
        row = jnp.where(slot < lives[where[0] * PEERS_Y + where[1]], row, -2 * NX)
        start = jnp.where(lane // TILE == slot, lane + row, start)
    hot = jnp.where(line == start, 1.0, 0.0).astype(bf16)
    for z in range(3 * SLAB):
        window = jnp.dot(hot, lifted[z], preferred_element_type=f32)
        own[z] = window[:ROWS]
        passed[z] = window[ROWS:].astype(bf16)


def source_rows_kernel(own, passed, here, after, second):
    for first, out in ((0, here), (SLAB, after), (2 * SLAB, second)):
        planes = pl.ds(first, SLAB)
        out[...] = own[planes].astype(out.dtype)
        out[:, :TILE, :] = (own[planes, :TILE, :] + passed[planes].astype(f32)).astype(out.dtype)


VMEM = pl.BlockSpec(memory_space=pltpu.VMEM)
SMEM = pl.BlockSpec(memory_space=pltpu.SMEM)
FAR = pl.BlockSpec(memory_space=pltpu.HBM)


def call(kernel, name, specs, arrays, shapes, outs, scratch=(), semaphores=0, limit=16):
    scratch = [pltpu.VMEM(shape, kind) for shape, kind in scratch]
    if semaphores:
        scratch.append(pltpu.SemaphoreType.DMA((semaphores,)))
    return pl.pallas_call(
        kernel,
        out_shape=[jax.ShapeDtypeStruct(shape, kind) for shape, kind in shapes],
        in_specs=specs,
        out_specs=outs,
        scratch_shapes=scratch,
        compiler_params=pltpu.CompilerParams(vmem_limit_bytes=limit << 20),
        cost_estimate=pl.CostEstimate(flops=int(4e8), bytes_accessed=1 << 20, transcendentals=0),
        name=name,
    )(*arrays)


def from_behind(x, axis, by):
    peers = lax.axis_size(axis)
    return lax.ppermute(x, axis, [(i, (i + by) % peers) for i in range(peers)])


def to_rows(slopes, row_block):
    blocks = [
        lax.dynamic_slice_in_dim(slopes, ROWS * ((row_block + ahead) % PEERS_Y), ROWS, 2)
        for ahead in range(PEERS_Y)
    ]
    arrived = [blocks[0]] + [
        from_behind(blocks[ahead].astype(f16), "gy", ahead).astype(f32)
        for ahead in range(1, PEERS_Y)
    ]
    ordered = [
        lax.select_n((row_block - device) % PEERS_Y, *arrived) for device in range(PEERS_Y)
    ]
    return jnp.concatenate(ordered, 1)


def exchange(columns, rows):
    blocks = columns.astype(f16).reshape(256, rows, HALF)
    return lax.all_to_all(blocks, ("gz", "gy"), 0, 0, tiled=True)


def arrived(moved):
    return moved.reshape(-1, HALF).astype(f32)


def local(pressure, velocity, bulk, buoyancy, tiles, tile_corner, live_count):
    slab_index = lax.axis_index("gz")
    row_block = lax.axis_index("gy")
    here = row_block.reshape(1).astype(jnp.int32)
    device = (slab_index * PEERS_Y + row_block).astype(jnp.int32)
    place = jnp.stack([slab_index, row_block]).astype(jnp.int32)
    table = {key: jnp.asarray(value) for key, value in TABLES.items()}
    wide, tall = ((256, 768), bf16), ((768, 256), bf16)
    numbers = ((HALF, HALF), f32)
    planes = ((SLAB, ROWS, NX), f32)

    (components,) = call(
        forward_lines_kernel,
        "forward_lines",
        [FAR, FAR],
        [pressure, table["x_forward"]],
        [((1024, HALF), f32)],
        [VMEM],
        [wide] + [((2, ROWS, NX), f32)] * 4,
        5,
    )
    velocity_later, buoyancy_later, tiles, tile_corner, components = lax.optimization_barrier(
        (velocity, buoyancy, tiles, tile_corner, components)
    )
    fields = jnp.concatenate([velocity_later, buoyancy_later[None]])
    sent = [
        lax.dynamic_slice_in_dim(fields, 2 * ((row_block + ahead) % PEERS_Y), 2, 1).astype(f16)
        for ahead in range(1, PEERS_Y)
    ]
    first, third = from_behind(sent[0], "gy", 1), from_behind(sent[2], "gy", 3)
    moved, sent[1] = lax.optimization_barrier((exchange(components, 4), sent[1]))
    (filtered,) = call(
        filter_out_kernel,
        "filter_out",
        [SMEM, VMEM, FAR, FAR, FAR, FAR],
        [
            device.reshape(1),
            arrived(moved),
            table["y_waves"],
            table["z_from_slabs"],
            table["z_to_pairs"],
            table["z_coefficients"],
        ],
        [((2048, HALF), f32)],
        [VMEM],
        [((NZ, NY), f32), tall, wide, numbers, wide],
        4,
    )
    filtered, first, third, second, tiles, tile_corner = lax.optimization_barrier(
        (filtered, first, third, sent[1], tiles, tile_corner)
    )
    second = from_behind(second, "gy", 2)
    corner = lax.dynamic_slice_in_dim(tile_corner, device * SLOTS_HERE, SLOTS_HERE, 0)
    source, passed = call(
        source_kernel,
        "source",
        [SMEM, SMEM, SMEM, VMEM],
        [place, live_count, corner, tiles],
        [((3 * SLAB, ROWS, NX), f32), ((3 * SLAB, TILE, NX), bf16)],
        [VMEM, VMEM],
        [((3 * SLAB, 256, NX), bf16)],
    )
    passed = from_behind(passed, "gy", 1)
    moved, source, passed, second = lax.optimization_barrier(
        (exchange(filtered, 8), source, passed, second)
    )
    slopes, middle = call(
        middle_kernel,
        "middle",
        [SMEM, VMEM] + [FAR] * 10,
        [
            here,
            arrived(moved),
            table["x_inverse_both"],
            table["x_inverse"],
            table["y_ahead"],
            table["y_behind"],
            table["x_forward_behind"],
            table["x_forward"],
            velocity,
            buoyancy,
            jnp.stack([first, third]).astype(f32),
            second.astype(f32),
        ],
        [((3, 2, NY, NX), f32), ((2048, HALF), f32)],
        [FAR, VMEM],
        [
            ((2, 3, NY, NX), f32),
            ((768, 512), bf16),
            tall,
            wide,
            wide,
            wide,
            wide,
            ((4, 2, NY, NX), f32),
        ],
        13,
        24,
    )
    new_velocity = velocity - buoyancy[None] * (to_rows(slopes, row_block) * (1.0 / SLOPE_LINK))
    own, after, beyond = call(
        source_rows_kernel,
        "source_rows",
        [VMEM, VMEM],
        [source, passed],
        [planes, ((SLAB, ROWS, NX), bf16), ((SLAB, ROWS, NX), bf16)],
        [VMEM, VMEM, VMEM],
    )
    moved, own, after, beyond = lax.optimization_barrier((exchange(middle, 8), own, after, beyond))
    after, beyond = from_behind(after, "gz", 1), from_behind(beyond, "gz", 2)
    (filtered_back,) = call(
        filter_back_kernel,
        "filter_back",
        [SMEM, VMEM, FAR, FAR, FAR, FAR],
        [
            device.reshape(1),
            arrived(moved),
            table["y_waves"],
            table["z_from_pairs"],
            table["z_to_slabs"],
            table["z_coefficients"],
        ],
        [((1024, HALF), f32)],
        [VMEM],
        [wide, numbers, tall, wide],
        4,
    )
    moved, new_velocity, after, beyond = lax.optimization_barrier(
        (exchange(filtered_back, 4), new_velocity, after, beyond)
    )
    (new_pressure,) = call(
        new_pressure_kernel,
        "new_pressure",
        [VMEM] + [FAR] * 6,
        [arrived(moved), table["x_inverse"], pressure, bulk, own, after, beyond],
        [planes],
        [FAR],
        [planes, planes, planes, *[((SLAB, ROWS, NX), bf16)] * 2, planes, tall],
        10,
    )
    return (new_pressure, new_velocity)


def solution(mesh):
    in_specs = (
        P("gz", "gy", None),
        P(None, "gz", "gy", None),
        P("gz", "gy", None),
        P("gz", "gy", None),
        P(("gz", "gy"), None, None, None),
        P(),
        P(),
    )
    out_specs = (P("gz", "gy", None), P(None, "gz", "gy", None))
    return jax.shard_map(local, mesh=mesh, in_specs=in_specs, out_specs=out_specs, check_vma=False)
```

```python
import math

import jax
import jax.numpy as jnp
import ml_dtypes
import numpy as np
from jax import lax
from jax.experimental import pallas as pl
from jax.experimental.pallas import tpu as pltpu
from jax.sharding import PartitionSpec as P

NX = 256
NY = 256
NZ = 512
HALF = 128
ROWS = 64
SLAB = 8
SLOTS_HERE = 8
TILE = 32
PEERS_Y = 4
PEERS_Z = 64
kappa_courant = 0.3
f32 = jnp.float32
bf16 = jnp.bfloat16
f16 = jnp.float16

X_SCALE = 1.0 / 16.0
SLOPE_LINK = 0.25
MIDDLE_LINK = 1.0 / 16.0
DIVERGENCE_LINK = 1.0 / 32.0


def split_table(table):
    high = table.astype(ml_dtypes.bfloat16)
    low = (table - high.astype(np.float64)).astype(ml_dtypes.bfloat16)
    return high, low


def packed_table(table):
    return np.concatenate(split_table(table), axis=1)


def signed_waves(length):
    index = np.arange(length)
    return 2.0 * np.pi / length * np.where(index < length // 2, index, index - length)


def derivative_matrix(length, orientation):
    wave = signed_waves(length)
    kernel = np.fft.ifft(1j * wave * np.exp(orientation * 0.5j * wave)).real
    index = np.arange(length)
    return kernel[(index[:, None] - index[None, :]) % length]


def make_tables():
    index = np.arange(256)
    angle = 2.0 * np.pi / 256 * (np.outer(index, index) % 256)
    wave_x = 2.0 * np.pi / NX * np.arange(HALF)

    spectrum = np.exp(-1j * angle[:HALF])
    weight = np.where(np.arange(HALF) == 0, 1.0, 2.0)
    ahead = 1j * wave_x * np.exp(0.5j * wave_x)
    behind = 1j * wave_x * np.exp(-0.5j * wave_x)
    x_rows = np.zeros((8, HALF), np.float32)
    x_rows[0], x_rows[1], x_rows[2] = weight, (weight * ahead).real, (weight * ahead).imag
    forward_z = np.concatenate([np.cos(angle[:HALF]), -np.sin(angle[:HALF])], axis=0)
    forward_z[HALF] = np.cos(angle[HALF])
    inverse_z = 2.0 * forward_z.T
    inverse_z[:, 0] = forward_z[0]
    inverse_z[:, HALF] = forward_z[HALF]
    slab_order = (4 * np.arange(64)[None, :] + np.arange(4)[:, None]).reshape(-1)
    low = np.arange(HALF)
    high = low - 256
    coefficients = np.zeros((HALF, HALF), np.float32)
    coefficients[:, 0] = np.cos(2.0 * np.pi / NZ * low)
    coefficients[:, 1] = np.sin(2.0 * np.pi / NZ * low)

    def derivative(number, orientation):
        wave = 2.0 * np.pi / NZ * number
        return -orientation * wave * np.sin(0.5 * wave), wave * np.cos(0.5 * wave)

    coefficients[:, 16], coefficients[:, 17] = behind.real, behind.imag
    for first, orientation in ((2, 1.0), (9, -1.0)):
        middle_real, middle_imag = derivative(128, orientation)
        for at, number in ((first, low), (first + 3, high)):
            real, imag = derivative(number, orientation)
            coefficients[:, at] = real
            coefficients[:, at + 1] = np.where((low == 0), 0.0, imag)
            coefficients[:, at + 2] = np.where((low == 0), middle_real, real)
        coefficients[:, first + 6] = np.where((low == 0), middle_imag, 0.0)
    return {
        "x_waves": packed_table(np.concatenate([spectrum.real, spectrum.imag], axis=0)),
        "x_rows": x_rows,
        "y_ahead": packed_table(derivative_matrix(NY, 1.0)),
        "y_behind": packed_table(derivative_matrix(NY, -1.0)),
        "y_waves": packed_table(np.cos(angle) + np.sin(angle)),
        "z_from_slabs": packed_table(forward_z[:, slab_order]),
        "z_to_pairs": packed_table(inverse_z),
        "z_from_pairs": packed_table(forward_z),
        "z_to_slabs": packed_table(inverse_z[slab_order]),
        "columns": coefficients,
    }


TABLES = make_tables()


def pieces(x, axis):
    high = x.astype(bf16)
    low = (x - high.astype(f32)).astype(bf16)
    return jnp.concatenate([high, low, high], axis=axis)


def contract(a, b, a_dim, b_dim):
    return lax.dot_general(a, b, (((a_dim,), (b_dim,)), ((), ())), preferred_element_type=f32)


def wide(table_ref):
    table = table_ref[...]
    return jnp.concatenate([table[:, :256], table], axis=1)


def tall(table_ref):
    table = table_ref[...]
    return jnp.concatenate([table[:, :256], table[:, :256], table[:, 256:]], axis=0)


def left(table_ref, x):
    return contract(wide(table_ref), pieces(x, 0), 1, 0)


def right(x, table_ref):
    return contract(pieces(x, 1), tall(table_ref), 1, 0)


def to_components(table_ref, lines):
    return contract(wide(table_ref), pieces(lines, 1), 1, 1)


class Fetch:
    def __init__(self, sources, targets, semaphores):
        self.targets = targets
        self.copies = [
            pltpu.make_async_copy(source, target, semaphores.at[i])
            for i, (source, target) in enumerate(zip(sources, targets))
        ]
        for copy in self.copies:
            copy.start()

    def __getitem__(self, i):
        if self.copies[i] is not None:
            self.copies[i].wait()
            self.copies[i] = None
        return self.targets[i]


def times(real, imag, factor_real, factor_imag):
    return real * factor_real - imag * factor_imag, real * factor_imag + imag * factor_real


def kappa_rows(kx, part):
    kz = lax.broadcasted_iota(jnp.int32, (HALF, NY), 0)
    ky = lax.broadcasted_iota(jnp.int32, (HALF, NY), 1)
    number = kz - 256 * (part // 2)
    if part % 2:
        number = jnp.where(kz == 0, 128, number)
    wave_z = number.astype(f32) * (2.0 * math.pi / NZ)
    wave_y = jnp.where(ky < NY // 2, ky, ky - NY).astype(f32) * (2.0 * math.pi / NY)
    wave_x = jnp.full((HALF, NY), kx, jnp.int32).astype(f32) * (2.0 * math.pi / NX)
    square = (kappa_courant / 2.0) ** 2 * (wave_x * wave_x + wave_z * wave_z + wave_y * wave_y)
    total = jnp.full((HALF, NY), 1.0 / math.factorial(15), f32)
    for order in range(6, -1, -1):
        total = 1.0 / math.factorial(2 * order + 1) - square * total
    return total


def forward_z(table_ref, coefficient, fields):
    sides = [side for field in fields for side in (field[:256], field[256:])]
    sums = left(table_ref, jnp.concatenate(sides, axis=1))
    cosine, sine = coefficient(0), coefficient(1)
    spectra = []
    for i in range(0, len(sides), 2):
        even = sums[:, NY * i : NY * (i + 1)]
        odd = sums[:, NY * (i + 1) : NY * (i + 2)]
        real = cosine * odd[:HALF] + sine * odd[HALF:]
        imag = cosine * odd[HALF:] - sine * odd[:HALF]
        spectra.append(
            [even[:HALF] + real, even[HALF:] + imag, even[:HALF] - real, even[HALF:] - imag]
        )
    return spectra


def inverse_z(table_ref, coefficient, spectra):
    cosine, sine = coefficient(0), coefficient(1)
    sides = []
    for a, b, c, d in spectra:
        real, imag = a - c, b - d
        sides.append(jnp.concatenate([a + c, b + d], axis=0))
        sides.append(jnp.concatenate([cosine * real - sine * imag, cosine * imag + sine * real], axis=0))
    return left(table_ref, jnp.concatenate(sides, axis=1))


def derivative_z(coefficient, first, spectrum):
    a, b, c, d = spectrum
    mixed = coefficient(first + 6)
    return [
        coefficient(first) * a - coefficient(first + 1) * b,
        coefficient(first + 2) * b + coefficient(first + 1) * a - mixed * d,
        coefficient(first + 3) * c - coefficient(first + 4) * d,
        coefficient(first + 5) * d + coefficient(first + 4) * c + mixed * b,
    ]


def blocks_of(x):
    return [x[HALF * i : HALF * (i + 1)] for i in range(4)]


def first_half():
    return lax.broadcasted_iota(jnp.int32, (64, HALF), 1) < ROWS


def forward_lines_kernel(pressure, x_ref, out):
    components = to_components(x_ref, pressure[...].reshape(512, NX)) * X_SCALE
    for i in range(4):
        out[pl.ds(i, 256, stride=4), :] = components[:, HALF * i : HALF * (i + 1)]


def filter_out_kernel(where, data, y_ref, z_from_ref, z_to_ref, numbers, out, plane):
    early = first_half()
    for pair in range(4):
        for side in range(2):
            a = data[pl.ds(8 * side + pair, 64, stride=16), :]
            b = data[pl.ds(8 * side + 4 + pair, 64, stride=16), :]
            span = pl.ds(HALF * side, HALF)
            plane[pl.ds(64 * pair, 64), span] = jnp.where(early, a, pltpu.roll(b, ROWS, 1))
            plane[pl.ds(256 + 64 * pair, 64), span] = jnp.where(early, pltpu.roll(a, ROWS, 1), b)
    mixed = right(plane[...], y_ref)

    def coefficient(i):
        return numbers[:, i : i + 1]

    (spectrum,) = forward_z(z_from_ref, coefficient, [mixed])
    scale = SLOPE_LINK / (NZ * NY)
    waves = [x * (kappa_rows(where[0] % HALF, part) * scale) for part, x in enumerate(spectrum)]
    waves = blocks_of(right(jnp.concatenate(waves, axis=0), y_ref))
    planes = inverse_z(z_to_ref, coefficient, [waves, derivative_z(coefficient, 2, waves)])
    for field in range(2):
        for r in range(2):
            for side in range(2):
                start = NY * (2 * field + r) + HALF * side
                out[pl.ds(4 * r + 2 * field + side, 256, stride=8), :] = planes[
                    :, start : start + HALF
                ]


def middle_kernel(
    where, data, x_ref, rows, ya_ref, yb_ref, columns, velocity, buoyancy, *rest
):
    blocks, (slopes, out, held, fields, semaphores) = rest[:3], rest[3:]
    own = pl.ds(2 * where[0], 2)
    starts = [
        pl.ds(pl.multiple_of(((where[0] + PEERS_Y - back) % PEERS_Y) * ROWS, ROWS), ROWS)
        for back in range(PEERS_Y)
    ]
    fetch = Fetch(
        (velocity.at[:, own], buoyancy.at[own], *blocks),
        (
            fields.at[pl.ds(0, 3), :, starts[0]],
            fields.at[3, :, starts[0]],
            *[fields.at[:, :, start] for start in starts[1:]],
        ),
        semaphores,
    )
    weight, ahead_real, ahead_imag = rows[0:1, :], rows[1:2, :], rows[2:3, :]
    behind = columns[:, 16:17], columns[:, 17:18]
    returned = []
    for r in range(2):
        q, g = [
            jnp.concatenate(
                [data[pl.ds(4 * r + 2 * field + side, 256, stride=8), :] for side in range(2)], axis=1
            )
            for field in range(2)
        ]
        lines = []
        for x, slope in ((q, True), (q, False), (g, False)):
            x = x.T
            real, imag = x[:, :HALF], x[:, HALF:]
            if slope:
                real, imag = (
                    ahead_real * real - ahead_imag * imag,
                    ahead_real * imag + ahead_imag * real,
                )
            else:
                real, imag = weight * real, weight * imag
            lines.append(jnp.concatenate([real, imag], axis=1))
        lines = right(jnp.concatenate(lines, axis=0), x_ref) * X_SCALE
        along = (lines[:NY], left(ya_ref, lines[NY : 2 * NY]), lines[2 * NY :])
        if r == 0:
            for i in range(5):
                fetch[i]
        moved = []
        for d, slope in enumerate(along):
            held[r, d] = slope
            moved.append(fields[d, r] - fields[3, r] * (slope * (1.0 / SLOPE_LINK)))
        returned.append(pltpu.make_async_copy(held.at[r], slopes.at[:, r], semaphores.at[5 + r]))
        returned[r].start()
        lines = jnp.concatenate([moved[0], left(yb_ref, moved[1]), moved[2]], axis=0)
        components = to_components(x_ref, lines) * (X_SCALE * MIDDLE_LINK)
        real, imag = components[:HALF, :NY], components[HALF:, :NY]
        across = jnp.concatenate(
            times(real, imag, behind[0], behind[1]), axis=0
        ) + components[:, NY : 2 * NY]
        for field, components in enumerate((across, components[:, 2 * NY :])):
            for side in range(2):
                out[pl.ds(4 * r + 2 * field + side, 256, stride=8), :] = components[
                    :, HALF * side : HALF * (side + 1)
                ]
    for copy in returned:
        copy.wait()


def filter_back_kernel(where, data, y_ref, z_from_ref, z_to_ref, numbers, out):
    arrived = [
        jnp.concatenate(
            [
                jnp.concatenate(
                    [data[pl.ds(4 * r + 2 * field + side, 256, stride=8), :] for side in range(2)],
                    axis=1,
                )
                for r in range(2)
            ],
            axis=0,
        )
        for field in range(2)
    ]
    def coefficient(i):
        return numbers[:, i : i + 1]

    across, along = forward_z(z_from_ref, coefficient, arrived)
    waves = [x + z for x, z in zip(across, derivative_z(coefficient, 9, along))]
    waves = blocks_of(right(jnp.concatenate(waves, axis=0), y_ref))
    scale = DIVERGENCE_LINK / MIDDLE_LINK / (NZ * NY)
    waves = [x * (kappa_rows(where[0] % HALF, part) * scale) for part, x in enumerate(waves)]
    waves = blocks_of(right(jnp.concatenate(waves, axis=0), y_ref))
    plane = inverse_z(z_to_ref, coefficient, [waves])
    early = first_half()
    for pair in range(4):
        for side in range(2):
            rows = slice(64 * pair, 64 * (pair + 1))
            even = plane[rows, HALF * side : HALF * (side + 1)]
            odd = plane[rows, NY + HALF * side : NY + HALF * (side + 1)]
            out[pl.ds(8 * side + pair, 64, stride=16), :] = jnp.where(
                early, even, pltpu.roll(odd, ROWS, 1)
            )
            out[pl.ds(8 * side + 4 + pair, 64, stride=16), :] = jnp.where(
                early, pltpu.roll(even, ROWS, 1), odd
            )


def new_pressure_kernel(data, x_ref, pressure, bulk, own, passed, out, held, semaphores):
    row = lax.broadcasted_iota(jnp.int32, (256, HALF), 0)
    weight = jnp.where((row & (HALF - 1)) == 0, 1.0, 2.0) * (X_SCALE / DIVERGENCE_LINK)
    components = [(data[pl.ds(i, 256, stride=4), :] * weight).T for i in range(4)]
    lines = right(jnp.concatenate(components, axis=0), x_ref).reshape(SLAB, ROWS, NX)
    sent = []
    for i in range(4):
        planes = pl.ds(2 * i, 2)
        source = own[planes].astype(f32)
        held[planes] = pressure[planes] - bulk[planes] * lines[2 * i : 2 * i + 2] + source
        held[planes, :TILE] += passed[planes].astype(f32)
        sent.append(pltpu.make_async_copy(held.at[planes], out.at[planes], semaphores.at[i]))
        sent[i].start()
    for copy in sent:
        copy.wait()


def source_kernel(where, lives, corner, tiles, here, after, beyond, lifted):
    lifted[:SLAB] = jnp.zeros((SLAB, 256, NX), bf16)
    lifted[2 * SLAB :] = jnp.zeros((SLAB, 256, NX), bf16)

    def place(slot, carry):
        rows = pl.ds(pl.multiple_of(slot * TILE, TILE), TILE)
        lane = lax.broadcasted_iota(jnp.int32, (TILE, NX), 1)
        line = lax.broadcasted_iota(jnp.int32, (TILE, NX), 0)
        hot = ((lane - line - corner[slot, 2]) & (NX - 1)) == 0
        hot = jnp.where(hot, 1.0, 0.0).astype(bf16)
        block = tiles[slot].reshape(2 * SLAB * TILE, TILE)
        across = jnp.dot(block, hot, preferred_element_type=f32).astype(bf16)
        planes = pl.ds(corner[slot, 0] & (SLAB - 1), 2 * SLAB)
        lifted[planes, rows, :] = across.reshape(2 * SLAB, TILE, NX)
        return carry

    lax.fori_loop(0, SLOTS_HERE, place, 0)
    line = lax.broadcasted_iota(jnp.int32, (ROWS + TILE, 256), 0)
    lane = lax.broadcasted_iota(jnp.int32, (ROWS + TILE, 256), 1)
    start = jnp.full((ROWS + TILE, 256), -2 * TILE, jnp.int32)
    for slot in range(SLOTS_HERE):
        row = corner[slot, 1] - where[1] * ROWS - slot * TILE
        row = jnp.where(slot < lives[where[0] * PEERS_Y + where[1]], row, -2 * NX)
        start = jnp.where(lane // TILE == slot, lane + row, start)
    hot = jnp.where(line == start, 1.0, 0.0).astype(bf16)
    for group, out in enumerate((here, after, beyond)):
        for z in range(SLAB):
            window = jnp.dot(hot, lifted[SLAB * group + z], preferred_element_type=f32)
            out[z] = window.astype(bf16)


def source_sum_kernel(here, after, beyond, own, passed):
    total = here[...].astype(f32) + after[...].astype(f32) + beyond[...].astype(f32)
    own[...] = total[:, :ROWS].astype(bf16)
    passed[...] = total[:, ROWS:].astype(bf16)


VMEM = pl.BlockSpec(memory_space=pltpu.VMEM)
SMEM = pl.BlockSpec(memory_space=pltpu.SMEM)
FAR = pl.BlockSpec(memory_space=pltpu.HBM)


def call(kernel, name, specs, arrays, shapes, outs, scratch=(), semaphores=0, limit=20):
    scratch = [pltpu.VMEM(shape, kind) for shape, kind in scratch]
    if semaphores:
        scratch.append(pltpu.SemaphoreType.DMA((semaphores,)))
    return pl.pallas_call(
        kernel,
        out_shape=[jax.ShapeDtypeStruct(shape, kind) for shape, kind in shapes],
        in_specs=specs,
        out_specs=outs,
        scratch_shapes=scratch,
        compiler_params=pltpu.CompilerParams(vmem_limit_bytes=limit << 20),
        cost_estimate=pl.CostEstimate(flops=int(4e8), bytes_accessed=1 << 20, transcendentals=0),
        name=name,
    )(*arrays)


def from_behind(x, axis, by):
    peers = lax.axis_size(axis)
    return lax.ppermute(x, axis, [(i, (i + by) % peers) for i in range(peers)])


def to_rows(slopes, row_block):
    blocks = [
        lax.dynamic_slice_in_dim(slopes, ROWS * ((row_block + ahead) % PEERS_Y), ROWS, 2)
        for ahead in range(PEERS_Y)
    ]
    arrived = [blocks[0]] + [from_behind(blocks[ahead], "gy", ahead) for ahead in range(1, PEERS_Y)]
    ordered = [
        lax.select_n((row_block - device) % PEERS_Y, *arrived) for device in range(PEERS_Y)
    ]
    return jnp.concatenate(ordered, 1).astype(f32)


def exchange(columns, rows):
    blocks = columns.astype(f16).reshape(256, rows, HALF)
    return lax.all_to_all(blocks, ("gz", "gy"), 0, 0, tiled=True)


def arrived(moved):
    return moved.reshape(-1, HALF).astype(f32)


def local(pressure, velocity, bulk, buoyancy, tiles, tile_corner, live_count):
    slab_index = lax.axis_index("gz")
    row_block = lax.axis_index("gy")
    here = row_block.reshape(1).astype(jnp.int32)
    device = (slab_index * PEERS_Y + row_block).astype(jnp.int32)
    place = jnp.stack([slab_index, row_block]).astype(jnp.int32)
    table = {key: jnp.asarray(value) for key, value in TABLES.items()}

    (components,) = call(
        forward_lines_kernel,
        "forward_lines",
        [VMEM, VMEM],
        [pressure, table["x_waves"]],
        [((1024, HALF), f32)],
        [VMEM],
    )
    velocity_later, buoyancy_later, tiles, device_later, components = lax.optimization_barrier(
        (velocity, buoyancy, tiles, device, components)
    )
    fields = jnp.concatenate([velocity_later, buoyancy_later[None]])
    sent = [
        lax.dynamic_slice_in_dim(fields, 2 * ((row_block + ahead) % PEERS_Y), 2, 1).astype(f16)
        for ahead in range(1, PEERS_Y)
    ]
    first, third = from_behind(sent[0], "gy", 1), from_behind(sent[2], "gy", 3)
    moved, second = lax.optimization_barrier((exchange(components, 4), sent[1]))
    (filtered,) = call(
        filter_out_kernel,
        "filter_out",
        [SMEM] + [VMEM] * 5,
        [
            device.reshape(1),
            arrived(moved),
            table["y_waves"],
            table["z_from_slabs"],
            table["z_to_pairs"],
            table["columns"],
        ],
        [((2048, HALF), f32)],
        [VMEM],
        [((NZ, NY), f32)],
    )
    filtered, tiles, device_later, first, second, third = lax.optimization_barrier(
        (filtered, tiles, device_later, first, second, third)
    )
    second = from_behind(second, "gy", 2)
    corner = lax.dynamic_slice_in_dim(tile_corner, device_later * SLOTS_HERE, SLOTS_HERE, 0)
    window = ((SLAB, ROWS + TILE, NX), bf16)
    source, after, beyond = call(
        source_kernel,
        "source",
        [SMEM, SMEM, SMEM, VMEM],
        [place, live_count, corner, tiles],
        [window] * 3,
        [VMEM] * 3,
        [((3 * SLAB, 256, NX), bf16)],
    )
    after, beyond = from_behind(after, "gz", 1), from_behind(beyond, "gz", 2)
    moved, source = lax.optimization_barrier((exchange(filtered, 8), source))
    slopes, middle = call(
        middle_kernel,
        "middle",
        [SMEM] + [VMEM] * 6 + [FAR] * 5,
        [
            here,
            arrived(moved),
            table["x_waves"],
            table["x_rows"],
            table["y_ahead"],
            table["y_behind"],
            table["columns"],
            velocity,
            buoyancy,
            *[block.astype(f32) for block in (first, second, third)],
        ],
        [((3, 2, NY, NX), f32), ((2048, HALF), f32)],
        [FAR, VMEM],
        [((2, 3, NY, NX), f32), ((4, 2, NY, NX), f32)],
        7,
    )
    middle, slopes = lax.optimization_barrier((middle, slopes.astype(f16)))
    slopes = to_rows(slopes, row_block)
    new_velocity = velocity - buoyancy[None] * (slopes * (1.0 / SLOPE_LINK))
    (filtered_back,) = call(
        filter_back_kernel,
        "filter_back",
        [SMEM] + [VMEM] * 5,
        [
            device.reshape(1),
            arrived(exchange(middle, 8)),
            table["y_waves"],
            table["z_from_pairs"],
            table["z_to_slabs"],
            table["columns"],
        ],
        [((1024, HALF), f32)],
        [VMEM],
    )
    filtered_back, source, after, beyond = lax.optimization_barrier(
        (filtered_back, source, after, beyond)
    )
    own, passed = call(
        source_sum_kernel,
        "source_sum",
        [VMEM] * 3,
        [source, after, beyond],
        [((SLAB, ROWS, NX), bf16), ((SLAB, TILE, NX), bf16)],
        [VMEM] * 2,
    )
    passed = from_behind(passed, "gy", 1)
    moved, new_velocity = lax.optimization_barrier((exchange(filtered_back, 4), new_velocity))
    (new_pressure,) = call(
        new_pressure_kernel,
        "new_pressure",
        [VMEM] * 6,
        [arrived(moved), table["x_waves"], pressure, bulk, own, passed],
        [((SLAB, ROWS, NX), f32)],
        [FAR],
        [((SLAB, ROWS, NX), f32)],
        4,
    )
    return (new_pressure, new_velocity)


def solution(mesh):
    in_specs = (
        P("gz", "gy", None),
        P(None, "gz", "gy", None),
        P("gz", "gy", None),
        P("gz", "gy", None),
        P(("gz", "gy"), None, None, None),
        P(),
        P(),
    )
    out_specs = (P("gz", "gy", None), P(None, "gz", "gy", None))
    return jax.shard_map(local, mesh=mesh, in_specs=in_specs, out_specs=out_specs, check_vma=False)
```

```python
import math

import jax
import jax.numpy as jnp
import ml_dtypes
import numpy as np
from jax import lax
from jax.experimental import pallas as pl
from jax.experimental.pallas import tpu as pltpu
from jax.sharding import PartitionSpec as P

NX = 256
NY = 256
NZ = 512
HALF = 128
ROWS = 64
SLAB = 8
SLOTS_HERE = 8
TILE = 32
PEERS_Y = 4
PEERS_Z = 64
kappa_courant = 0.3
f32 = jnp.float32
bf16 = jnp.bfloat16
f16 = jnp.float16

X_SCALE = 1.0 / 16.0
FIELD_LINK = 4096.0
COMPONENT_LINK = 256.0
SLOPE_LINK = 128.0
RETURN_LINK = 1024.0
MIDDLE_LINK = 16.0
DIVERGENCE_LINK = 8.0


def split_table(table):
    high = table.astype(ml_dtypes.bfloat16)
    low = (table - high.astype(np.float64)).astype(ml_dtypes.bfloat16)
    return high, low


def packed_table(table):
    return np.concatenate(split_table(table), axis=1)


def signed_waves(length):
    index = np.arange(length)
    return 2.0 * np.pi / length * np.where(index < length // 2, index, index - length)


def derivative_matrix(length, orientation):
    wave = signed_waves(length)
    kernel = np.fft.ifft(1j * wave * np.exp(orientation * 0.5j * wave)).real
    index = np.arange(length)
    return kernel[(index[:, None] - index[None, :]) % length]


def make_tables():
    index = np.arange(256)
    angle = 2.0 * np.pi / 256 * (np.outer(index, index) % 256)
    wave_x = 2.0 * np.pi / NX * np.arange(HALF)

    spectrum = np.exp(-1j * angle[:HALF])
    weight = np.where(np.arange(HALF) == 0, 1.0, 2.0)
    ahead = 1j * wave_x * np.exp(0.5j * wave_x)
    behind = 1j * wave_x * np.exp(-0.5j * wave_x)
    x_rows = np.zeros((8, HALF), np.float32)
    x_rows[0], x_rows[1], x_rows[2] = weight, (weight * ahead).real, (weight * ahead).imag
    forward_z = np.concatenate([np.cos(angle[:HALF]), -np.sin(angle[:HALF])], axis=0)
    forward_z[HALF] = np.cos(angle[HALF])
    inverse_z = 2.0 * forward_z.T
    inverse_z[:, 0] = forward_z[0]
    inverse_z[:, HALF] = forward_z[HALF]
    slab_order = (4 * np.arange(64)[None, :] + np.arange(4)[:, None]).reshape(-1)
    low = np.arange(HALF)
    high = low - 256
    coefficients = np.zeros((HALF, HALF), np.float32)
    coefficients[:, 0] = np.cos(2.0 * np.pi / NZ * low)
    coefficients[:, 1] = np.sin(2.0 * np.pi / NZ * low)

    def derivative(number, orientation):
        wave = 2.0 * np.pi / NZ * number
        return -orientation * wave * np.sin(0.5 * wave), wave * np.cos(0.5 * wave)

    coefficients[:, 16], coefficients[:, 17] = behind.real, behind.imag
    for first, orientation in ((2, 1.0), (9, -1.0)):
        middle_real, middle_imag = derivative(128, orientation)
        for at, number in ((first, low), (first + 3, high)):
            real, imag = derivative(number, orientation)
            coefficients[:, at] = real
            coefficients[:, at + 1] = np.where((low == 0), 0.0, imag)
            coefficients[:, at + 2] = np.where((low == 0), middle_real, real)
        coefficients[:, first + 6] = np.where((low == 0), middle_imag, 0.0)
    x_waves = packed_table(np.concatenate([spectrum.real, spectrum.imag], axis=0))
    y_waves = packed_table(np.cos(angle) + np.sin(angle))
    return {
        "x_waves": x_waves,
        "middle": np.concatenate(
            [
                x_waves,
                packed_table(derivative_matrix(NY, 1.0)),
                packed_table(derivative_matrix(NY, -1.0)),
            ],
            axis=1,
        ),
        "filter_out": np.concatenate(
            [y_waves, packed_table(forward_z[:, slab_order]), packed_table(inverse_z)], axis=1
        ),
        "filter_back": np.concatenate(
            [y_waves, packed_table(forward_z), packed_table(inverse_z[slab_order])], axis=1
        ),
        "numbers": np.concatenate([coefficients, x_rows], axis=0),
    }


TABLES = make_tables()


def pieces(x, axis):
    high = x.astype(bf16)
    low = (x - high.astype(f32)).astype(bf16)
    return jnp.concatenate([high, low, high], axis=axis)


def contract(a, b, a_dim, b_dim):
    return lax.dot_general(a, b, (((a_dim,), (b_dim,)), ((), ())), preferred_element_type=f32)


def wide(table):
    return jnp.concatenate([table[:, :256], table[:, :512]], axis=1)


def tall(table):
    return jnp.concatenate([table[:, :256], table[:, :256], table[:, 256:512]], axis=0)


def left(table_ref, x):
    return contract(wide(table_ref), pieces(x, 0), 1, 0)


def right(x, table_ref):
    return contract(pieces(x, 1), tall(table_ref), 1, 0)


def to_components(table_ref, lines):
    return contract(wide(table_ref), pieces(lines, 1), 1, 1)


class Fetch:
    def __init__(self, sources, targets, semaphores):
        self.targets = targets
        self.copies = [
            pltpu.make_async_copy(source, target, semaphores.at[i])
            for i, (source, target) in enumerate(zip(sources, targets))
        ]
        for copy in self.copies:
            copy.start()

    def __getitem__(self, i):
        if self.copies[i] is not None:
            self.copies[i].wait()
            self.copies[i] = None
        return self.targets[i]


def times(real, imag, factor_real, factor_imag):
    return real * factor_real - imag * factor_imag, real * factor_imag + imag * factor_real


def kappa_rows(kx, part):
    kz = lax.broadcasted_iota(jnp.int32, (HALF, NY), 0)
    ky = lax.broadcasted_iota(jnp.int32, (HALF, NY), 1)
    number = kz - 256 * (part // 2)
    if part % 2:
        number = jnp.where(kz == 0, 128, number)
    wave_z = number.astype(f32) * (2.0 * math.pi / NZ)
    wave_y = jnp.where(ky < NY // 2, ky, ky - NY).astype(f32) * (2.0 * math.pi / NY)
    wave_x = jnp.full((HALF, NY), kx, jnp.int32).astype(f32) * (2.0 * math.pi / NX)
    square = (kappa_courant / 2.0) ** 2 * (wave_x * wave_x + wave_z * wave_z + wave_y * wave_y)
    total = jnp.full((HALF, NY), 1.0 / math.factorial(15), f32)
    for order in range(6, -1, -1):
        total = 1.0 / math.factorial(2 * order + 1) - square * total
    return total


def forward_z(table_ref, coefficient, fields):
    sides = [side for field in fields for side in (field[:256], field[256:])]
    sums = left(table_ref, jnp.concatenate(sides, axis=1))
    cosine, sine = coefficient(0), coefficient(1)
    spectra = []
    for i in range(0, len(sides), 2):
        even = sums[:, NY * i : NY * (i + 1)]
        odd = sums[:, NY * (i + 1) : NY * (i + 2)]
        real = cosine * odd[:HALF] + sine * odd[HALF:]
        imag = cosine * odd[HALF:] - sine * odd[:HALF]
        spectra.append(
            [even[:HALF] + real, even[HALF:] + imag, even[:HALF] - real, even[HALF:] - imag]
        )
    return spectra


def inverse_z(table_ref, coefficient, spectra):
    cosine, sine = coefficient(0), coefficient(1)
    sides = []
    for a, b, c, d in spectra:
        real, imag = a - c, b - d
        sides.append(jnp.concatenate([a + c, b + d], axis=0))
        sides.append(jnp.concatenate([cosine * real - sine * imag, cosine * imag + sine * real], axis=0))
    return left(table_ref, jnp.concatenate(sides, axis=1))


def derivative_z(coefficient, first, spectrum):
    a, b, c, d = spectrum
    mixed = coefficient(first + 6)
    return [
        coefficient(first) * a - coefficient(first + 1) * b,
        coefficient(first + 2) * b + coefficient(first + 1) * a - mixed * d,
        coefficient(first + 3) * c - coefficient(first + 4) * d,
        coefficient(first + 5) * d + coefficient(first + 4) * c + mixed * b,
    ]


def blocks_of(x):
    return [x[HALF * i : HALF * (i + 1)] for i in range(4)]


def first_half():
    return lax.broadcasted_iota(jnp.int32, (64, HALF), 1) < ROWS


def forward_lines_kernel(pressure, x_ref, out):
    components = to_components(x_ref, pressure[...].reshape(512, NX)) * (X_SCALE * COMPONENT_LINK)
    for i in range(4):
        out[pl.ds(i, 256, stride=4), :] = components[:, HALF * i : HALF * (i + 1)]


def filter_out_kernel(where, data, tables, numbers, out, plane):
    y_ref, z_from_ref, z_to_ref = (tables[:, 512 * i : 512 * (i + 1)] for i in range(3))
    early = first_half()
    for pair in range(4):
        for side in range(2):
            a = data[pl.ds(8 * side + pair, 64, stride=16), :]
            b = data[pl.ds(8 * side + 4 + pair, 64, stride=16), :]
            span = pl.ds(HALF * side, HALF)
            plane[pl.ds(64 * pair, 64), span] = jnp.where(early, a, pltpu.roll(b, ROWS, 1))
            plane[pl.ds(256 + 64 * pair, 64), span] = jnp.where(early, pltpu.roll(a, ROWS, 1), b)
    mixed = right(plane[...], y_ref)

    def coefficient(i):
        return numbers[:HALF, i : i + 1]

    (spectrum,) = forward_z(z_from_ref, coefficient, [mixed])
    scale = SLOPE_LINK / COMPONENT_LINK / (NZ * NY)
    waves = [x * (kappa_rows(where[0] % HALF, part) * scale) for part, x in enumerate(spectrum)]
    waves = blocks_of(right(jnp.concatenate(waves, axis=0), y_ref))
    planes = inverse_z(z_to_ref, coefficient, [waves, derivative_z(coefficient, 2, waves)])
    for field in range(2):
        for r in range(2):
            for side in range(2):
                start = NY * (2 * field + r) + HALF * side
                out[pl.ds(4 * r + 2 * field + side, 256, stride=8), :] = planes[
                    :, start : start + HALF
                ]


def middle_kernel(
    where, data, tables, numbers, velocity, buoyancy, *rest
):
    blocks, (slopes, out, held, fields, semaphores) = rest[:3], rest[3:]
    own = pl.ds(2 * where[0], 2)
    starts = [
        pl.ds(pl.multiple_of(((where[0] + PEERS_Y - back) % PEERS_Y) * ROWS, ROWS), ROWS)
        for back in range(PEERS_Y)
    ]
    fetch = Fetch(
        (velocity.at[:, own], buoyancy.at[own], *blocks),
        (
            fields.at[pl.ds(0, 3), :, starts[0]],
            fields.at[3, :, starts[0]],
            *[fields.at[:, :, start] for start in starts[1:]],
        ),
        semaphores,
    )
    x_ref, ya_ref, yb_ref = (tables[:, 512 * i : 512 * (i + 1)] for i in range(3))
    weight, ahead_real, ahead_imag = (numbers[HALF + i : HALF + i + 1, :] for i in range(3))
    behind = numbers[:HALF, 16:17], numbers[:HALF, 17:18]
    returned = []
    for r in range(2):
        q, g = [
            jnp.concatenate(
                [data[pl.ds(4 * r + 2 * field + side, 256, stride=8), :] for side in range(2)], axis=1
            )
            for field in range(2)
        ]
        lines = []
        for x, slope in ((q, True), (q, False), (g, False)):
            x = x.T
            real, imag = x[:, :HALF], x[:, HALF:]
            if slope:
                real, imag = (
                    ahead_real * real - ahead_imag * imag,
                    ahead_real * imag + ahead_imag * real,
                )
            else:
                real, imag = weight * real, weight * imag
            lines.append(jnp.concatenate([real, imag], axis=1))
        lines = right(jnp.concatenate(lines, axis=0), x_ref) * (X_SCALE / SLOPE_LINK)
        along = (lines[:NY], left(ya_ref, lines[NY : 2 * NY]), lines[2 * NY :])
        if r == 0:
            for i in range(5):
                fetch[i]
        moved = []
        for d, slope in enumerate(along):
            held[r, d] = slope * RETURN_LINK
            moved.append(fields[d, r] - fields[3, r] * slope)
        returned.append(pltpu.make_async_copy(held.at[r], slopes.at[:, r], semaphores.at[5 + r]))
        returned[r].start()
        lines = jnp.concatenate([moved[0], left(yb_ref, moved[1]), moved[2]], axis=0)
        components = to_components(x_ref, lines) * (X_SCALE * MIDDLE_LINK)
        real, imag = components[:HALF, :NY], components[HALF:, :NY]
        across = jnp.concatenate(
            times(real, imag, behind[0], behind[1]), axis=0
        ) + components[:, NY : 2 * NY]
        for field, components in enumerate((across, components[:, 2 * NY :])):
            for side in range(2):
                out[pl.ds(4 * r + 2 * field + side, 256, stride=8), :] = components[
                    :, HALF * side : HALF * (side + 1)
                ]
    for copy in returned:
        copy.wait()


def filter_back_kernel(where, data, tables, numbers, out):
    y_ref, z_from_ref, z_to_ref = (tables[:, 512 * i : 512 * (i + 1)] for i in range(3))
    arrived = [
        jnp.concatenate(
            [
                jnp.concatenate(
                    [data[pl.ds(4 * r + 2 * field + side, 256, stride=8), :] for side in range(2)],
                    axis=1,
                )
                for r in range(2)
            ],
            axis=0,
        )
        for field in range(2)
    ]
    def coefficient(i):
        return numbers[:HALF, i : i + 1]

    across, along = forward_z(z_from_ref, coefficient, arrived)
    waves = [x + z for x, z in zip(across, derivative_z(coefficient, 9, along))]
    waves = blocks_of(right(jnp.concatenate(waves, axis=0), y_ref))
    scale = DIVERGENCE_LINK / MIDDLE_LINK / (NZ * NY)
    waves = [x * (kappa_rows(where[0] % HALF, part) * scale) for part, x in enumerate(waves)]
    waves = blocks_of(right(jnp.concatenate(waves, axis=0), y_ref))
    plane = inverse_z(z_to_ref, coefficient, [waves])
    early = first_half()
    for pair in range(4):
        for side in range(2):
            rows = slice(64 * pair, 64 * (pair + 1))
            even = plane[rows, HALF * side : HALF * (side + 1)]
            odd = plane[rows, NY + HALF * side : NY + HALF * (side + 1)]
            out[pl.ds(8 * side + pair, 64, stride=16), :] = jnp.where(
                early, even, pltpu.roll(odd, ROWS, 1)
            )
            out[pl.ds(8 * side + 4 + pair, 64, stride=16), :] = jnp.where(
                early, pltpu.roll(even, ROWS, 1), odd
            )


def new_pressure_kernel(data, x_ref, bulk, own, passed, out, held, semaphores):
    row = lax.broadcasted_iota(jnp.int32, (256, HALF), 0)
    weight = jnp.where((row & (HALF - 1)) == 0, 1.0, 2.0) * (X_SCALE / DIVERGENCE_LINK)
    components = [(data[pl.ds(i, 256, stride=4), :] * weight).T for i in range(4)]
    lines = right(jnp.concatenate(components, axis=0), x_ref).reshape(SLAB, ROWS, NX)
    sent = []
    for i in range(4):
        planes = pl.ds(2 * i, 2)
        held[planes] = own[planes] - bulk[planes] * lines[2 * i : 2 * i + 2]
        held[planes, :TILE] += passed[planes].astype(f32)
        sent.append(pltpu.make_async_copy(held.at[planes], out.at[planes], semaphores.at[i]))
        sent[i].start()
    for copy in sent:
        copy.wait()


def source_kernel(where, lives, c0, c1, c2, t0, t1, t2, pressure, own, passed, l0, l1, l2):
    blank = jnp.zeros((SLAB, 256, NX), bf16)
    l0[:SLAB] = blank
    l2[SLAB:] = blank
    corners = (c0, c1, c2)

    def place(slot, carry):
        rows = pl.ds(pl.multiple_of(slot * TILE, TILE), TILE)
        lane = lax.broadcasted_iota(jnp.int32, (HALF, NX), 1)
        line = lax.broadcasted_iota(jnp.int32, (HALF, NX), 0) & (TILE - 1)
        quarter = lax.broadcasted_iota(jnp.int32, (SLAB, 8, HALF), 2) // TILE
        for reach, (tiles, placed) in enumerate(((t0, l0), (t1, l1), (t2, l2))):
            offset = corners[reach][slot, 0] & (SLAB - 1)
            hot = ((lane - line - corners[reach][slot, 2]) & (NX - 1)) == 0
            hot = jnp.where(hot, 1.0, 0.0).astype(bf16)
            first = SLAB - offset if reach == 1 else 0
            to = 0 if reach == 1 else offset
            block = tiles[slot, pl.ds(first, SLAB)].astype(f32)
            block = jnp.stack([jnp.where(quarter == i, block, 0.0) for i in range(4)], axis=1)
            block = block.reshape(SLAB * TILE, HALF).astype(bf16)
            across = jnp.dot(block, hot, preferred_element_type=f32).astype(bf16)
            placed[pl.ds(to, SLAB), rows, :] = across.reshape(SLAB, TILE, NX)
        return carry

    lax.fori_loop(0, SLOTS_HERE, place, 0)
    line = lax.broadcasted_iota(jnp.int32, (ROWS + TILE, 256), 0)
    lane = lax.broadcasted_iota(jnp.int32, (ROWS + TILE, 256), 1)
    hots = []
    for reach in range(3):
        sender = ((where[0] + PEERS_Z - reach) % PEERS_Z) * PEERS_Y + where[1]
        start = jnp.full((ROWS + TILE, 256), -2 * TILE, jnp.int32)
        for slot in range(SLOTS_HERE):
            row = corners[reach][slot, 1] - where[1] * ROWS
            row = jnp.where(slot < lives[sender], row, -2 * NX)
            within = 4 * (lane & 7) + ((lane // 8) & 3)
            start = jnp.where(lane // TILE == slot, within + row, start)
        hots.append(jnp.where(line == start, 1.0, 0.0).astype(bf16))
    for z in range(SLAB):
        window = jnp.dot(hots[0], l0[z], preferred_element_type=f32)
        window += jnp.dot(hots[1], l1[z], preferred_element_type=f32)
        window += jnp.dot(hots[2], l2[SLAB + z], preferred_element_type=f32)
        own[z] = pressure[z] + window[:ROWS]
        passed[z] = window[ROWS:].astype(bf16)


VMEM = pl.BlockSpec(memory_space=pltpu.VMEM)
SMEM = pl.BlockSpec(memory_space=pltpu.SMEM)
FAR = pl.BlockSpec(memory_space=pltpu.HBM)


def call(kernel, name, specs, arrays, shapes, outs, scratch=(), semaphores=0, limit=20):
    scratch = [pltpu.VMEM(shape, kind) for shape, kind in scratch]
    if semaphores:
        scratch.append(pltpu.SemaphoreType.DMA((semaphores,)))
    return pl.pallas_call(
        kernel,
        out_shape=[jax.ShapeDtypeStruct(shape, kind) for shape, kind in shapes],
        in_specs=specs,
        out_specs=outs,
        scratch_shapes=scratch,
        compiler_params=pltpu.CompilerParams(vmem_limit_bytes=limit << 20),
        cost_estimate=pl.CostEstimate(flops=int(4e8), bytes_accessed=1 << 20, transcendentals=0),
        name=name,
    )(*arrays)


def from_behind(x, axis, by):
    peers = lax.axis_size(axis)
    return lax.ppermute(x, axis, [(i, (i + by) % peers) for i in range(peers)])


def to_rows(slopes, row_block):
    blocks = [
        lax.dynamic_slice_in_dim(slopes, ROWS * ((row_block + ahead) % PEERS_Y), ROWS, 2)
        for ahead in range(PEERS_Y)
    ]
    arrived = [blocks[0]] + [from_behind(blocks[ahead], "gy", ahead) for ahead in range(1, PEERS_Y)]
    ordered = [
        lax.select_n((row_block - device) % PEERS_Y, *arrived) for device in range(PEERS_Y)
    ]
    return jnp.concatenate(ordered, 1).astype(f32)


def exchange(columns, rows):
    blocks = columns.astype(f16).reshape(256, rows, HALF)
    return lax.all_to_all(blocks, ("gz", "gy"), 0, 0, tiled=True)


def arrived(moved):
    return moved.reshape(-1, HALF).astype(f32)


def local(pressure, velocity, bulk, buoyancy, tiles, tile_corner, live_count):
    slab_index = lax.axis_index("gz")
    row_block = lax.axis_index("gy")
    here = row_block.reshape(1).astype(jnp.int32)
    device = (slab_index * PEERS_Y + row_block).astype(jnp.int32)
    place = jnp.stack([slab_index, row_block]).astype(jnp.int32)
    table = {key: jnp.asarray(value) for key, value in TABLES.items()}

    (components,) = call(
        forward_lines_kernel,
        "forward_lines",
        [VMEM, VMEM],
        [pressure, table["x_waves"]],
        [((1024, HALF), f32)],
        [VMEM],
    )
    velocity_later, buoyancy_later, tiles, slab_later, components = lax.optimization_barrier(
        (velocity, buoyancy, tiles, slab_index, components)
    )
    fields = jnp.concatenate([velocity_later, buoyancy_later[None]])
    sent = [
        (
            lax.dynamic_slice_in_dim(fields, 2 * ((row_block + ahead) % PEERS_Y), 2, 1) * FIELD_LINK
        ).astype(f16)
        for ahead in range(1, PEERS_Y)
    ]
    first, third = from_behind(sent[0], "gy", 1), from_behind(sent[2], "gy", 3)
    packed = tiles.reshape(SLOTS_HERE, 2 * SLAB, 8, HALF)
    moved, second, packed, packed_end = lax.optimization_barrier(
        (exchange(components, 4), sent[1], packed, packed[:, SLAB:])
    )
    (filtered,) = call(
        filter_out_kernel,
        "filter_out",
        [SMEM] + [VMEM] * 3,
        [
            device.reshape(1),
            arrived(moved),
            table["filter_out"],
            table["numbers"],
        ],
        [((2048, HALF), f32)],
        [VMEM],
        [((NZ, NY), f32)],
    )
    filtered, first, second, third, packed, packed_end = lax.optimization_barrier(
        (filtered, first, second, third, packed, packed_end)
    )
    second = from_behind(second, "gy", 2)
    tiles_before, tiles_second = from_behind(packed, "gz", 1), from_behind(packed_end, "gz", 2)
    moved = exchange(filtered, 8)
    slopes, middle = call(
        middle_kernel,
        "middle",
        [SMEM] + [VMEM] * 3 + [FAR] * 5,
        [
            here,
            arrived(moved),
            table["middle"],
            table["numbers"],
            velocity,
            buoyancy,
            *[block.astype(f32) * (1.0 / FIELD_LINK) for block in (first, second, third)],
        ],
        [((3, 2, NY, NX), f32), ((2048, HALF), f32)],
        [FAR, VMEM],
        [((2, 3, NY, NX), f32), ((4, 2, NY, NX), f32)],
        7,
    )
    middle, slopes, tiles_before, tiles_second = lax.optimization_barrier(
        (middle, slopes.astype(f16), tiles_before, tiles_second)
    )
    slopes = to_rows(slopes, row_block)
    new_velocity = velocity - buoyancy[None] * (slopes * (1.0 / RETURN_LINK))
    corners = [
        lax.dynamic_slice_in_dim(
            tile_corner,
            ((slab_later - reach) % PEERS_Z * PEERS_Y + row_block) * SLOTS_HERE,
            SLOTS_HERE,
            0,
        )
        for reach in range(3)
    ]
    own, passed = call(
        source_kernel,
        "source",
        [SMEM] * 5 + [VMEM] * 4,
        [
            place,
            live_count,
            *corners,
            packed,
            tiles_before,
            tiles_second,
            pressure,
        ],
        [((SLAB, ROWS, NX), f32), ((SLAB, TILE, NX), bf16)],
        [VMEM] * 2,
        [((2 * SLAB, 256, NX), bf16), ((SLAB, 256, NX), bf16), ((2 * SLAB, 256, NX), bf16)],
    )
    (filtered_back,) = call(
        filter_back_kernel,
        "filter_back",
        [SMEM] + [VMEM] * 3,
        [
            device.reshape(1),
            arrived(exchange(middle, 8)),
            table["filter_back"],
            table["numbers"],
        ],
        [((1024, HALF), f32)],
        [VMEM],
    )
    filtered_back, own, passed = lax.optimization_barrier((filtered_back, own, passed))
    passed = from_behind(passed, "gy", 1)
    moved, new_velocity = lax.optimization_barrier((exchange(filtered_back, 4), new_velocity))
    (new_pressure,) = call(
        new_pressure_kernel,
        "new_pressure",
        [VMEM] * 5,
        [arrived(moved), table["x_waves"], bulk, own, passed],
        [((SLAB, ROWS, NX), f32)],
        [FAR],
        [((SLAB, ROWS, NX), f32)],
        4,
    )
    return (new_pressure, new_velocity)


def solution(mesh):
    in_specs = (
        P("gz", "gy", None),
        P(None, "gz", "gy", None),
        P("gz", "gy", None),
        P("gz", "gy", None),
        P(("gz", "gy"), None, None, None),
        P(),
        P(),
    )
    out_specs = (P("gz", "gy", None), P(None, "gz", "gy", None))
    return jax.shard_map(local, mesh=mesh, in_specs=in_specs, out_specs=out_specs, check_vma=False)
```

```python
import math

import jax
import jax.numpy as jnp
import ml_dtypes
import numpy as np
from jax import lax
from jax.experimental import pallas as pl
from jax.experimental.pallas import tpu as pltpu
from jax.sharding import PartitionSpec as P

NX = 256
NY = 256
NZ = 512
HALF = 128
ROWS = 64
SLAB = 8
SLOTS_HERE = 8
TILE = 32
PEERS_Y = 4
PEERS_Z = 64
kappa_courant = 0.3
f32 = jnp.float32
bf16 = jnp.bfloat16
f16 = jnp.float16

X_SCALE = 1.0 / 16.0
FIELD_LINK = 4096.0
COMPONENT_LINK = 256.0
SLOPE_LINK = 128.0
RETURN_LINK = 1024.0
MIDDLE_LINK = 16.0
DIVERGENCE_LINK = 8.0


def split_table(table):
    high = table.astype(ml_dtypes.bfloat16)
    low = (table - high.astype(np.float64)).astype(ml_dtypes.bfloat16)
    return high, low


def packed_table(table):
    return np.concatenate(split_table(table), axis=1)


def signed_waves(length):
    index = np.arange(length)
    return 2.0 * np.pi / length * np.where(index < length // 2, index, index - length)


def derivative_matrix(length, orientation):
    wave = signed_waves(length)
    kernel = np.fft.ifft(1j * wave * np.exp(orientation * 0.5j * wave)).real
    index = np.arange(length)
    return kernel[(index[:, None] - index[None, :]) % length]


def make_tables():
    index = np.arange(256)
    angle = 2.0 * np.pi / 256 * (np.outer(index, index) % 256)
    wave_x = 2.0 * np.pi / NX * np.arange(HALF)

    spectrum = np.exp(-1j * angle[:HALF])
    weight = np.where(np.arange(HALF) == 0, 1.0, 2.0)
    ahead = 1j * wave_x * np.exp(0.5j * wave_x)
    behind = 1j * wave_x * np.exp(-0.5j * wave_x)
    x_rows = np.zeros((8, HALF), np.float32)
    x_rows[0], x_rows[1], x_rows[2] = weight, (weight * ahead).real, (weight * ahead).imag
    forward_z = np.concatenate([np.cos(angle[:HALF]), -np.sin(angle[:HALF])], axis=0)
    forward_z[HALF] = np.cos(angle[HALF])
    inverse_z = 2.0 * forward_z.T
    inverse_z[:, 0] = forward_z[0]
    inverse_z[:, HALF] = forward_z[HALF]
    slab_order = (4 * np.arange(64)[None, :] + np.arange(4)[:, None]).reshape(-1)
    low = np.arange(HALF)
    high = low - 256
    coefficients = np.zeros((HALF, HALF), np.float32)
    coefficients[:, 0] = np.cos(2.0 * np.pi / NZ * low)
    coefficients[:, 1] = np.sin(2.0 * np.pi / NZ * low)

    def derivative(number, orientation):
        wave = 2.0 * np.pi / NZ * number
        return -orientation * wave * np.sin(0.5 * wave), wave * np.cos(0.5 * wave)

    coefficients[:, 16], coefficients[:, 17] = behind.real, behind.imag
    for first, orientation in ((2, 1.0), (9, -1.0)):
        middle_real, middle_imag = derivative(128, orientation)
        for at, number in ((first, low), (first + 3, high)):
            real, imag = derivative(number, orientation)
            coefficients[:, at] = real
            coefficients[:, at + 1] = np.where((low == 0), 0.0, imag)
            coefficients[:, at + 2] = np.where((low == 0), middle_real, real)
        coefficients[:, first + 6] = np.where((low == 0), middle_imag, 0.0)
    x_waves = packed_table(np.concatenate([spectrum.real, spectrum.imag], axis=0))
    y_waves = packed_table(np.cos(angle) + np.sin(angle))
    return {
        "x_waves": x_waves,
        "x_lines": (
            np.concatenate([spectrum.real, spectrum.imag], axis=0) * (X_SCALE * COMPONENT_LINK)
        ).astype(np.float32),
        "middle": np.concatenate(
            [
                x_waves,
                packed_table(derivative_matrix(NY, 1.0)),
                packed_table(derivative_matrix(NY, -1.0)),
            ],
            axis=1,
        ),
        "filter_out": np.concatenate(
            [y_waves, packed_table(forward_z[:, slab_order]), packed_table(inverse_z)], axis=1
        ),
        "filter_back": np.concatenate(
            [y_waves, packed_table(forward_z), packed_table(inverse_z[slab_order])], axis=1
        ),
        "numbers": np.concatenate([coefficients, x_rows], axis=0),
    }


TABLES = make_tables()


def pieces(x, axis):
    high = x.astype(bf16)
    low = (x - high.astype(f32)).astype(bf16)
    return jnp.concatenate([high, low, high], axis=axis)


def contract(a, b, a_dim, b_dim):
    return lax.dot_general(a, b, (((a_dim,), (b_dim,)), ((), ())), preferred_element_type=f32)


def wide(table):
    return jnp.concatenate([table[:, :256], table[:, :512]], axis=1)


def tall(table):
    return jnp.concatenate([table[:, :256], table[:, :256], table[:, 256:512]], axis=0)


def left(table_ref, x):
    return contract(wide(table_ref), pieces(x, 0), 1, 0)


def right(x, table_ref):
    return contract(pieces(x, 1), tall(table_ref), 1, 0)


def to_components(table_ref, lines):
    return contract(wide(table_ref), pieces(lines, 1), 1, 1)


class Fetch:
    def __init__(self, sources, targets, semaphores):
        self.targets = targets
        self.copies = [
            pltpu.make_async_copy(source, target, semaphores.at[i])
            for i, (source, target) in enumerate(zip(sources, targets))
        ]
        for copy in self.copies:
            copy.start()

    def __getitem__(self, i):
        if self.copies[i] is not None:
            self.copies[i].wait()
            self.copies[i] = None
        return self.targets[i]


def times(real, imag, factor_real, factor_imag):
    return real * factor_real - imag * factor_imag, real * factor_imag + imag * factor_real


def kappa_rows(kx, part):
    kz = lax.broadcasted_iota(jnp.int32, (HALF, NY), 0)
    ky = lax.broadcasted_iota(jnp.int32, (HALF, NY), 1)
    number = kz - 256 * (part // 2)
    if part % 2:
        number = jnp.where(kz == 0, 128, number)
    wave_z = number.astype(f32) * (2.0 * math.pi / NZ)
    wave_y = jnp.where(ky < NY // 2, ky, ky - NY).astype(f32) * (2.0 * math.pi / NY)
    wave_x = jnp.full((HALF, NY), kx, jnp.int32).astype(f32) * (2.0 * math.pi / NX)
    square = (kappa_courant / 2.0) ** 2 * (wave_x * wave_x + wave_z * wave_z + wave_y * wave_y)
    total = jnp.full((HALF, NY), 1.0 / math.factorial(15), f32)
    for order in range(6, -1, -1):
        total = 1.0 / math.factorial(2 * order + 1) - square * total
    return total


def forward_z(table_ref, coefficient, fields):
    sides = [side for field in fields for side in (field[:256], field[256:])]
    sums = left(table_ref, jnp.concatenate(sides, axis=1))
    cosine, sine = coefficient(0), coefficient(1)
    spectra = []
    for i in range(0, len(sides), 2):
        even = sums[:, NY * i : NY * (i + 1)]
        odd = sums[:, NY * (i + 1) : NY * (i + 2)]
        real = cosine * odd[:HALF] + sine * odd[HALF:]
        imag = cosine * odd[HALF:] - sine * odd[:HALF]
        spectra.append(
            [even[:HALF] + real, even[HALF:] + imag, even[:HALF] - real, even[HALF:] - imag]
        )
    return spectra


def inverse_z(table_ref, coefficient, spectra):
    cosine, sine = coefficient(0), coefficient(1)
    sides = []
    for a, b, c, d in spectra:
        real, imag = a - c, b - d
        sides.append(jnp.concatenate([a + c, b + d], axis=0))
        sides.append(jnp.concatenate([cosine * real - sine * imag, cosine * imag + sine * real], axis=0))
    return left(table_ref, jnp.concatenate(sides, axis=1))


def derivative_z(coefficient, first, spectrum):
    a, b, c, d = spectrum
    mixed = coefficient(first + 6)
    return [
        coefficient(first) * a - coefficient(first + 1) * b,
        coefficient(first + 2) * b + coefficient(first + 1) * a - mixed * d,
        coefficient(first + 3) * c - coefficient(first + 4) * d,
        coefficient(first + 5) * d + coefficient(first + 4) * c + mixed * b,
    ]


def blocks_of(x):
    return [x[HALF * i : HALF * (i + 1)] for i in range(4)]


def first_half():
    return lax.broadcasted_iota(jnp.int32, (64, HALF), 1) < ROWS


def forward_lines_kernel(pressure, x_ref, out):
    components = to_components(x_ref, pressure[...].reshape(512, NX)) * (X_SCALE * COMPONENT_LINK)
    for i in range(4):
        out[pl.ds(i, 256, stride=4), :] = components[:, HALF * i : HALF * (i + 1)]


def filter_out_kernel(where, data, tables, numbers, out, plane):
    y_ref, z_from_ref, z_to_ref = (tables[:, 512 * i : 512 * (i + 1)] for i in range(3))
    early = first_half()
    for pair in range(4):
        for side in range(2):
            a = data[pl.ds(8 * side + pair, 64, stride=16), :]
            b = data[pl.ds(8 * side + 4 + pair, 64, stride=16), :]
            span = pl.ds(HALF * side, HALF)
            plane[pl.ds(64 * pair, 64), span] = jnp.where(early, a, pltpu.roll(b, ROWS, 1))
            plane[pl.ds(256 + 64 * pair, 64), span] = jnp.where(early, pltpu.roll(a, ROWS, 1), b)
    mixed = right(plane[...], y_ref)

    def coefficient(i):
        return numbers[:HALF, i : i + 1]

    (spectrum,) = forward_z(z_from_ref, coefficient, [mixed])
    scale = SLOPE_LINK / COMPONENT_LINK / (NZ * NY)
    waves = [x * (kappa_rows(where[0] % HALF, part) * scale) for part, x in enumerate(spectrum)]
    waves = blocks_of(right(jnp.concatenate(waves, axis=0), y_ref))
    planes = inverse_z(z_to_ref, coefficient, [waves, derivative_z(coefficient, 2, waves)])
    for field in range(2):
        for r in range(2):
            for side in range(2):
                start = NY * (2 * field + r) + HALF * side
                out[pl.ds(4 * r + 2 * field + side, 256, stride=8), :] = planes[
                    :, start : start + HALF
                ]


def middle_kernel(
    where, data, tables, numbers, near, second, slopes, out, held, fields, semaphores
):
    starts = [
        pl.ds(pl.multiple_of(((where[0] + PEERS_Y - back) % PEERS_Y) * ROWS, ROWS), ROWS)
        for back in range(PEERS_Y)
    ]
    fetch = Fetch(
        (near.at[0], near.at[1], second, near.at[2]),
        [fields.at[:, :, start] for start in starts],
        semaphores,
    )
    x_ref, ya_ref, yb_ref = (tables[:, 512 * i : 512 * (i + 1)] for i in range(3))
    weight, ahead_real, ahead_imag = (numbers[HALF + i : HALF + i + 1, :] for i in range(3))
    behind = numbers[:HALF, 16:17], numbers[:HALF, 17:18]
    returned = []
    for r in range(2):
        q, g = [
            jnp.concatenate(
                [data[pl.ds(4 * r + 2 * field + side, 256, stride=8), :] for side in range(2)], axis=1
            )
            for field in range(2)
        ]
        lines = []
        for x, slope in ((q, True), (q, False), (g, False)):
            x = x.T
            real, imag = x[:, :HALF], x[:, HALF:]
            if slope:
                real, imag = (
                    ahead_real * real - ahead_imag * imag,
                    ahead_real * imag + ahead_imag * real,
                )
            else:
                real, imag = weight * real, weight * imag
            lines.append(jnp.concatenate([real, imag], axis=1))
        lines = right(jnp.concatenate(lines, axis=0), x_ref) * (X_SCALE / SLOPE_LINK)
        along = (lines[:NY], left(ya_ref, lines[NY : 2 * NY]), lines[2 * NY :])
        if r == 0:
            for i in range(4):
                fetch[i]
        moved = []
        for d, slope in enumerate(along):
            held[r, d] = slope * RETURN_LINK
            moved.append(fields[d, r] - fields[3, r] * slope)
        returned.append(pltpu.make_async_copy(held.at[r], slopes.at[:, r], semaphores.at[4 + r]))
        returned[r].start()
        lines = jnp.concatenate([moved[0], left(yb_ref, moved[1]), moved[2]], axis=0)
        components = to_components(x_ref, lines) * (X_SCALE * MIDDLE_LINK)
        real, imag = components[:HALF, :NY], components[HALF:, :NY]
        across = jnp.concatenate(
            times(real, imag, behind[0], behind[1]), axis=0
        ) + components[:, NY : 2 * NY]
        for field, components in enumerate((across, components[:, 2 * NY :])):
            for side in range(2):
                out[pl.ds(4 * r + 2 * field + side, 256, stride=8), :] = components[
                    :, HALF * side : HALF * (side + 1)
                ]
    for copy in returned:
        copy.wait()


def filter_back_kernel(where, data, tables, numbers, out):
    y_ref, z_from_ref, z_to_ref = (tables[:, 512 * i : 512 * (i + 1)] for i in range(3))
    arrived = [
        jnp.concatenate(
            [
                jnp.concatenate(
                    [data[pl.ds(4 * r + 2 * field + side, 256, stride=8), :] for side in range(2)],
                    axis=1,
                )
                for r in range(2)
            ],
            axis=0,
        )
        for field in range(2)
    ]
    def coefficient(i):
        return numbers[:HALF, i : i + 1]

    across, along = forward_z(z_from_ref, coefficient, arrived)
    waves = [x + z for x, z in zip(across, derivative_z(coefficient, 9, along))]
    waves = blocks_of(right(jnp.concatenate(waves, axis=0), y_ref))
    scale = DIVERGENCE_LINK / MIDDLE_LINK / (NZ * NY)
    waves = [x * (kappa_rows(where[0] % HALF, part) * scale) for part, x in enumerate(waves)]
    waves = blocks_of(right(jnp.concatenate(waves, axis=0), y_ref))
    plane = inverse_z(z_to_ref, coefficient, [waves])
    early = first_half()
    for pair in range(4):
        for side in range(2):
            rows = slice(64 * pair, 64 * (pair + 1))
            even = plane[rows, HALF * side : HALF * (side + 1)]
            odd = plane[rows, NY + HALF * side : NY + HALF * (side + 1)]
            out[pl.ds(8 * side + pair, 64, stride=16), :] = jnp.where(
                early, even, pltpu.roll(odd, ROWS, 1)
            )
            out[pl.ds(8 * side + 4 + pair, 64, stride=16), :] = jnp.where(
                early, pltpu.roll(even, ROWS, 1), odd
            )


def new_pressure_kernel(data, x_ref, bulk, own, passed, out, held, semaphores):
    row = lax.broadcasted_iota(jnp.int32, (256, HALF), 0)
    weight = jnp.where((row & (HALF - 1)) == 0, 1.0, 2.0) * (X_SCALE / DIVERGENCE_LINK)
    components = [(data[pl.ds(i, 256, stride=4), :] * weight).T for i in range(4)]
    lines = right(jnp.concatenate(components, axis=0), x_ref).reshape(SLAB, ROWS, NX)
    sent = []
    for i in range(4):
        planes = pl.ds(2 * i, 2)
        held[planes] = own[planes] - bulk[planes] * lines[2 * i : 2 * i + 2]
        held[planes, :TILE] += passed[planes].astype(f32)
        sent.append(pltpu.make_async_copy(held.at[planes], out.at[planes], semaphores.at[i]))
        sent[i].start()
    for copy in sent:
        copy.wait()


def source_kernel(where, lives, c0, c1, c2, t0, t1, t2, pressure, own, passed, l0, l1, l2):
    blank = jnp.zeros((SLAB, 256, NX), bf16)
    l0[:SLAB] = blank
    l2[SLAB:] = blank
    corners = (c0, c1, c2)

    def place(slot, carry):
        rows = pl.ds(pl.multiple_of(slot * TILE, TILE), TILE)
        lane = lax.broadcasted_iota(jnp.int32, (HALF, NX), 1)
        line = lax.broadcasted_iota(jnp.int32, (HALF, NX), 0) & (TILE - 1)
        quarter = lax.broadcasted_iota(jnp.int32, (SLAB, 8, HALF), 2) // TILE
        for reach, (tiles, placed) in enumerate(((t0, l0), (t1, l1), (t2, l2))):
            offset = corners[reach][slot, 0] & (SLAB - 1)
            hot = ((lane - line - corners[reach][slot, 2]) & (NX - 1)) == 0
            hot = jnp.where(hot, 1.0, 0.0).astype(bf16)
            first = SLAB - offset if reach == 1 else 0
            to = 0 if reach == 1 else offset
            block = tiles[slot, pl.ds(first, SLAB)].astype(f32)
            block = jnp.stack([jnp.where(quarter == i, block, 0.0) for i in range(4)], axis=1)
            block = block.reshape(SLAB * TILE, HALF).astype(bf16)
            across = jnp.dot(block, hot, preferred_element_type=f32).astype(bf16)
            placed[pl.ds(to, SLAB), rows, :] = across.reshape(SLAB, TILE, NX)
        return carry

    lax.fori_loop(0, SLOTS_HERE, place, 0)
    line = lax.broadcasted_iota(jnp.int32, (ROWS + TILE, 256), 0)
    lane = lax.broadcasted_iota(jnp.int32, (ROWS + TILE, 256), 1)
    hots = []
    for reach in range(3):
        sender = ((where[0] + PEERS_Z - reach) % PEERS_Z) * PEERS_Y + where[1]
        start = jnp.full((ROWS + TILE, 256), -2 * TILE, jnp.int32)
        for slot in range(SLOTS_HERE):
            row = corners[reach][slot, 1] - where[1] * ROWS
            row = jnp.where(slot < lives[sender], row, -2 * NX)
            within = 4 * (lane & 7) + ((lane // 8) & 3)
            start = jnp.where(lane // TILE == slot, within + row, start)
        hots.append(jnp.where(line == start, 1.0, 0.0).astype(bf16))
    for z in range(SLAB):
        window = jnp.dot(hots[0], l0[z], preferred_element_type=f32)
        window += jnp.dot(hots[1], l1[z], preferred_element_type=f32)
        window += jnp.dot(hots[2], l2[SLAB + z], preferred_element_type=f32)
        own[z] = pressure[z] + window[:ROWS]
        passed[z] = window[ROWS:].astype(bf16)


VMEM = pl.BlockSpec(memory_space=pltpu.VMEM)
SMEM = pl.BlockSpec(memory_space=pltpu.SMEM)
FAR = pl.BlockSpec(memory_space=pltpu.HBM)


def call(kernel, name, specs, arrays, shapes, outs, scratch=(), semaphores=0, limit=20):
    scratch = [pltpu.VMEM(shape, kind) for shape, kind in scratch]
    if semaphores:
        scratch.append(pltpu.SemaphoreType.DMA((semaphores,)))
    return pl.pallas_call(
        kernel,
        out_shape=[jax.ShapeDtypeStruct(shape, kind) for shape, kind in shapes],
        in_specs=specs,
        out_specs=outs,
        scratch_shapes=scratch,
        compiler_params=pltpu.CompilerParams(vmem_limit_bytes=limit << 20),
        cost_estimate=pl.CostEstimate(flops=int(4e8), bytes_accessed=1 << 20, transcendentals=0),
        name=name,
    )(*arrays)


def from_behind(x, axis, by):
    peers = lax.axis_size(axis)
    return lax.ppermute(x, axis, [(i, (i + by) % peers) for i in range(peers)])


def to_rows(slopes, row_block):
    blocks = [
        lax.dynamic_slice_in_dim(slopes, ROWS * ((row_block + ahead) % PEERS_Y), ROWS, 2)
        for ahead in range(PEERS_Y)
    ]
    arrived = [blocks[0]] + [from_behind(blocks[ahead], "gy", ahead) for ahead in range(1, PEERS_Y)]
    ordered = [
        lax.select_n((row_block - device) % PEERS_Y, *arrived) for device in range(PEERS_Y)
    ]
    return jnp.concatenate(ordered, 1).astype(f32)


def exchange(columns, rows):
    blocks = columns.astype(f16).reshape(256, rows, HALF)
    return lax.all_to_all(blocks, ("gz", "gy"), 0, 0, tiled=True)


def arrived(moved):
    return moved.reshape(-1, HALF).astype(f32)


def local(pressure, velocity, bulk, buoyancy, tiles, tile_corner, live_count):
    slab_index = lax.axis_index("gz")
    row_block = lax.axis_index("gy")
    here = row_block.reshape(1).astype(jnp.int32)
    device = (slab_index * PEERS_Y + row_block).astype(jnp.int32)
    place = jnp.stack([slab_index, row_block]).astype(jnp.int32)
    table = {key: jnp.asarray(value) for key, value in TABLES.items()}

    components = jnp.einsum(
        "cx,abx->cab",
        table["x_lines"],
        pressure.reshape(4, HALF, NX),
        precision=lax.Precision.HIGHEST,
    )
    velocity_later, buoyancy_later, tiles, slab_later, components = lax.optimization_barrier(
        (velocity, buoyancy, tiles, slab_index, components)
    )
    fields = jnp.concatenate([velocity_later, buoyancy_later[None]])
    sent = [
        (
            lax.dynamic_slice_in_dim(fields, 2 * ((row_block + ahead) % PEERS_Y), 2, 1) * FIELD_LINK
        ).astype(f16)
        for ahead in range(1, PEERS_Y)
    ]
    own = lax.dynamic_slice_in_dim(fields, 2 * row_block, 2, 1) * FIELD_LINK
    second = from_behind(sent[1], "gy", 2)
    packed = tiles.reshape(SLOTS_HERE, 2 * SLAB, 8, HALF)
    moved, first, third, packed, packed_end = lax.optimization_barrier(
        (exchange(components, 4), sent[0], sent[2], packed, packed[:, SLAB:])
    )
    (filtered,) = call(
        filter_out_kernel,
        "filter_out",
        [SMEM] + [VMEM] * 3,
        [
            device.reshape(1),
            arrived(moved),
            table["filter_out"],
            table["numbers"],
        ],
        [((2048, HALF), f32)],
        [VMEM],
        [((NZ, NY), f32)],
    )
    filtered, own, first, second, third, packed, packed_end = lax.optimization_barrier(
        (filtered, own, first, second, third, packed, packed_end)
    )
    first, third = from_behind(first, "gy", 1), from_behind(third, "gy", 3)
    tiles_before, tiles_second = from_behind(packed, "gz", 1), from_behind(packed_end, "gz", 2)
    moved = exchange(filtered, 8)
    slopes, middle = call(
        middle_kernel,
        "middle",
        [SMEM] + [VMEM] * 3 + [FAR] * 2,
        [
            here,
            arrived(moved),
            table["middle"],
            table["numbers"],
            jnp.stack([own, first.astype(f32), third.astype(f32)]) * (1.0 / FIELD_LINK),
            second.astype(f32) * (1.0 / FIELD_LINK),
        ],
        [((3, 2, NY, NX), f32), ((2048, HALF), f32)],
        [FAR, VMEM],
        [((2, 3, NY, NX), f32), ((4, 2, NY, NX), f32)],
        6,
    )
    middle, slopes, tiles_before, tiles_second = lax.optimization_barrier(
        (middle, slopes.astype(f16), tiles_before, tiles_second)
    )
    slopes = to_rows(slopes, row_block)
    new_velocity = velocity - buoyancy[None] * (slopes * (1.0 / RETURN_LINK))
    corners = [
        lax.dynamic_slice_in_dim(
            tile_corner,
            ((slab_later - reach) % PEERS_Z * PEERS_Y + row_block) * SLOTS_HERE,
            SLOTS_HERE,
            0,
        )
        for reach in range(3)
    ]
    own, passed = call(
        source_kernel,
        "source",
        [SMEM] * 5 + [VMEM] * 4,
        [
            place,
            live_count,
            *corners,
            packed,
            tiles_before,
            tiles_second,
            pressure,
        ],
        [((SLAB, ROWS, NX), f32), ((SLAB, TILE, NX), bf16)],
        [VMEM] * 2,
        [((2 * SLAB, 256, NX), bf16), ((SLAB, 256, NX), bf16), ((2 * SLAB, 256, NX), bf16)],
    )
    (filtered_back,) = call(
        filter_back_kernel,
        "filter_back",
        [SMEM] + [VMEM] * 3,
        [
            device.reshape(1),
            arrived(exchange(middle, 8)),
            table["filter_back"],
            table["numbers"],
        ],
        [((1024, HALF), f32)],
        [VMEM],
    )
    filtered_back, own, passed = lax.optimization_barrier((filtered_back, own, passed))
    passed = from_behind(passed, "gy", 1)
    moved, new_velocity = lax.optimization_barrier((exchange(filtered_back, 4), new_velocity))
    (new_pressure,) = call(
        new_pressure_kernel,
        "new_pressure",
        [VMEM] * 5,
        [arrived(moved), table["x_waves"], bulk, own, passed],
        [((SLAB, ROWS, NX), f32)],
        [FAR],
        [((SLAB, ROWS, NX), f32)],
        4,
    )
    return (new_pressure, new_velocity)


def solution(mesh):
    in_specs = (
        P("gz", "gy", None),
        P(None, "gz", "gy", None),
        P("gz", "gy", None),
        P("gz", "gy", None),
        P(("gz", "gy"), None, None, None),
        P(),
        P(),
    )
    out_specs = (P("gz", "gy", None), P(None, "gz", "gy", None))
    return jax.shard_map(local, mesh=mesh, in_specs=in_specs, out_specs=out_specs, check_vma=False)
```

```python
import math

import jax
import jax.numpy as jnp
import ml_dtypes
import numpy as np
from jax import lax
from jax.experimental import pallas as pl
from jax.experimental.pallas import tpu as pltpu
from jax.sharding import PartitionSpec as P

NX = 256
NY = 256
NZ = 512
HALF = 128
ROWS = 64
SLAB = 8
SLOTS_HERE = 8
TILE = 32
PEERS_Y = 4
PEERS_Z = 64
kappa_courant = 0.3
f32 = jnp.float32
bf16 = jnp.bfloat16
f16 = jnp.float16

X_SCALE = 1.0 / 16.0
FIELD_LINK = 4096.0
COMPONENT_LINK = 256.0
SLOPE_LINK = 128.0
RETURN_LINK = 1024.0
MIDDLE_LINK = 16.0
DIVERGENCE_LINK = 8.0


def split_table(table):
    high = table.astype(ml_dtypes.bfloat16)
    low = (table - high.astype(np.float64)).astype(ml_dtypes.bfloat16)
    return high, low


def packed_table(table):
    return np.concatenate(split_table(table), axis=1)


def signed_waves(length):
    index = np.arange(length)
    return 2.0 * np.pi / length * np.where(index < length // 2, index, index - length)


def derivative_matrix(length, orientation):
    wave = signed_waves(length)
    kernel = np.fft.ifft(1j * wave * np.exp(orientation * 0.5j * wave)).real
    index = np.arange(length)
    return kernel[(index[:, None] - index[None, :]) % length]


def make_tables():
    index = np.arange(256)
    angle = 2.0 * np.pi / 256 * (np.outer(index, index) % 256)
    wave_x = 2.0 * np.pi / NX * np.arange(HALF)

    spectrum = np.exp(-1j * angle[:HALF])
    weight = np.where(np.arange(HALF) == 0, 1.0, 2.0)
    ahead = 1j * wave_x * np.exp(0.5j * wave_x)
    behind = 1j * wave_x * np.exp(-0.5j * wave_x)
    x_rows = np.zeros((8, HALF), np.float32)
    x_rows[0], x_rows[1], x_rows[2] = weight, (weight * ahead).real, (weight * ahead).imag
    forward_z = np.concatenate([np.cos(angle[:HALF]), -np.sin(angle[:HALF])], axis=0)
    forward_z[HALF] = np.cos(angle[HALF])
    inverse_z = 2.0 * forward_z.T
    inverse_z[:, 0] = forward_z[0]
    inverse_z[:, HALF] = forward_z[HALF]
    slab_order = (4 * np.arange(64)[None, :] + np.arange(4)[:, None]).reshape(-1)
    low = np.arange(HALF)
    high = low - 256
    coefficients = np.zeros((HALF, HALF), np.float32)
    coefficients[:, 0] = np.cos(2.0 * np.pi / NZ * low)
    coefficients[:, 1] = np.sin(2.0 * np.pi / NZ * low)

    def derivative(number, orientation):
        wave = 2.0 * np.pi / NZ * number
        return -orientation * wave * np.sin(0.5 * wave), wave * np.cos(0.5 * wave)

    coefficients[:, 16], coefficients[:, 17] = behind.real, behind.imag
    for first, orientation in ((2, 1.0), (9, -1.0)):
        middle_real, middle_imag = derivative(128, orientation)
        for at, number in ((first, low), (first + 3, high)):
            real, imag = derivative(number, orientation)
            coefficients[:, at] = real
            coefficients[:, at + 1] = np.where((low == 0), 0.0, imag)
            coefficients[:, at + 2] = np.where((low == 0), middle_real, real)
        coefficients[:, first + 6] = np.where((low == 0), middle_imag, 0.0)
    x_waves = packed_table(np.concatenate([spectrum.real, spectrum.imag], axis=0))
    y_waves = packed_table(np.cos(angle) + np.sin(angle))
    return {
        "x_waves": x_waves,
        "x_lines": (
            np.concatenate([spectrum.real, spectrum.imag], axis=0) * (X_SCALE * COMPONENT_LINK)
        ).astype(np.float32),
        "middle": np.concatenate(
            [
                x_waves,
                packed_table(derivative_matrix(NY, 1.0)),
                packed_table(derivative_matrix(NY, -1.0)),
            ],
            axis=1,
        ),
        "filter_out": np.concatenate(
            [y_waves, packed_table(forward_z[:, slab_order]), packed_table(inverse_z)], axis=1
        ),
        "filter_back": np.concatenate(
            [y_waves, packed_table(forward_z), packed_table(inverse_z[slab_order])], axis=1
        ),
        "numbers": np.concatenate([coefficients, x_rows], axis=0),
    }


TABLES = make_tables()


def pieces(x, axis):
    high = x.astype(bf16)
    low = (x - high.astype(f32)).astype(bf16)
    return jnp.concatenate([high, low, high], axis=axis)


def contract(a, b, a_dim, b_dim):
    return lax.dot_general(a, b, (((a_dim,), (b_dim,)), ((), ())), preferred_element_type=f32)


def wide(table):
    return jnp.concatenate([table[:, :256], table[:, :512]], axis=1)


def tall(table):
    return jnp.concatenate([table[:, :256], table[:, :256], table[:, 256:512]], axis=0)


def left(table_ref, x):
    return contract(wide(table_ref), pieces(x, 0), 1, 0)


def right(x, table_ref):
    return contract(pieces(x, 1), tall(table_ref), 1, 0)


def to_components(table_ref, lines):
    return contract(wide(table_ref), pieces(lines, 1), 1, 1)


class Fetch:
    def __init__(self, sources, targets, semaphores):
        self.targets = targets
        self.copies = [
            pltpu.make_async_copy(source, target, semaphores.at[i])
            for i, (source, target) in enumerate(zip(sources, targets))
        ]
        for copy in self.copies:
            copy.start()

    def __getitem__(self, i):
        if self.copies[i] is not None:
            self.copies[i].wait()
            self.copies[i] = None
        return self.targets[i]


def times(real, imag, factor_real, factor_imag):
    return real * factor_real - imag * factor_imag, real * factor_imag + imag * factor_real


def kappa_rows(kx, part):
    kz = lax.broadcasted_iota(jnp.int32, (HALF, NY), 0)
    ky = lax.broadcasted_iota(jnp.int32, (HALF, NY), 1)
    number = kz - 256 * (part // 2)
    if part % 2:
        number = jnp.where(kz == 0, 128, number)
    wave_z = number.astype(f32) * (2.0 * math.pi / NZ)
    wave_y = jnp.where(ky < NY // 2, ky, ky - NY).astype(f32) * (2.0 * math.pi / NY)
    wave_x = jnp.full((HALF, NY), kx, jnp.int32).astype(f32) * (2.0 * math.pi / NX)
    square = (kappa_courant / 2.0) ** 2 * (wave_x * wave_x + wave_z * wave_z + wave_y * wave_y)
    total = jnp.full((HALF, NY), 1.0 / math.factorial(15), f32)
    for order in range(6, -1, -1):
        total = 1.0 / math.factorial(2 * order + 1) - square * total
    return total


def forward_z(table_ref, coefficient, fields):
    sides = [side for field in fields for side in (field[:256], field[256:])]
    sums = left(table_ref, jnp.concatenate(sides, axis=1))
    cosine, sine = coefficient(0), coefficient(1)
    spectra = []
    for i in range(0, len(sides), 2):
        even = sums[:, NY * i : NY * (i + 1)]
        odd = sums[:, NY * (i + 1) : NY * (i + 2)]
        real = cosine * odd[:HALF] + sine * odd[HALF:]
        imag = cosine * odd[HALF:] - sine * odd[:HALF]
        spectra.append(
            [even[:HALF] + real, even[HALF:] + imag, even[:HALF] - real, even[HALF:] - imag]
        )
    return spectra


def inverse_z(table_ref, coefficient, spectra):
    cosine, sine = coefficient(0), coefficient(1)
    sides = []
    for a, b, c, d in spectra:
        real, imag = a - c, b - d
        sides.append(jnp.concatenate([a + c, b + d], axis=0))
        sides.append(jnp.concatenate([cosine * real - sine * imag, cosine * imag + sine * real], axis=0))
    return left(table_ref, jnp.concatenate(sides, axis=1))


def derivative_z(coefficient, first, spectrum):
    a, b, c, d = spectrum
    mixed = coefficient(first + 6)
    return [
        coefficient(first) * a - coefficient(first + 1) * b,
        coefficient(first + 2) * b + coefficient(first + 1) * a - mixed * d,
        coefficient(first + 3) * c - coefficient(first + 4) * d,
        coefficient(first + 5) * d + coefficient(first + 4) * c + mixed * b,
    ]


def blocks_of(x):
    return [x[HALF * i : HALF * (i + 1)] for i in range(4)]


def filtered_rows(blocks, y_ref, kx, scale):
    out = []
    for part, block in enumerate(blocks):
        waves = right(block, y_ref) * (kappa_rows(kx, part) * scale)
        out.append(right(waves, y_ref))
    return out


def first_half():
    return lax.broadcasted_iota(jnp.int32, (64, HALF), 1) < ROWS


def forward_lines_kernel(pressure, x_ref, out):
    components = to_components(x_ref, pressure[...].reshape(512, NX)) * (X_SCALE * COMPONENT_LINK)
    for i in range(4):
        out[pl.ds(i, 256, stride=4), :] = components[:, HALF * i : HALF * (i + 1)]


def filter_out_kernel(where, data, tables, numbers, out, plane):
    y_ref, z_from_ref, z_to_ref = (tables[:, 512 * i : 512 * (i + 1)] for i in range(3))
    early = first_half()
    for pair in range(4):
        for side in range(2):
            a = data[pl.ds(8 * side + pair, 64, stride=16), :]
            b = data[pl.ds(8 * side + 4 + pair, 64, stride=16), :]
            span = pl.ds(HALF * side, HALF)
            plane[pl.ds(64 * pair, 64), span] = jnp.where(early, a, pltpu.roll(b, ROWS, 1))
            plane[pl.ds(256 + 64 * pair, 64), span] = jnp.where(early, pltpu.roll(a, ROWS, 1), b)
    def coefficient(i):
        return numbers[:HALF, i : i + 1]

    (waves,) = forward_z(z_from_ref, coefficient, [plane[...]])
    waves = filtered_rows(waves, y_ref, where[0] % HALF, SLOPE_LINK / COMPONENT_LINK / (NZ * NY))
    planes = inverse_z(z_to_ref, coefficient, [waves, derivative_z(coefficient, 2, waves)])
    for field in range(2):
        for r in range(2):
            for side in range(2):
                start = NY * (2 * field + r) + HALF * side
                out[pl.ds(4 * r + 2 * field + side, 256, stride=8), :] = planes[
                    :, start : start + HALF
                ]


def middle_kernel(
    where, data, tables, numbers, near, second, slopes, out, held, fields, semaphores
):
    starts = [
        pl.ds(pl.multiple_of(((where[0] + PEERS_Y - back) % PEERS_Y) * ROWS, ROWS), ROWS)
        for back in range(PEERS_Y)
    ]
    fetch = Fetch(
        (near.at[0], near.at[1], second, near.at[2]),
        [fields.at[:, :, start] for start in starts],
        semaphores,
    )
    x_ref, ya_ref, yb_ref = (tables[:, 512 * i : 512 * (i + 1)] for i in range(3))
    weight, ahead_real, ahead_imag = (numbers[HALF + i : HALF + i + 1, :] for i in range(3))
    behind = numbers[:HALF, 16:17], numbers[:HALF, 17:18]
    q, g = [
        jnp.concatenate(
            [
                data[pl.ds(4 * r + 2 * field + side, 256, stride=8), :]
                for r in range(2)
                for side in range(2)
            ],
            axis=1,
        ).T
        for field in range(2)
    ]
    real, imag = q[:, :HALF], q[:, HALF:]
    lines = jnp.concatenate(
        [
            ahead_real * real - ahead_imag * imag,
            weight * real,
            weight * g[:, :HALF],
            ahead_real * imag + ahead_imag * real,
            weight * imag,
            weight * g[:, HALF:],
        ],
        axis=0,
    )
    lines = jnp.concatenate([lines[: 3 * 512], lines[3 * 512 :]], axis=1)
    lines = right(lines, x_ref) * (X_SCALE / SLOPE_LINK)
    along_y = left(ya_ref, jnp.concatenate([lines[512:768], lines[768:1024]], axis=1))
    along = (
        (lines[:256], lines[256:512]),
        (along_y[:, :NX], along_y[:, NX:]),
        (lines[1024:1280], lines[1280:]),
    )
    for d in range(3):
        for r in range(2):
            held[d, r] = along[d][r] * RETURN_LINK
    returned = pltpu.make_async_copy(held, slopes, semaphores.at[4])
    returned.start()
    for i in range(4):
        fetch[i]
    moved = [[fields[d, r] - fields[3, r] * along[d][r] for r in range(2)] for d in range(3)]
    along_y = left(yb_ref, jnp.concatenate(moved[1], axis=1))
    lines = jnp.concatenate([*moved[0], along_y[:, :NX], along_y[:, NX:], *moved[2]], axis=0)
    components = to_components(x_ref, lines) * (X_SCALE * MIDDLE_LINK)
    real, imag = components[:HALF, : 2 * NY], components[HALF:, : 2 * NY]
    across = jnp.concatenate(times(real, imag, behind[0], behind[1]), axis=0)
    for field, part in enumerate((across + components[:, 2 * NY : 4 * NY], components[:, 4 * NY :])):
        for r in range(2):
            for side in range(2):
                out[pl.ds(4 * r + 2 * field + side, 256, stride=8), :] = part[
                    :, NY * r + HALF * side : NY * r + HALF * (side + 1)
                ]
    returned.wait()


def filter_back_kernel(where, data, tables, numbers, out):
    y_ref, z_from_ref, z_to_ref = (tables[:, 512 * i : 512 * (i + 1)] for i in range(3))
    arrived = [
        jnp.concatenate(
            [
                jnp.concatenate(
                    [data[pl.ds(4 * r + 2 * field + side, 256, stride=8), :] for side in range(2)],
                    axis=1,
                )
                for r in range(2)
            ],
            axis=0,
        )
        for field in range(2)
    ]
    def coefficient(i):
        return numbers[:HALF, i : i + 1]

    across, along = forward_z(z_from_ref, coefficient, arrived)
    waves = [x + z for x, z in zip(across, derivative_z(coefficient, 9, along))]
    scale = DIVERGENCE_LINK / MIDDLE_LINK / (NZ * NY)
    waves = filtered_rows(waves, y_ref, where[0] % HALF, scale)
    plane = inverse_z(z_to_ref, coefficient, [waves])
    early = first_half()
    for pair in range(4):
        for side in range(2):
            rows = slice(64 * pair, 64 * (pair + 1))
            even = plane[rows, HALF * side : HALF * (side + 1)]
            odd = plane[rows, NY + HALF * side : NY + HALF * (side + 1)]
            out[pl.ds(8 * side + pair, 64, stride=16), :] = jnp.where(
                early, even, pltpu.roll(odd, ROWS, 1)
            )
            out[pl.ds(8 * side + 4 + pair, 64, stride=16), :] = jnp.where(
                early, pltpu.roll(even, ROWS, 1), odd
            )


def new_pressure_kernel(data, x_ref, bulk, own, passed, out, held, semaphores):
    row = lax.broadcasted_iota(jnp.int32, (256, HALF), 0)
    weight = jnp.where((row & (HALF - 1)) == 0, 1.0, 2.0) * (X_SCALE / DIVERGENCE_LINK)
    components = [(data[pl.ds(i, 256, stride=4), :] * weight).T for i in range(4)]
    lines = right(jnp.concatenate(components, axis=0), x_ref).reshape(SLAB, ROWS, NX)
    sent = []
    for i in range(4):
        planes = pl.ds(2 * i, 2)
        held[planes] = own[planes] - bulk[planes] * lines[2 * i : 2 * i + 2]
        held[planes, :TILE] += passed[planes].astype(f32)
        sent.append(pltpu.make_async_copy(held.at[planes], out.at[planes], semaphores.at[i]))
        sent[i].start()
    for copy in sent:
        copy.wait()


def source_kernel(where, lives, c0, c1, c2, t0, t1, t2, pressure, own, passed, l0, l1, l2):
    blank = jnp.zeros((SLAB, 256, NX), bf16)
    l0[:SLAB] = blank
    l2[SLAB:] = blank
    corners = (c0, c1, c2)

    def place(slot, carry):
        rows = pl.ds(pl.multiple_of(slot * TILE, TILE), TILE)
        lane = lax.broadcasted_iota(jnp.int32, (HALF, NX), 1)
        line = lax.broadcasted_iota(jnp.int32, (HALF, NX), 0) & (TILE - 1)
        quarter = lax.broadcasted_iota(jnp.int32, (SLAB, 8, HALF), 2) // TILE
        for reach, (tiles, placed) in enumerate(((t0, l0), (t1, l1), (t2, l2))):
            offset = corners[reach][slot, 0] & (SLAB - 1)
            hot = ((lane - line - corners[reach][slot, 2]) & (NX - 1)) == 0
            hot = jnp.where(hot, 1.0, 0.0).astype(bf16)
            first = SLAB - offset if reach == 1 else 0
            to = 0 if reach == 1 else offset
            block = tiles[slot, pl.ds(first, SLAB)].astype(f32)
            block = jnp.stack([jnp.where(quarter == i, block, 0.0) for i in range(4)], axis=1)
            block = block.reshape(SLAB * TILE, HALF).astype(bf16)
            across = jnp.dot(block, hot, preferred_element_type=f32).astype(bf16)
            placed[pl.ds(to, SLAB), rows, :] = across.reshape(SLAB, TILE, NX)
        return carry

    lax.fori_loop(0, SLOTS_HERE, place, 0)
    line = lax.broadcasted_iota(jnp.int32, (ROWS + TILE, 256), 0)
    lane = lax.broadcasted_iota(jnp.int32, (ROWS + TILE, 256), 1)
    hots = []
    for reach in range(3):
        sender = ((where[0] + PEERS_Z - reach) % PEERS_Z) * PEERS_Y + where[1]
        start = jnp.full((ROWS + TILE, 256), -2 * TILE, jnp.int32)
        for slot in range(SLOTS_HERE):
            row = corners[reach][slot, 1] - where[1] * ROWS
            row = jnp.where(slot < lives[sender], row, -2 * NX)
            within = 4 * (lane & 7) + ((lane // 8) & 3)
            start = jnp.where(lane // TILE == slot, within + row, start)
        hots.append(jnp.where(line == start, 1.0, 0.0).astype(bf16))
    for z in range(SLAB):
        window = jnp.dot(hots[0], l0[z], preferred_element_type=f32)
        window += jnp.dot(hots[1], l1[z], preferred_element_type=f32)
        window += jnp.dot(hots[2], l2[SLAB + z], preferred_element_type=f32)
        own[z] = pressure[z] + window[:ROWS]
        passed[z] = window[ROWS:].astype(bf16)


VMEM = pl.BlockSpec(memory_space=pltpu.VMEM)
SMEM = pl.BlockSpec(memory_space=pltpu.SMEM)
FAR = pl.BlockSpec(memory_space=pltpu.HBM)


def call(kernel, name, specs, arrays, shapes, outs, scratch=(), semaphores=0, limit=20):
    scratch = [pltpu.VMEM(shape, kind) for shape, kind in scratch]
    if semaphores:
        scratch.append(pltpu.SemaphoreType.DMA((semaphores,)))
    return pl.pallas_call(
        kernel,
        out_shape=[jax.ShapeDtypeStruct(shape, kind) for shape, kind in shapes],
        in_specs=specs,
        out_specs=outs,
        scratch_shapes=scratch,
        compiler_params=pltpu.CompilerParams(vmem_limit_bytes=limit << 20),
        cost_estimate=pl.CostEstimate(flops=int(4e8), bytes_accessed=1 << 20, transcendentals=0),
        name=name,
    )(*arrays)


def from_behind(x, axis, by):
    peers = lax.axis_size(axis)
    return lax.ppermute(x, axis, [(i, (i + by) % peers) for i in range(peers)])


def to_rows(slopes, row_block):
    blocks = [
        lax.dynamic_slice_in_dim(slopes, ROWS * ((row_block + ahead) % PEERS_Y), ROWS, 2)
        for ahead in range(PEERS_Y)
    ]
    arrived = [blocks[0]] + [from_behind(blocks[ahead], "gy", ahead) for ahead in range(1, PEERS_Y)]
    ordered = [
        lax.select_n((row_block - device) % PEERS_Y, *arrived) for device in range(PEERS_Y)
    ]
    return jnp.concatenate(ordered, 1).astype(f32)


def exchange(columns, rows):
    blocks = columns.astype(f16).reshape(256, rows, HALF)
    return lax.all_to_all(blocks, ("gz", "gy"), 0, 0, tiled=True)


def arrived(moved):
    return moved.reshape(-1, HALF).astype(f32)


def local(pressure, velocity, bulk, buoyancy, tiles, tile_corner, live_count):
    slab_index = lax.axis_index("gz")
    row_block = lax.axis_index("gy")
    here = row_block.reshape(1).astype(jnp.int32)
    device = (slab_index * PEERS_Y + row_block).astype(jnp.int32)
    place = jnp.stack([slab_index, row_block]).astype(jnp.int32)
    table = {key: jnp.asarray(value) for key, value in TABLES.items()}

    components = jnp.einsum(
        "cx,abx->cab",
        table["x_lines"],
        pressure.reshape(4, HALF, NX),
        precision=lax.Precision.HIGHEST,
    )
    velocity_later, buoyancy_later, tiles, slab_later, components = lax.optimization_barrier(
        (velocity, buoyancy, tiles, slab_index, components)
    )
    fields = jnp.concatenate([velocity_later, buoyancy_later[None]])
    sent = [
        (
            lax.dynamic_slice_in_dim(fields, 2 * ((row_block + ahead) % PEERS_Y), 2, 1) * FIELD_LINK
        ).astype(f16)
        for ahead in range(1, PEERS_Y)
    ]
    own = lax.dynamic_slice_in_dim(fields, 2 * row_block, 2, 1) * FIELD_LINK
    first, third = from_behind(sent[0], "gy", 1), from_behind(sent[2], "gy", 3)
    packed = tiles.reshape(SLOTS_HERE, 2 * SLAB, 8, HALF)
    moved, second, packed, packed_end = lax.optimization_barrier(
        (exchange(components, 4), sent[1], packed, packed[:, SLAB:])
    )
    (filtered,) = call(
        filter_out_kernel,
        "filter_out",
        [SMEM] + [VMEM] * 3,
        [
            device.reshape(1),
            arrived(moved),
            table["filter_out"],
            table["numbers"],
        ],
        [((2048, HALF), f32)],
        [VMEM],
        [((NZ, NY), f32)],
    )
    filtered, own, first, second, third, packed, packed_end = lax.optimization_barrier(
        (filtered, own, first, second, third, packed, packed_end)
    )
    second = from_behind(second, "gy", 2)
    tiles_before, tiles_second = from_behind(packed, "gz", 1), from_behind(packed_end, "gz", 2)
    moved = exchange(filtered, 8)
    slopes, middle = call(
        middle_kernel,
        "middle",
        [SMEM] + [VMEM] * 3 + [FAR] * 2,
        [
            here,
            arrived(moved),
            table["middle"],
            table["numbers"],
            jnp.stack([own, first.astype(f32), third.astype(f32)]) * (1.0 / FIELD_LINK),
            second.astype(f32) * (1.0 / FIELD_LINK),
        ],
        [((3, 2, NY, NX), f32), ((2048, HALF), f32)],
        [FAR, VMEM],
        [((3, 2, NY, NX), f32), ((4, 2, NY, NX), f32)],
        5,
    )
    middle, slopes, tiles_before, tiles_second = lax.optimization_barrier(
        (middle, slopes.astype(f16), tiles_before, tiles_second)
    )
    slopes = to_rows(slopes, row_block)
    new_velocity = velocity - buoyancy[None] * (slopes * (1.0 / RETURN_LINK))
    corners = [
        lax.dynamic_slice_in_dim(
            tile_corner,
            ((slab_later - reach) % PEERS_Z * PEERS_Y + row_block) * SLOTS_HERE,
            SLOTS_HERE,
            0,
        )
        for reach in range(3)
    ]
    own, passed = call(
        source_kernel,
        "source",
        [SMEM] * 5 + [VMEM] * 4,
        [
            place,
            live_count,
            *corners,
            packed,
            tiles_before,
            tiles_second,
            pressure,
        ],
        [((SLAB, ROWS, NX), f32), ((SLAB, TILE, NX), bf16)],
        [VMEM] * 2,
        [((2 * SLAB, 256, NX), bf16), ((SLAB, 256, NX), bf16), ((2 * SLAB, 256, NX), bf16)],
    )
    (filtered_back,) = call(
        filter_back_kernel,
        "filter_back",
        [SMEM] + [VMEM] * 3,
        [
            device.reshape(1),
            arrived(exchange(middle, 8)),
            table["filter_back"],
            table["numbers"],
        ],
        [((1024, HALF), f32)],
        [VMEM],
    )
    filtered_back, own, passed = lax.optimization_barrier((filtered_back, own, passed))
    passed = from_behind(passed, "gy", 1)
    moved, new_velocity = lax.optimization_barrier((exchange(filtered_back, 4), new_velocity))
    (new_pressure,) = call(
        new_pressure_kernel,
        "new_pressure",
        [VMEM] * 5,
        [arrived(moved), table["x_waves"], bulk, own, passed],
        [((SLAB, ROWS, NX), f32)],
        [FAR],
        [((SLAB, ROWS, NX), f32)],
        4,
    )
    return (new_pressure, new_velocity)


def solution(mesh):
    in_specs = (
        P("gz", "gy", None),
        P(None, "gz", "gy", None),
        P("gz", "gy", None),
        P("gz", "gy", None),
        P(("gz", "gy"), None, None, None),
        P(),
        P(),
    )
    out_specs = (P("gz", "gy", None), P(None, "gz", "gy", None))
    return jax.shard_map(local, mesh=mesh, in_specs=in_specs, out_specs=out_specs, check_vma=False)
```

```python
import math

import jax
import jax.numpy as jnp
import ml_dtypes
import numpy as np
from jax import lax
from jax.experimental import pallas as pl
from jax.experimental.pallas import tpu as pltpu
from jax.sharding import PartitionSpec as P

NX = 256
NY = 256
NZ = 512
HALF = 128
ROWS = 64
SLAB = 8
SLOTS_HERE = 8
TILE = 32
PEERS_Y = 4
PEERS_Z = 64
kappa_courant = 0.3
f32 = jnp.float32
bf16 = jnp.bfloat16
f16 = jnp.float16

X_SCALE = 1.0 / 16.0
FIELD_LINK = 4096.0
COMPONENT_LINK = 256.0
SLOPE_LINK = 128.0
RETURN_LINK = 1024.0
MIDDLE_LINK = 16.0
DIVERGENCE_LINK = 8.0


def split_table(table):
    high = table.astype(ml_dtypes.bfloat16)
    low = (table - high.astype(np.float64)).astype(ml_dtypes.bfloat16)
    return high, low


def packed_table(table):
    return np.concatenate(split_table(table), axis=1)


def signed_waves(length):
    index = np.arange(length)
    return 2.0 * np.pi / length * np.where(index < length // 2, index, index - length)


def derivative_matrix(length, orientation):
    wave = signed_waves(length)
    kernel = np.fft.ifft(1j * wave * np.exp(orientation * 0.5j * wave)).real
    index = np.arange(length)
    return kernel[(index[:, None] - index[None, :]) % length]


def make_tables():
    index = np.arange(256)
    angle = 2.0 * np.pi / 256 * (np.outer(index, index) % 256)
    wave_x = 2.0 * np.pi / NX * np.arange(HALF)

    spectrum = np.exp(-1j * angle[:HALF])
    weight = np.where(np.arange(HALF) == 0, 1.0, 2.0)
    ahead = 1j * wave_x * np.exp(0.5j * wave_x)
    behind = 1j * wave_x * np.exp(-0.5j * wave_x)
    x_rows = np.zeros((8, HALF), np.float32)
    x_rows[0], x_rows[1], x_rows[2] = weight, (weight * ahead).real, (weight * ahead).imag
    forward_z = np.concatenate([np.cos(angle[:HALF]), -np.sin(angle[:HALF])], axis=0)
    forward_z[HALF] = np.cos(angle[HALF])
    inverse_z = 2.0 * forward_z.T
    inverse_z[:, 0] = forward_z[0]
    inverse_z[:, HALF] = forward_z[HALF]
    slab_order = (4 * np.arange(64)[None, :] + np.arange(4)[:, None]).reshape(-1)
    low = np.arange(HALF)
    high = low - 256
    coefficients = np.zeros((HALF, HALF), np.float32)
    coefficients[:, 0] = np.cos(2.0 * np.pi / NZ * low)
    coefficients[:, 1] = np.sin(2.0 * np.pi / NZ * low)

    def derivative(number, orientation):
        wave = 2.0 * np.pi / NZ * number
        return -orientation * wave * np.sin(0.5 * wave), wave * np.cos(0.5 * wave)

    coefficients[:, 16], coefficients[:, 17] = behind.real, behind.imag
    for first, orientation in ((2, 1.0), (9, -1.0)):
        middle_real, middle_imag = derivative(128, orientation)
        for at, number in ((first, low), (first + 3, high)):
            real, imag = derivative(number, orientation)
            coefficients[:, at] = real
            coefficients[:, at + 1] = np.where((low == 0), 0.0, imag)
            coefficients[:, at + 2] = np.where((low == 0), middle_real, real)
        coefficients[:, first + 6] = np.where((low == 0), middle_imag, 0.0)
    x_waves = packed_table(np.concatenate([spectrum.real, spectrum.imag], axis=0))
    y_waves = packed_table(np.cos(angle) + np.sin(angle))
    return {
        "x_waves": x_waves,
        "x_lines": (
            np.concatenate([spectrum.real, spectrum.imag], axis=0) * (X_SCALE * COMPONENT_LINK)
        ).astype(np.float32),
        "middle": np.concatenate(
            [
                x_waves,
                packed_table(derivative_matrix(NY, 1.0)),
                packed_table(derivative_matrix(NY, -1.0)),
            ],
            axis=1,
        ),
        "filter_out": np.concatenate(
            [y_waves, packed_table(forward_z[:, slab_order]), packed_table(inverse_z)], axis=1
        ),
        "filter_back": np.concatenate(
            [y_waves, packed_table(forward_z), packed_table(inverse_z[slab_order])], axis=1
        ),
        "numbers": np.concatenate([coefficients, x_rows], axis=0),
    }


TABLES = make_tables()


def pieces(x, axis):
    high = x.astype(bf16)
    low = (x - high.astype(f32)).astype(bf16)
    return jnp.concatenate([high, low, high], axis=axis)


def contract(a, b, a_dim, b_dim):
    return lax.dot_general(a, b, (((a_dim,), (b_dim,)), ((), ())), preferred_element_type=f32)


def wide(table):
    return jnp.concatenate([table[:, :256], table[:, :512]], axis=1)


def tall(table):
    return jnp.concatenate([table[:, :256], table[:, :256], table[:, 256:512]], axis=0)


def left(table_ref, x):
    return contract(wide(table_ref), pieces(x, 0), 1, 0)


def right(x, table_ref):
    return contract(pieces(x, 1), tall(table_ref), 1, 0)


def to_components(table_ref, lines):
    return contract(wide(table_ref), pieces(lines, 1), 1, 1)


class Fetch:
    def __init__(self, sources, targets, semaphores):
        self.targets = targets
        self.copies = [
            pltpu.make_async_copy(source, target, semaphores.at[i])
            for i, (source, target) in enumerate(zip(sources, targets))
        ]
        for copy in self.copies:
            copy.start()

    def __getitem__(self, i):
        if self.copies[i] is not None:
            self.copies[i].wait()
            self.copies[i] = None
        return self.targets[i]


def times(real, imag, factor_real, factor_imag):
    return real * factor_real - imag * factor_imag, real * factor_imag + imag * factor_real


def kappa_rows(kx, part):
    kz = lax.broadcasted_iota(jnp.int32, (HALF, NY), 0)
    ky = lax.broadcasted_iota(jnp.int32, (HALF, NY), 1)
    number = kz - 256 * (part // 2)
    if part % 2:
        number = jnp.where(kz == 0, 128, number)
    wave_z = number.astype(f32) * (2.0 * math.pi / NZ)
    wave_y = jnp.where(ky < NY // 2, ky, ky - NY).astype(f32) * (2.0 * math.pi / NY)
    wave_x = jnp.full((HALF, NY), kx, jnp.int32).astype(f32) * (2.0 * math.pi / NX)
    square = (kappa_courant / 2.0) ** 2 * (wave_x * wave_x + wave_z * wave_z + wave_y * wave_y)
    total = jnp.full((HALF, NY), 1.0 / math.factorial(15), f32)
    for order in range(6, -1, -1):
        total = 1.0 / math.factorial(2 * order + 1) - square * total
    return total


def forward_z(table_ref, coefficient, fields):
    sides = [side for field in fields for side in (field[:256], field[256:])]
    sums = left(table_ref, jnp.concatenate(sides, axis=1))
    cosine, sine = coefficient(0), coefficient(1)
    spectra = []
    for i in range(0, len(sides), 2):
        even = sums[:, NY * i : NY * (i + 1)]
        odd = sums[:, NY * (i + 1) : NY * (i + 2)]
        real = cosine * odd[:HALF] + sine * odd[HALF:]
        imag = cosine * odd[HALF:] - sine * odd[:HALF]
        spectra.append(
            [even[:HALF] + real, even[HALF:] + imag, even[:HALF] - real, even[HALF:] - imag]
        )
    return spectra


def inverse_z(table_ref, coefficient, spectra):
    cosine, sine = coefficient(0), coefficient(1)
    sides = []
    for a, b, c, d in spectra:
        real, imag = a - c, b - d
        sides.append(jnp.concatenate([a + c, b + d], axis=0))
        sides.append(jnp.concatenate([cosine * real - sine * imag, cosine * imag + sine * real], axis=0))
    return left(table_ref, jnp.concatenate(sides, axis=1))


def derivative_z(coefficient, first, spectrum):
    a, b, c, d = spectrum
    mixed = coefficient(first + 6)
    return [
        coefficient(first) * a - coefficient(first + 1) * b,
        coefficient(first + 2) * b + coefficient(first + 1) * a - mixed * d,
        coefficient(first + 3) * c - coefficient(first + 4) * d,
        coefficient(first + 5) * d + coefficient(first + 4) * c + mixed * b,
    ]


def blocks_of(x):
    return [x[HALF * i : HALF * (i + 1)] for i in range(4)]


def filtered_rows(blocks, y_ref, kx, scale):
    out = []
    for part, block in enumerate(blocks):
        waves = right(block, y_ref) * (kappa_rows(kx, part) * scale)
        out.append(right(waves, y_ref))
    return out


def first_half():
    return lax.broadcasted_iota(jnp.int32, (64, HALF), 1) < ROWS


def forward_lines_kernel(pressure, x_ref, out):
    components = to_components(x_ref, pressure[...].reshape(512, NX)) * (X_SCALE * COMPONENT_LINK)
    for i in range(4):
        out[pl.ds(i, 256, stride=4), :] = components[:, HALF * i : HALF * (i + 1)]


def filter_out_kernel(where, data, tables, numbers, out, plane):
    y_ref, z_from_ref, z_to_ref = (tables[:, 512 * i : 512 * (i + 1)] for i in range(3))
    early = first_half()
    for pair in range(4):
        for side in range(2):
            a = data[pl.ds(8 * side + pair, 64, stride=16), :]
            b = data[pl.ds(8 * side + 4 + pair, 64, stride=16), :]
            span = pl.ds(HALF * side, HALF)
            plane[pl.ds(64 * pair, 64), span] = jnp.where(early, a, pltpu.roll(b, ROWS, 1))
            plane[pl.ds(256 + 64 * pair, 64), span] = jnp.where(early, pltpu.roll(a, ROWS, 1), b)
    def coefficient(i):
        return numbers[:HALF, i : i + 1]

    (waves,) = forward_z(z_from_ref, coefficient, [plane[...]])
    waves = filtered_rows(waves, y_ref, where[0] % HALF, SLOPE_LINK / COMPONENT_LINK / (NZ * NY))
    planes = inverse_z(z_to_ref, coefficient, [waves, derivative_z(coefficient, 2, waves)])
    for field in range(2):
        for r in range(2):
            for side in range(2):
                start = NY * (2 * field + r) + HALF * side
                out[pl.ds(4 * r + 2 * field + side, 256, stride=8), :] = planes[
                    :, start : start + HALF
                ]


def middle_kernel(
    where, data, tables, numbers, near, second, slopes, out, held, fields, semaphores
):
    starts = [
        pl.ds(pl.multiple_of(((where[0] + PEERS_Y - back) % PEERS_Y) * ROWS, ROWS), ROWS)
        for back in range(PEERS_Y)
    ]
    fetch = Fetch(
        (near.at[0], near.at[1], second, near.at[2]),
        [fields.at[:, :, start] for start in starts],
        semaphores,
    )
    x_ref, ya_ref, yb_ref = (tables[:, 512 * i : 512 * (i + 1)] for i in range(3))
    weight, ahead_real, ahead_imag = (numbers[HALF + i : HALF + i + 1, :] for i in range(3))
    behind = numbers[:HALF, 16:17], numbers[:HALF, 17:18]
    q, g = [
        jnp.concatenate(
            [
                data[pl.ds(4 * r + 2 * field + side, 256, stride=8), :]
                for r in range(2)
                for side in range(2)
            ],
            axis=1,
        ).T
        for field in range(2)
    ]
    real, imag = q[:, :HALF], q[:, HALF:]
    scale = X_SCALE / SLOPE_LINK
    plain = right(jnp.concatenate([weight * real, weight * imag], axis=1), x_ref) * scale
    steep = jnp.concatenate(
        [ahead_real * real - ahead_imag * imag, ahead_real * imag + ahead_imag * real], axis=1
    )
    steep = right(steep, x_ref) * scale
    along_y = left(ya_ref, jnp.concatenate([plain[:256], plain[256:]], axis=1))
    along_z = jnp.concatenate([weight * g[:, :HALF], weight * g[:, HALF:]], axis=1)
    along_z = right(along_z, x_ref) * scale
    along = (
        (steep[:256], steep[256:]),
        (along_y[:, :NX], along_y[:, NX:]),
        (along_z[:256], along_z[256:]),
    )
    for d in range(3):
        for r in range(2):
            held[d, r] = along[d][r] * RETURN_LINK
    returned = pltpu.make_async_copy(held, slopes, semaphores.at[4])
    returned.start()
    for i in range(4):
        fetch[i]
    moved = [[fields[d, r] - fields[3, r] * along[d][r] for r in range(2)] for d in range(3)]
    along_y = left(yb_ref, jnp.concatenate(moved[1], axis=1))
    scale = X_SCALE * MIDDLE_LINK
    steep, along_z, along_y = [
        to_components(x_ref, jnp.concatenate(lines, axis=0)) * scale
        for lines in (moved[0], moved[2], (along_y[:, :NX], along_y[:, NX:]))
    ]
    across = jnp.concatenate(times(steep[:HALF], steep[HALF:], behind[0], behind[1]), axis=0)
    for field, part in enumerate((across + along_y, along_z)):
        for r in range(2):
            for side in range(2):
                out[pl.ds(4 * r + 2 * field + side, 256, stride=8), :] = part[
                    :, NY * r + HALF * side : NY * r + HALF * (side + 1)
                ]
    returned.wait()


def filter_back_kernel(where, data, tables, numbers, out):
    y_ref, z_from_ref, z_to_ref = (tables[:, 512 * i : 512 * (i + 1)] for i in range(3))
    arrived = [
        jnp.concatenate(
            [
                jnp.concatenate(
                    [data[pl.ds(4 * r + 2 * field + side, 256, stride=8), :] for side in range(2)],
                    axis=1,
                )
                for r in range(2)
            ],
            axis=0,
        )
        for field in range(2)
    ]
    def coefficient(i):
        return numbers[:HALF, i : i + 1]

    across, along = forward_z(z_from_ref, coefficient, arrived)
    waves = [x + z for x, z in zip(across, derivative_z(coefficient, 9, along))]
    scale = DIVERGENCE_LINK / MIDDLE_LINK / (NZ * NY)
    waves = filtered_rows(waves, y_ref, where[0] % HALF, scale)
    plane = inverse_z(z_to_ref, coefficient, [waves])
    early = first_half()
    for pair in range(4):
        for side in range(2):
            rows = slice(64 * pair, 64 * (pair + 1))
            even = plane[rows, HALF * side : HALF * (side + 1)]
            odd = plane[rows, NY + HALF * side : NY + HALF * (side + 1)]
            out[pl.ds(8 * side + pair, 64, stride=16), :] = jnp.where(
                early, even, pltpu.roll(odd, ROWS, 1)
            )
            out[pl.ds(8 * side + 4 + pair, 64, stride=16), :] = jnp.where(
                early, pltpu.roll(even, ROWS, 1), odd
            )


def new_pressure_kernel(data, x_ref, bulk, own, passed, out, held, semaphores):
    row = lax.broadcasted_iota(jnp.int32, (256, HALF), 0)
    weight = jnp.where((row & (HALF - 1)) == 0, 1.0, 2.0) * (X_SCALE / DIVERGENCE_LINK)
    components = [(data[pl.ds(i, 256, stride=4), :] * weight).T for i in range(4)]
    lines = right(jnp.concatenate(components, axis=0), x_ref).reshape(SLAB, ROWS, NX)
    sent = []
    for i in range(4):
        planes = pl.ds(2 * i, 2)
        held[planes] = own[planes] - bulk[planes] * lines[2 * i : 2 * i + 2]
        held[planes, :TILE] += passed[planes].astype(f32)
        sent.append(pltpu.make_async_copy(held.at[planes], out.at[planes], semaphores.at[i]))
        sent[i].start()
    for copy in sent:
        copy.wait()


def source_kernel(where, lives, c0, c1, c2, t0, t1, t2, pressure, own, passed, l0, l1, l2):
    blank = jnp.zeros((SLAB, 256, NX), bf16)
    l0[:SLAB] = blank
    l2[SLAB:] = blank
    corners = (c0, c1, c2)

    def place(slot, carry):
        rows = pl.ds(pl.multiple_of(slot * TILE, TILE), TILE)
        lane = lax.broadcasted_iota(jnp.int32, (HALF, NX), 1)
        line = lax.broadcasted_iota(jnp.int32, (HALF, NX), 0) & (TILE - 1)
        quarter = lax.broadcasted_iota(jnp.int32, (SLAB, 8, HALF), 2) // TILE
        for reach, (tiles, placed) in enumerate(((t0, l0), (t1, l1), (t2, l2))):
            offset = corners[reach][slot, 0] & (SLAB - 1)
            hot = ((lane - line - corners[reach][slot, 2]) & (NX - 1)) == 0
            hot = jnp.where(hot, 1.0, 0.0).astype(bf16)
            first = SLAB - offset if reach == 1 else 0
            to = 0 if reach == 1 else offset
            block = tiles[slot, pl.ds(first, SLAB)].astype(f32)
            block = jnp.stack([jnp.where(quarter == i, block, 0.0) for i in range(4)], axis=1)
            block = block.reshape(SLAB * TILE, HALF).astype(bf16)
            across = jnp.dot(block, hot, preferred_element_type=f32).astype(bf16)
            placed[pl.ds(to, SLAB), rows, :] = across.reshape(SLAB, TILE, NX)
        return carry

    lax.fori_loop(0, SLOTS_HERE, place, 0)
    line = lax.broadcasted_iota(jnp.int32, (ROWS + TILE, 256), 0)
    lane = lax.broadcasted_iota(jnp.int32, (ROWS + TILE, 256), 1)
    hots = []
    for reach in range(3):
        sender = ((where[0] + PEERS_Z - reach) % PEERS_Z) * PEERS_Y + where[1]
        start = jnp.full((ROWS + TILE, 256), -2 * TILE, jnp.int32)
        for slot in range(SLOTS_HERE):
            row = corners[reach][slot, 1] - where[1] * ROWS
            row = jnp.where(slot < lives[sender], row, -2 * NX)
            within = 4 * (lane & 7) + ((lane // 8) & 3)
            start = jnp.where(lane // TILE == slot, within + row, start)
        hots.append(jnp.where(line == start, 1.0, 0.0).astype(bf16))
    for z in range(SLAB):
        window = jnp.dot(hots[0], l0[z], preferred_element_type=f32)
        window += jnp.dot(hots[1], l1[z], preferred_element_type=f32)
        window += jnp.dot(hots[2], l2[SLAB + z], preferred_element_type=f32)
        own[z] = pressure[z] + window[:ROWS]
        passed[z] = window[ROWS:].astype(bf16)


VMEM = pl.BlockSpec(memory_space=pltpu.VMEM)
SMEM = pl.BlockSpec(memory_space=pltpu.SMEM)
FAR = pl.BlockSpec(memory_space=pltpu.HBM)


def call(kernel, name, specs, arrays, shapes, outs, scratch=(), semaphores=0, limit=20):
    scratch = [pltpu.VMEM(shape, kind) for shape, kind in scratch]
    if semaphores:
        scratch.append(pltpu.SemaphoreType.DMA((semaphores,)))
    return pl.pallas_call(
        kernel,
        out_shape=[jax.ShapeDtypeStruct(shape, kind) for shape, kind in shapes],
        in_specs=specs,
        out_specs=outs,
        scratch_shapes=scratch,
        compiler_params=pltpu.CompilerParams(vmem_limit_bytes=limit << 20),
        cost_estimate=pl.CostEstimate(flops=int(4e8), bytes_accessed=1 << 20, transcendentals=0),
        name=name,
    )(*arrays)


def from_behind(x, axis, by):
    peers = lax.axis_size(axis)
    return lax.ppermute(x, axis, [(i, (i + by) % peers) for i in range(peers)])


def to_rows(slopes, row_block):
    blocks = [
        lax.dynamic_slice_in_dim(slopes, ROWS * ((row_block + ahead) % PEERS_Y), ROWS, 2)
        for ahead in range(PEERS_Y)
    ]
    arrived = [blocks[0]] + [from_behind(blocks[ahead], "gy", ahead) for ahead in range(1, PEERS_Y)]
    ordered = [
        lax.select_n((row_block - device) % PEERS_Y, *arrived) for device in range(PEERS_Y)
    ]
    return jnp.concatenate(ordered, 1).astype(f32)


def exchange(columns, rows):
    blocks = columns.astype(f16).reshape(256, rows, HALF)
    return lax.all_to_all(blocks, ("gz", "gy"), 0, 0, tiled=True)


def arrived(moved):
    return moved.reshape(-1, HALF).astype(f32)


def local(pressure, velocity, bulk, buoyancy, tiles, tile_corner, live_count):
    slab_index = lax.axis_index("gz")
    row_block = lax.axis_index("gy")
    here = row_block.reshape(1).astype(jnp.int32)
    device = (slab_index * PEERS_Y + row_block).astype(jnp.int32)
    place = jnp.stack([slab_index, row_block]).astype(jnp.int32)
    table = {key: jnp.asarray(value) for key, value in TABLES.items()}

    components = jnp.einsum(
        "cx,abx->cab",
        table["x_lines"],
        pressure.reshape(4, HALF, NX),
        precision=lax.Precision.HIGH,
    )
    velocity_later, buoyancy_later, tiles, slab_later, components = lax.optimization_barrier(
        (velocity, buoyancy, tiles, slab_index, components)
    )
    fields = jnp.concatenate([velocity_later, buoyancy_later[None]])
    sent = [
        (
            lax.dynamic_slice_in_dim(fields, 2 * ((row_block + ahead) % PEERS_Y), 2, 1) * FIELD_LINK
        ).astype(f16)
        for ahead in range(1, PEERS_Y)
    ]
    own = lax.dynamic_slice_in_dim(fields, 2 * row_block, 2, 1) * FIELD_LINK
    first, third = from_behind(sent[0], "gy", 1), from_behind(sent[2], "gy", 3)
    packed = tiles.reshape(SLOTS_HERE, 2 * SLAB, 8, HALF)
    moved, second, packed, packed_end = lax.optimization_barrier(
        (exchange(components, 4), sent[1], packed, packed[:, SLAB:])
    )
    (filtered,) = call(
        filter_out_kernel,
        "filter_out",
        [SMEM] + [VMEM] * 3,
        [
            device.reshape(1),
            arrived(moved),
            table["filter_out"],
            table["numbers"],
        ],
        [((2048, HALF), f32)],
        [VMEM],
        [((NZ, NY), f32)],
    )
    filtered, own, first, second, third, packed, packed_end = lax.optimization_barrier(
        (filtered, own, first, second, third, packed, packed_end)
    )
    second = from_behind(second, "gy", 2)
    tiles_before, tiles_second = from_behind(packed, "gz", 1), from_behind(packed_end, "gz", 2)
    moved = exchange(filtered, 8)
    slopes, middle = call(
        middle_kernel,
        "middle",
        [SMEM] + [VMEM] * 3 + [FAR] * 2,
        [
            here,
            arrived(moved),
            table["middle"],
            table["numbers"],
            jnp.stack([own, first.astype(f32), third.astype(f32)]) * (1.0 / FIELD_LINK),
            second.astype(f32) * (1.0 / FIELD_LINK),
        ],
        [((3, 2, NY, NX), f32), ((2048, HALF), f32)],
        [FAR, VMEM],
        [((3, 2, NY, NX), f32), ((4, 2, NY, NX), f32)],
        5,
    )
    middle, slopes, tiles_before, tiles_second = lax.optimization_barrier(
        (middle, slopes.astype(f16), tiles_before, tiles_second)
    )
    slopes = to_rows(slopes, row_block)
    new_velocity = velocity - buoyancy[None] * (slopes * (1.0 / RETURN_LINK))
    corners = [
        lax.dynamic_slice_in_dim(
            tile_corner,
            ((slab_later - reach) % PEERS_Z * PEERS_Y + row_block) * SLOTS_HERE,
            SLOTS_HERE,
            0,
        )
        for reach in range(3)
    ]
    own, passed = call(
        source_kernel,
        "source",
        [SMEM] * 5 + [VMEM] * 4,
        [
            place,
            live_count,
            *corners,
            packed,
            tiles_before,
            tiles_second,
            pressure,
        ],
        [((SLAB, ROWS, NX), f32), ((SLAB, TILE, NX), bf16)],
        [VMEM] * 2,
        [((2 * SLAB, 256, NX), bf16), ((SLAB, 256, NX), bf16), ((2 * SLAB, 256, NX), bf16)],
    )
    (filtered_back,) = call(
        filter_back_kernel,
        "filter_back",
        [SMEM] + [VMEM] * 3,
        [
            device.reshape(1),
            arrived(exchange(middle, 8)),
            table["filter_back"],
            table["numbers"],
        ],
        [((1024, HALF), f32)],
        [VMEM],
    )
    passed = from_behind(passed, "gy", 1)
    filtered_back, own = lax.optimization_barrier((filtered_back, own))
    moved, new_velocity = lax.optimization_barrier((exchange(filtered_back, 4), new_velocity))
    (new_pressure,) = call(
        new_pressure_kernel,
        "new_pressure",
        [VMEM] * 5,
        [arrived(moved), table["x_waves"], bulk, own, passed],
        [((SLAB, ROWS, NX), f32)],
        [FAR],
        [((SLAB, ROWS, NX), f32)],
        4,
    )
    return (new_pressure, new_velocity)


def solution(mesh):
    in_specs = (
        P("gz", "gy", None),
        P(None, "gz", "gy", None),
        P("gz", "gy", None),
        P("gz", "gy", None),
        P(("gz", "gy"), None, None, None),
        P(),
        P(),
    )
    out_specs = (P("gz", "gy", None), P(None, "gz", "gy", None))
    return jax.shard_map(local, mesh=mesh, in_specs=in_specs, out_specs=out_specs, check_vma=False)
```

```python
import math

import jax
import jax.numpy as jnp
import ml_dtypes
import numpy as np
from jax import lax
from jax.experimental import pallas as pl
from jax.experimental.pallas import tpu as pltpu
from jax.sharding import PartitionSpec as P

NX = 256
NY = 256
NZ = 512
HALF = 128
ROWS = 64
SLAB = 8
SLOTS_HERE = 8
TILE = 32
PEERS_Y = 4
PEERS_Z = 64
kappa_courant = 0.3
f32 = jnp.float32
bf16 = jnp.bfloat16
f16 = jnp.float16

X_SCALE = 1.0 / 16.0
FIELD_LINK = 4096.0
COMPONENT_LINK = 256.0
SLOPE_LINK = 128.0
RETURN_LINK = 1024.0
MIDDLE_LINK = 16.0
DIVERGENCE_LINK = 8.0


def split_table(table):
    high = table.astype(ml_dtypes.bfloat16)
    low = (table - high.astype(np.float64)).astype(ml_dtypes.bfloat16)
    return high, low


def packed_table(table):
    return np.concatenate(split_table(table), axis=1)


def signed_waves(length):
    index = np.arange(length)
    return 2.0 * np.pi / length * np.where(index < length // 2, index, index - length)


def derivative_matrix(length, orientation):
    wave = signed_waves(length)
    kernel = np.fft.ifft(1j * wave * np.exp(orientation * 0.5j * wave)).real
    index = np.arange(length)
    return kernel[(index[:, None] - index[None, :]) % length]


def make_tables():
    index = np.arange(256)
    angle = 2.0 * np.pi / 256 * (np.outer(index, index) % 256)
    wave_x = 2.0 * np.pi / NX * np.arange(HALF)

    spectrum = np.exp(-1j * angle[:HALF])
    weight = np.where(np.arange(HALF) == 0, 1.0, 2.0)
    ahead = 1j * wave_x * np.exp(0.5j * wave_x)
    behind = 1j * wave_x * np.exp(-0.5j * wave_x)
    x_rows = np.zeros((8, HALF), np.float32)
    x_rows[0], x_rows[1], x_rows[2] = weight, (weight * ahead).real, (weight * ahead).imag
    forward_z = np.concatenate([np.cos(angle[:HALF]), -np.sin(angle[:HALF])], axis=0)
    forward_z[HALF] = np.cos(angle[HALF])
    inverse_z = 2.0 * forward_z.T
    inverse_z[:, 0] = forward_z[0]
    inverse_z[:, HALF] = forward_z[HALF]
    slab_order = (4 * np.arange(64)[None, :] + np.arange(4)[:, None]).reshape(-1)
    low = np.arange(HALF)
    high = low - 256
    coefficients = np.zeros((HALF, HALF), np.float32)
    coefficients[:, 0] = np.cos(2.0 * np.pi / NZ * low)
    coefficients[:, 1] = np.sin(2.0 * np.pi / NZ * low)

    def derivative(number, orientation):
        wave = 2.0 * np.pi / NZ * number
        return -orientation * wave * np.sin(0.5 * wave), wave * np.cos(0.5 * wave)

    coefficients[:, 16], coefficients[:, 17] = behind.real, behind.imag
    for first, orientation in ((2, 1.0), (9, -1.0)):
        middle_real, middle_imag = derivative(128, orientation)
        for at, number in ((first, low), (first + 3, high)):
            real, imag = derivative(number, orientation)
            coefficients[:, at] = real
            coefficients[:, at + 1] = np.where((low == 0), 0.0, imag)
            coefficients[:, at + 2] = np.where((low == 0), middle_real, real)
        coefficients[:, first + 6] = np.where((low == 0), middle_imag, 0.0)
    x_waves = packed_table(np.concatenate([spectrum.real, spectrum.imag], axis=0))
    y_waves = packed_table(np.cos(angle) + np.sin(angle))
    return {
        "x_waves": x_waves,
        "x_lines": (
            np.concatenate([spectrum.real, spectrum.imag], axis=0) * (X_SCALE * COMPONENT_LINK)
        ).astype(np.float32),
        "middle": np.concatenate(
            [
                x_waves,
                packed_table(derivative_matrix(NY, 1.0)),
                packed_table(derivative_matrix(NY, -1.0)),
            ],
            axis=1,
        ),
        "filter_out": np.concatenate(
            [y_waves, packed_table(forward_z[:, slab_order]), packed_table(inverse_z)], axis=1
        ),
        "filter_back": np.concatenate(
            [y_waves, packed_table(forward_z), packed_table(inverse_z[slab_order])], axis=1
        ),
        "numbers": np.concatenate([coefficients, x_rows], axis=0),
    }


TABLES = make_tables()


def pieces(x, axis):
    high = x.astype(bf16)
    low = (x - high.astype(f32)).astype(bf16)
    return jnp.concatenate([high, low, high], axis=axis)


def contract(a, b, a_dim, b_dim):
    return lax.dot_general(a, b, (((a_dim,), (b_dim,)), ((), ())), preferred_element_type=f32)


def wide(table):
    return jnp.concatenate([table[:, :256], table[:, :512]], axis=1)


def tall(table):
    return jnp.concatenate([table[:, :256], table[:, :256], table[:, 256:512]], axis=0)


def left(table_ref, x):
    return contract(wide(table_ref), pieces(x, 0), 1, 0)


def right(x, table_ref):
    return contract(pieces(x, 1), tall(table_ref), 1, 0)


def to_components(table_ref, lines):
    return contract(wide(table_ref), pieces(lines, 1), 1, 1)


class Fetch:
    def __init__(self, sources, targets, semaphores):
        self.targets = targets
        self.copies = [
            pltpu.make_async_copy(source, target, semaphores.at[i])
            for i, (source, target) in enumerate(zip(sources, targets))
        ]
        for copy in self.copies:
            copy.start()

    def __getitem__(self, i):
        if self.copies[i] is not None:
            self.copies[i].wait()
            self.copies[i] = None
        return self.targets[i]


def times(real, imag, factor_real, factor_imag):
    return real * factor_real - imag * factor_imag, real * factor_imag + imag * factor_real


def kappa_rows(kx, part):
    kz = lax.broadcasted_iota(jnp.int32, (HALF, NY), 0)
    ky = lax.broadcasted_iota(jnp.int32, (HALF, NY), 1)
    number = kz - 256 * (part // 2)
    if part % 2:
        number = jnp.where(kz == 0, 128, number)
    wave_z = number.astype(f32) * (2.0 * math.pi / NZ)
    wave_y = jnp.where(ky < NY // 2, ky, ky - NY).astype(f32) * (2.0 * math.pi / NY)
    wave_x = jnp.full((HALF, NY), kx, jnp.int32).astype(f32) * (2.0 * math.pi / NX)
    square = (kappa_courant / 2.0) ** 2 * (wave_x * wave_x + wave_z * wave_z + wave_y * wave_y)
    total = jnp.full((HALF, NY), 1.0 / math.factorial(15), f32)
    for order in range(6, -1, -1):
        total = 1.0 / math.factorial(2 * order + 1) - square * total
    return total


def forward_z(table_ref, coefficient, fields):
    sides = [side for field in fields for side in (field[:256], field[256:])]
    sums = left(table_ref, jnp.concatenate(sides, axis=1))
    cosine, sine = coefficient(0), coefficient(1)
    spectra = []
    for i in range(0, len(sides), 2):
        even = sums[:, NY * i : NY * (i + 1)]
        odd = sums[:, NY * (i + 1) : NY * (i + 2)]
        real = cosine * odd[:HALF] + sine * odd[HALF:]
        imag = cosine * odd[HALF:] - sine * odd[:HALF]
        spectra.append(
            [even[:HALF] + real, even[HALF:] + imag, even[:HALF] - real, even[HALF:] - imag]
        )
    return spectra


def inverse_z(table_ref, coefficient, spectra):
    cosine, sine = coefficient(0), coefficient(1)
    sides = []
    for a, b, c, d in spectra:
        real, imag = a - c, b - d
        sides.append(jnp.concatenate([a + c, b + d], axis=0))
        sides.append(jnp.concatenate([cosine * real - sine * imag, cosine * imag + sine * real], axis=0))
    return left(table_ref, jnp.concatenate(sides, axis=1))


def derivative_z(coefficient, first, spectrum):
    a, b, c, d = spectrum
    mixed = coefficient(first + 6)
    return [
        coefficient(first) * a - coefficient(first + 1) * b,
        coefficient(first + 2) * b + coefficient(first + 1) * a - mixed * d,
        coefficient(first + 3) * c - coefficient(first + 4) * d,
        coefficient(first + 5) * d + coefficient(first + 4) * c + mixed * b,
    ]


def blocks_of(x):
    return [x[HALF * i : HALF * (i + 1)] for i in range(4)]


def filtered_rows(blocks, y_ref, kx, scale):
    out = []
    for part, block in enumerate(blocks):
        waves = right(block, y_ref) * (kappa_rows(kx, part) * scale)
        out.append(right(waves, y_ref))
    return out


def first_half():
    return lax.broadcasted_iota(jnp.int32, (64, HALF), 1) < ROWS


def forward_lines_kernel(pressure, x_ref, out):
    components = to_components(x_ref, pressure[...].reshape(512, NX)) * (X_SCALE * COMPONENT_LINK)
    for i in range(4):
        out[pl.ds(i, 256, stride=4), :] = components[:, HALF * i : HALF * (i + 1)]


def filter_out_kernel(where, data, tables, numbers, out, plane):
    y_ref, z_from_ref, z_to_ref = (tables[:, 512 * i : 512 * (i + 1)] for i in range(3))
    early = first_half()
    for pair in range(4):
        for side in range(2):
            a = data[pl.ds(8 * side + pair, 64, stride=16), :]
            b = data[pl.ds(8 * side + 4 + pair, 64, stride=16), :]
            span = pl.ds(HALF * side, HALF)
            plane[pl.ds(64 * pair, 64), span] = jnp.where(early, a, pltpu.roll(b, ROWS, 1))
            plane[pl.ds(256 + 64 * pair, 64), span] = jnp.where(early, pltpu.roll(a, ROWS, 1), b)
    def coefficient(i):
        return numbers[:HALF, i : i + 1]

    (waves,) = forward_z(z_from_ref, coefficient, [plane[...]])
    waves = filtered_rows(waves, y_ref, where[0] % HALF, SLOPE_LINK / COMPONENT_LINK / (NZ * NY))
    planes = inverse_z(z_to_ref, coefficient, [waves, derivative_z(coefficient, 2, waves)])
    for field in range(2):
        for r in range(2):
            for side in range(2):
                start = NY * (2 * field + r) + HALF * side
                out[pl.ds(4 * r + 2 * field + side, 256, stride=8), :] = planes[
                    :, start : start + HALF
                ]


def middle_kernel(
    where, data, tables, numbers, near, second, slopes, out, held, fields, semaphores
):
    starts = [
        pl.ds(pl.multiple_of(((where[0] + PEERS_Y - back) % PEERS_Y) * ROWS, ROWS), ROWS)
        for back in range(PEERS_Y)
    ]
    fetch = Fetch(
        (near.at[0], near.at[1], second, near.at[2]),
        [fields.at[:, :, start] for start in starts],
        semaphores,
    )
    x_ref, ya_ref, yb_ref = (tables[:, 512 * i : 512 * (i + 1)] for i in range(3))
    weight, ahead_real, ahead_imag = (numbers[HALF + i : HALF + i + 1, :] for i in range(3))
    behind = numbers[:HALF, 16:17], numbers[:HALF, 17:18]
    q, g = [
        jnp.concatenate(
            [
                data[pl.ds(4 * r + 2 * field + side, 256, stride=8), :]
                for r in range(2)
                for side in range(2)
            ],
            axis=1,
        ).T
        for field in range(2)
    ]
    real, imag = q[:, :HALF], q[:, HALF:]
    scale = X_SCALE / SLOPE_LINK
    plain = right(jnp.concatenate([weight * real, weight * imag], axis=1), x_ref) * scale
    steep = jnp.concatenate(
        [ahead_real * real - ahead_imag * imag, ahead_real * imag + ahead_imag * real], axis=1
    )
    steep = right(steep, x_ref) * scale
    along_y = left(ya_ref, jnp.concatenate([plain[:256], plain[256:]], axis=1))
    along_z = jnp.concatenate([weight * g[:, :HALF], weight * g[:, HALF:]], axis=1)
    along_z = right(along_z, x_ref) * scale
    along = (
        (steep[:256], steep[256:]),
        (along_y[:, :NX], along_y[:, NX:]),
        (along_z[:256], along_z[256:]),
    )
    for d in range(3):
        for r in range(2):
            held[d, r] = along[d][r] * RETURN_LINK
    returned = pltpu.make_async_copy(held, slopes, semaphores.at[4])
    returned.start()
    for i in range(4):
        fetch[i]
    moved = [[fields[d, r] - fields[3, r] * along[d][r] for r in range(2)] for d in range(3)]
    along_y = left(yb_ref, jnp.concatenate(moved[1], axis=1))
    scale = X_SCALE * MIDDLE_LINK
    steep, along_z, along_y = [
        to_components(x_ref, jnp.concatenate(lines, axis=0)) * scale
        for lines in (moved[0], moved[2], (along_y[:, :NX], along_y[:, NX:]))
    ]
    across = jnp.concatenate(times(steep[:HALF], steep[HALF:], behind[0], behind[1]), axis=0)
    for field, part in enumerate((across + along_y, along_z)):
        for r in range(2):
            for side in range(2):
                out[pl.ds(4 * r + 2 * field + side, 256, stride=8), :] = part[
                    :, NY * r + HALF * side : NY * r + HALF * (side + 1)
                ]
    returned.wait()


def filter_back_kernel(where, data, tables, numbers, out):
    y_ref, z_from_ref, z_to_ref = (tables[:, 512 * i : 512 * (i + 1)] for i in range(3))
    arrived = [
        jnp.concatenate(
            [
                jnp.concatenate(
                    [data[pl.ds(4 * r + 2 * field + side, 256, stride=8), :] for side in range(2)],
                    axis=1,
                )
                for r in range(2)
            ],
            axis=0,
        )
        for field in range(2)
    ]
    def coefficient(i):
        return numbers[:HALF, i : i + 1]

    across, along = forward_z(z_from_ref, coefficient, arrived)
    waves = [x + z for x, z in zip(across, derivative_z(coefficient, 9, along))]
    scale = DIVERGENCE_LINK / MIDDLE_LINK / (NZ * NY)
    waves = filtered_rows(waves, y_ref, where[0] % HALF, scale)
    plane = inverse_z(z_to_ref, coefficient, [waves])
    early = first_half()
    for pair in range(4):
        for side in range(2):
            rows = slice(64 * pair, 64 * (pair + 1))
            even = plane[rows, HALF * side : HALF * (side + 1)]
            odd = plane[rows, NY + HALF * side : NY + HALF * (side + 1)]
            out[pl.ds(8 * side + pair, 64, stride=16), :] = jnp.where(
                early, even, pltpu.roll(odd, ROWS, 1)
            )
            out[pl.ds(8 * side + 4 + pair, 64, stride=16), :] = jnp.where(
                early, pltpu.roll(even, ROWS, 1), odd
            )


def new_pressure_kernel(data, x_ref, bulk, own, passed, out, held, semaphores):
    row = lax.broadcasted_iota(jnp.int32, (256, HALF), 0)
    weight = jnp.where((row & (HALF - 1)) == 0, 1.0, 2.0) * (X_SCALE / DIVERGENCE_LINK)
    components = [(data[pl.ds(i, 256, stride=4), :] * weight).T for i in range(4)]
    lines = right(jnp.concatenate(components, axis=0), x_ref).reshape(SLAB, ROWS, NX)
    sent = []
    for i in range(4):
        planes = pl.ds(2 * i, 2)
        held[planes] = own[planes] - bulk[planes] * lines[2 * i : 2 * i + 2]
        held[planes, :TILE] += passed[planes].astype(f32)
        sent.append(pltpu.make_async_copy(held.at[planes], out.at[planes], semaphores.at[i]))
        sent[i].start()
    for copy in sent:
        copy.wait()


def source_kernel(where, lives, c0, c1, c2, t0, t1, t2, pressure, own, passed, l0, l1, l2):
    blank = jnp.zeros((SLAB, 256, NX), bf16)
    l0[:SLAB] = blank
    l2[SLAB:] = blank
    corners = (c0, c1, c2)

    def place(slot, carry):
        rows = pl.ds(pl.multiple_of(slot * TILE, TILE), TILE)
        lane = lax.broadcasted_iota(jnp.int32, (HALF, NX), 1)
        line = lax.broadcasted_iota(jnp.int32, (HALF, NX), 0) & (TILE - 1)
        quarter = lax.broadcasted_iota(jnp.int32, (SLAB, 8, HALF), 2) // TILE
        for reach, (tiles, placed) in enumerate(((t0, l0), (t1, l1), (t2, l2))):
            offset = corners[reach][slot, 0] & (SLAB - 1)
            hot = ((lane - line - corners[reach][slot, 2]) & (NX - 1)) == 0
            hot = jnp.where(hot, 1.0, 0.0).astype(bf16)
            first = SLAB - offset if reach == 1 else 0
            to = 0 if reach == 1 else offset
            block = tiles[slot, pl.ds(first, SLAB)].astype(f32)
            block = jnp.stack([jnp.where(quarter == i, block, 0.0) for i in range(4)], axis=1)
            block = block.reshape(SLAB * TILE, HALF).astype(bf16)
            across = jnp.dot(block, hot, preferred_element_type=f32).astype(bf16)
            placed[pl.ds(to, SLAB), rows, :] = across.reshape(SLAB, TILE, NX)
        return carry

    lax.fori_loop(0, SLOTS_HERE, place, 0)
    line = lax.broadcasted_iota(jnp.int32, (ROWS + TILE, 256), 0)
    lane = lax.broadcasted_iota(jnp.int32, (ROWS + TILE, 256), 1)
    hots = []
    for reach in range(3):
        sender = ((where[0] + PEERS_Z - reach) % PEERS_Z) * PEERS_Y + where[1]
        start = jnp.full((ROWS + TILE, 256), -2 * TILE, jnp.int32)
        for slot in range(SLOTS_HERE):
            row = corners[reach][slot, 1] - where[1] * ROWS
            row = jnp.where(slot < lives[sender], row, -2 * NX)
            within = 4 * (lane & 7) + ((lane // 8) & 3)
            start = jnp.where(lane // TILE == slot, within + row, start)
        hots.append(jnp.where(line == start, 1.0, 0.0).astype(bf16))
    for z in range(SLAB):
        window = jnp.dot(hots[0], l0[z], preferred_element_type=f32)
        window += jnp.dot(hots[1], l1[z], preferred_element_type=f32)
        window += jnp.dot(hots[2], l2[SLAB + z], preferred_element_type=f32)
        own[z] = pressure[z] + window[:ROWS]
        passed[z] = window[ROWS:].astype(bf16)


VMEM = pl.BlockSpec(memory_space=pltpu.VMEM)
SMEM = pl.BlockSpec(memory_space=pltpu.SMEM)
FAR = pl.BlockSpec(memory_space=pltpu.HBM)


def call(kernel, name, specs, arrays, shapes, outs, scratch=(), semaphores=0, limit=20):
    scratch = [pltpu.VMEM(shape, kind) for shape, kind in scratch]
    if semaphores:
        scratch.append(pltpu.SemaphoreType.DMA((semaphores,)))
    return pl.pallas_call(
        kernel,
        out_shape=[jax.ShapeDtypeStruct(shape, kind) for shape, kind in shapes],
        in_specs=specs,
        out_specs=outs,
        scratch_shapes=scratch,
        compiler_params=pltpu.CompilerParams(vmem_limit_bytes=limit << 20),
        cost_estimate=pl.CostEstimate(flops=int(4e8), bytes_accessed=1 << 20, transcendentals=0),
        name=name,
    )(*arrays)


def from_behind(x, axis, by):
    peers = lax.axis_size(axis)
    return lax.ppermute(x, axis, [(i, (i + by) % peers) for i in range(peers)])


def to_rows(slopes, row_block):
    blocks = [
        lax.dynamic_slice_in_dim(slopes, ROWS * ((row_block + ahead) % PEERS_Y), ROWS, 2)
        for ahead in range(PEERS_Y)
    ]
    arrived = [blocks[0]] + [from_behind(blocks[ahead], "gy", ahead) for ahead in range(1, PEERS_Y)]
    ordered = [
        lax.select_n((row_block - device) % PEERS_Y, *arrived) for device in range(PEERS_Y)
    ]
    return jnp.concatenate(ordered, 1).astype(f32)


def exchange(columns, rows):
    blocks = columns.astype(f16).reshape(256, rows, HALF)
    return lax.all_to_all(blocks, ("gz", "gy"), 0, 0, tiled=True)


def arrived(moved):
    return moved.reshape(-1, HALF).astype(f32)


def local(pressure, velocity, bulk, buoyancy, tiles, tile_corner, live_count):
    slab_index = lax.axis_index("gz")
    row_block = lax.axis_index("gy")
    here = row_block.reshape(1).astype(jnp.int32)
    device = (slab_index * PEERS_Y + row_block).astype(jnp.int32)
    place = jnp.stack([slab_index, row_block]).astype(jnp.int32)
    table = {key: jnp.asarray(value) for key, value in TABLES.items()}

    components = jnp.einsum(
        "cx,abx->cab",
        table["x_lines"],
        pressure.reshape(4, HALF, NX),
        precision=lax.Precision.HIGH,
    )
    velocity_later, buoyancy_later, tiles, slab_later, components = lax.optimization_barrier(
        (velocity, buoyancy, tiles, slab_index, components)
    )
    fields = jnp.concatenate([velocity_later, buoyancy_later[None]])
    sent = [
        (
            lax.dynamic_slice_in_dim(fields, 2 * ((row_block + ahead) % PEERS_Y), 2, 1) * FIELD_LINK
        ).astype(f16)
        for ahead in range(1, PEERS_Y)
    ]
    own = lax.dynamic_slice_in_dim(fields, 2 * row_block, 2, 1) * FIELD_LINK
    first, third = from_behind(sent[0], "gy", 1), from_behind(sent[2], "gy", 3)
    packed = tiles.reshape(SLOTS_HERE, 2 * SLAB, 8, HALF)
    moved, second, packed, packed_end = lax.optimization_barrier(
        (exchange(components, 4), sent[1], packed, packed[:, SLAB:])
    )
    (filtered,) = call(
        filter_out_kernel,
        "filter_out",
        [SMEM] + [VMEM] * 3,
        [
            device.reshape(1),
            arrived(moved),
            table["filter_out"],
            table["numbers"],
        ],
        [((2048, HALF), f32)],
        [VMEM],
        [((NZ, NY), f32)],
    )
    filtered, own, first, second, third, packed, packed_end = lax.optimization_barrier(
        (filtered, own, first, second, third, packed, packed_end)
    )
    second = from_behind(second, "gy", 2)
    tiles_before, tiles_second = from_behind(packed, "gz", 1), from_behind(packed_end, "gz", 2)
    moved = exchange(filtered, 8)
    slopes, middle = call(
        middle_kernel,
        "middle",
        [SMEM] + [VMEM] * 3 + [FAR] * 2,
        [
            here,
            arrived(moved),
            table["middle"],
            table["numbers"],
            jnp.stack([own, first.astype(f32), third.astype(f32)]) * (1.0 / FIELD_LINK),
            second.astype(f32) * (1.0 / FIELD_LINK),
        ],
        [((3, 2, NY, NX), f32), ((2048, HALF), f32)],
        [FAR, VMEM],
        [((3, 2, NY, NX), f32), ((4, 2, NY, NX), f32)],
        5,
    )
    middle, slopes, tiles_before, tiles_second = lax.optimization_barrier(
        (middle, slopes.astype(f16), tiles_before, tiles_second)
    )
    slopes = to_rows(slopes, row_block)
    new_velocity = (velocity * RETURN_LINK - buoyancy[None] * slopes) * (1.0 / RETURN_LINK)
    corners = [
        lax.dynamic_slice_in_dim(
            tile_corner,
            ((slab_later - reach) % PEERS_Z * PEERS_Y + row_block) * SLOTS_HERE,
            SLOTS_HERE,
            0,
        )
        for reach in range(3)
    ]
    own, passed = call(
        source_kernel,
        "source",
        [SMEM] * 5 + [VMEM] * 4,
        [
            place,
            live_count,
            *corners,
            packed,
            tiles_before,
            tiles_second,
            pressure,
        ],
        [((SLAB, ROWS, NX), f32), ((SLAB, TILE, NX), bf16)],
        [VMEM] * 2,
        [((2 * SLAB, 256, NX), bf16), ((SLAB, 256, NX), bf16), ((2 * SLAB, 256, NX), bf16)],
    )
    (filtered_back,) = call(
        filter_back_kernel,
        "filter_back",
        [SMEM] + [VMEM] * 3,
        [
            device.reshape(1),
            arrived(exchange(middle, 8)),
            table["filter_back"],
            table["numbers"],
        ],
        [((1024, HALF), f32)],
        [VMEM],
    )
    passed = from_behind(passed, "gy", 1)
    filtered_back, own = lax.optimization_barrier((filtered_back, own))
    moved, new_velocity = lax.optimization_barrier((exchange(filtered_back, 4), new_velocity))
    (new_pressure,) = call(
        new_pressure_kernel,
        "new_pressure",
        [VMEM] * 5,
        [arrived(moved), table["x_waves"], bulk, own, passed],
        [((SLAB, ROWS, NX), f32)],
        [FAR],
        [((SLAB, ROWS, NX), f32)],
        4,
    )
    return (new_pressure, new_velocity)


def solution(mesh):
    in_specs = (
        P("gz", "gy", None),
        P(None, "gz", "gy", None),
        P("gz", "gy", None),
        P("gz", "gy", None),
        P(("gz", "gy"), None, None, None),
        P(),
        P(),
    )
    out_specs = (P("gz", "gy", None), P(None, "gz", "gy", None))
    return jax.shard_map(local, mesh=mesh, in_specs=in_specs, out_specs=out_specs, check_vma=False)
```

```python
import math

import jax
import jax.numpy as jnp
import ml_dtypes
import numpy as np
from jax import lax
from jax.experimental import pallas as pl
from jax.experimental.pallas import tpu as pltpu
from jax.sharding import PartitionSpec as P

NX = 256
NY = 256
NZ = 512
HALF = 128
ROWS = 64
SLAB = 8
SLOTS_HERE = 8
TILE = 32
PEERS_Y = 4
PEERS_Z = 64
kappa_courant = 0.3
f32 = jnp.float32
bf16 = jnp.bfloat16
f16 = jnp.float16

X_SCALE = 1.0 / 16.0
FIELD_LINK = 4096.0
COMPONENT_LINK = 256.0
SLOPE_LINK = 128.0
RETURN_LINK = 1024.0
MIDDLE_LINK = 16.0
DIVERGENCE_LINK = 8.0


def split_table(table):
    high = table.astype(ml_dtypes.bfloat16)
    low = (table - high.astype(np.float64)).astype(ml_dtypes.bfloat16)
    return high, low


def packed_table(table):
    return np.concatenate(split_table(table), axis=1)


def signed_waves(length):
    index = np.arange(length)
    return 2.0 * np.pi / length * np.where(index < length // 2, index, index - length)


def derivative_matrix(length, orientation):
    wave = signed_waves(length)
    kernel = np.fft.ifft(1j * wave * np.exp(orientation * 0.5j * wave)).real
    index = np.arange(length)
    return kernel[(index[:, None] - index[None, :]) % length]


def make_tables():
    index = np.arange(256)
    angle = 2.0 * np.pi / 256 * (np.outer(index, index) % 256)
    wave_x = 2.0 * np.pi / NX * np.arange(HALF)

    spectrum = np.exp(-1j * angle[:HALF])
    weight = np.where(np.arange(HALF) == 0, 1.0, 2.0)
    ahead = 1j * wave_x * np.exp(0.5j * wave_x)
    behind = 1j * wave_x * np.exp(-0.5j * wave_x)
    x_rows = np.zeros((8, HALF), np.float32)
    x_rows[0], x_rows[1], x_rows[2] = weight, (weight * ahead).real, (weight * ahead).imag
    forward_z = np.concatenate([np.cos(angle[:HALF]), -np.sin(angle[:HALF])], axis=0)
    forward_z[HALF] = np.cos(angle[HALF])
    inverse_z = 2.0 * forward_z.T
    inverse_z[:, 0] = forward_z[0]
    inverse_z[:, HALF] = forward_z[HALF]
    slab_order = (4 * np.arange(64)[None, :] + np.arange(4)[:, None]).reshape(-1)
    low = np.arange(HALF)
    high = low - 256
    coefficients = np.zeros((HALF, HALF), np.float32)
    coefficients[:, 0] = np.cos(2.0 * np.pi / NZ * low)
    coefficients[:, 1] = np.sin(2.0 * np.pi / NZ * low)

    def derivative(number, orientation):
        wave = 2.0 * np.pi / NZ * number
        return -orientation * wave * np.sin(0.5 * wave), wave * np.cos(0.5 * wave)

    coefficients[:, 16], coefficients[:, 17] = behind.real, behind.imag
    for first, orientation in ((2, 1.0), (9, -1.0)):
        middle_real, middle_imag = derivative(128, orientation)
        for at, number in ((first, low), (first + 3, high)):
            real, imag = derivative(number, orientation)
            coefficients[:, at] = real
            coefficients[:, at + 1] = np.where((low == 0), 0.0, imag)
            coefficients[:, at + 2] = np.where((low == 0), middle_real, real)
        coefficients[:, first + 6] = np.where((low == 0), middle_imag, 0.0)
    x_waves = packed_table(np.concatenate([spectrum.real, spectrum.imag], axis=0))
    y_waves = packed_table(np.cos(angle) + np.sin(angle))
    return {
        "x_waves": x_waves,
        "x_lines": (
            np.concatenate([spectrum.real, spectrum.imag], axis=0) * (X_SCALE * COMPONENT_LINK)
        ).astype(np.float32),
        "middle": np.concatenate(
            [
                x_waves,
                packed_table(derivative_matrix(NY, 1.0)),
                packed_table(derivative_matrix(NY, -1.0)),
            ],
            axis=1,
        ),
        "filter_out": np.concatenate(
            [y_waves, packed_table(forward_z[:, slab_order]), packed_table(inverse_z)], axis=1
        ),
        "filter_back": np.concatenate(
            [y_waves, packed_table(forward_z), packed_table(inverse_z[slab_order])], axis=1
        ),
        "numbers": np.concatenate([coefficients, x_rows], axis=0),
    }


TABLES = make_tables()


def pieces(x, axis):
    high = x.astype(bf16)
    low = (x - high.astype(f32)).astype(bf16)
    return jnp.concatenate([high, low, high], axis=axis)


def contract(a, b, a_dim, b_dim):
    return lax.dot_general(a, b, (((a_dim,), (b_dim,)), ((), ())), preferred_element_type=f32)


def wide(table):
    return jnp.concatenate([table[:, :256], table[:, :512]], axis=1)


def tall(table):
    return jnp.concatenate([table[:, :256], table[:, :256], table[:, 256:512]], axis=0)


def left(table_ref, x):
    return contract(wide(table_ref), pieces(x, 0), 1, 0)


def right(x, table_ref):
    return contract(pieces(x, 1), tall(table_ref), 1, 0)


def to_components(table_ref, lines):
    return contract(wide(table_ref), pieces(lines, 1), 1, 1)


class Fetch:
    def __init__(self, sources, targets, semaphores):
        self.targets = targets
        self.copies = [
            pltpu.make_async_copy(source, target, semaphores.at[i])
            for i, (source, target) in enumerate(zip(sources, targets))
        ]
        for copy in self.copies:
            copy.start()

    def __getitem__(self, i):
        if self.copies[i] is not None:
            self.copies[i].wait()
            self.copies[i] = None
        return self.targets[i]


def times(real, imag, factor_real, factor_imag):
    return real * factor_real - imag * factor_imag, real * factor_imag + imag * factor_real


def kappa_rows(kx, part):
    kz = lax.broadcasted_iota(jnp.int32, (HALF, NY), 0)
    ky = lax.broadcasted_iota(jnp.int32, (HALF, NY), 1)
    number = kz - 256 * (part // 2)
    if part % 2:
        number = jnp.where(kz == 0, 128, number)
    wave_z = number.astype(f32) * (2.0 * math.pi / NZ)
    wave_y = jnp.where(ky < NY // 2, ky, ky - NY).astype(f32) * (2.0 * math.pi / NY)
    wave_x = jnp.full((HALF, NY), kx, jnp.int32).astype(f32) * (2.0 * math.pi / NX)
    square = (kappa_courant / 2.0) ** 2 * (wave_x * wave_x + wave_z * wave_z + wave_y * wave_y)
    total = jnp.full((HALF, NY), 1.0 / math.factorial(15), f32)
    for order in range(6, -1, -1):
        total = 1.0 / math.factorial(2 * order + 1) - square * total
    return total


def forward_z(table_ref, coefficient, fields):
    sides = [side for field in fields for side in (field[:256], field[256:])]
    sums = left(table_ref, jnp.concatenate(sides, axis=1))
    cosine, sine = coefficient(0), coefficient(1)
    spectra = []
    for i in range(0, len(sides), 2):
        even = sums[:, NY * i : NY * (i + 1)]
        odd = sums[:, NY * (i + 1) : NY * (i + 2)]
        real = cosine * odd[:HALF] + sine * odd[HALF:]
        imag = cosine * odd[HALF:] - sine * odd[:HALF]
        spectra.append(
            [even[:HALF] + real, even[HALF:] + imag, even[:HALF] - real, even[HALF:] - imag]
        )
    return spectra


def inverse_z(table_ref, coefficient, spectra):
    cosine, sine = coefficient(0), coefficient(1)
    sides = []
    for a, b, c, d in spectra:
        real, imag = a - c, b - d
        sides.append(jnp.concatenate([a + c, b + d], axis=0))
        sides.append(jnp.concatenate([cosine * real - sine * imag, cosine * imag + sine * real], axis=0))
    return left(table_ref, jnp.concatenate(sides, axis=1))


def derivative_z(coefficient, first, spectrum):
    a, b, c, d = spectrum
    mixed = coefficient(first + 6)
    return [
        coefficient(first) * a - coefficient(first + 1) * b,
        coefficient(first + 2) * b + coefficient(first + 1) * a - mixed * d,
        coefficient(first + 3) * c - coefficient(first + 4) * d,
        coefficient(first + 5) * d + coefficient(first + 4) * c + mixed * b,
    ]


def blocks_of(x):
    return [x[HALF * i : HALF * (i + 1)] for i in range(4)]


def filtered_rows(blocks, y_ref, kx, scale):
    out = []
    for part, block in enumerate(blocks):
        waves = right(block, y_ref) * (kappa_rows(kx, part) * scale)
        out.append(right(waves, y_ref))
    return out


def first_half():
    return lax.broadcasted_iota(jnp.int32, (64, HALF), 1) < ROWS


def forward_lines_kernel(pressure, x_ref, out):
    components = to_components(x_ref, pressure[...].reshape(512, NX)) * (X_SCALE * COMPONENT_LINK)
    for i in range(4):
        out[pl.ds(i, 256, stride=4), :] = components[:, HALF * i : HALF * (i + 1)]


def filter_out_kernel(where, data, tables, numbers, out, plane):
    y_ref, z_from_ref, z_to_ref = (tables[:, 512 * i : 512 * (i + 1)] for i in range(3))
    early = first_half()
    for pair in range(4):
        for side in range(2):
            a = data[pl.ds(8 * side + pair, 64, stride=16), :]
            b = data[pl.ds(8 * side + 4 + pair, 64, stride=16), :]
            span = pl.ds(HALF * side, HALF)
            plane[pl.ds(64 * pair, 64), span] = jnp.where(early, a, pltpu.roll(b, ROWS, 1))
            plane[pl.ds(256 + 64 * pair, 64), span] = jnp.where(early, pltpu.roll(a, ROWS, 1), b)
    def coefficient(i):
        return numbers[:HALF, i : i + 1]

    (waves,) = forward_z(z_from_ref, coefficient, [plane[...]])
    waves = filtered_rows(waves, y_ref, where[0] % HALF, SLOPE_LINK / COMPONENT_LINK / (NZ * NY))
    planes = inverse_z(z_to_ref, coefficient, [waves, derivative_z(coefficient, 2, waves)])
    for field in range(2):
        for r in range(2):
            for side in range(2):
                start = NY * (2 * field + r) + HALF * side
                out[pl.ds(4 * r + 2 * field + side, 256, stride=8), :] = planes[
                    :, start : start + HALF
                ]


def middle_kernel(
    where, data, tables, numbers, near, second, slopes, out, held, fields, semaphores
):
    starts = [
        pl.ds(pl.multiple_of(((where[0] + PEERS_Y - back) % PEERS_Y) * ROWS, ROWS), ROWS)
        for back in range(PEERS_Y)
    ]
    fetch = Fetch(
        (near.at[0], near.at[1], second, near.at[2]),
        [fields.at[:, :, start] for start in starts],
        semaphores,
    )
    x_ref, ya_ref, yb_ref = (tables[:, 512 * i : 512 * (i + 1)] for i in range(3))
    weight, ahead_real, ahead_imag = (numbers[HALF + i : HALF + i + 1, :] for i in range(3))
    behind = numbers[:HALF, 16:17], numbers[:HALF, 17:18]
    q, g = [
        jnp.concatenate(
            [
                data[pl.ds(4 * r + 2 * field + side, 256, stride=8), :]
                for r in range(2)
                for side in range(2)
            ],
            axis=1,
        ).T
        for field in range(2)
    ]
    real, imag = q[:, :HALF], q[:, HALF:]
    scale = X_SCALE / SLOPE_LINK
    plain = right(jnp.concatenate([weight * real, weight * imag], axis=1), x_ref) * scale
    steep = jnp.concatenate(
        [ahead_real * real - ahead_imag * imag, ahead_real * imag + ahead_imag * real], axis=1
    )
    steep = right(steep, x_ref) * scale
    along_y = left(ya_ref, jnp.concatenate([plain[:256], plain[256:]], axis=1))
    along_z = jnp.concatenate([weight * g[:, :HALF], weight * g[:, HALF:]], axis=1)
    along_z = right(along_z, x_ref) * scale
    along = (
        (steep[:256], steep[256:]),
        (along_y[:, :NX], along_y[:, NX:]),
        (along_z[:256], along_z[256:]),
    )
    for d in range(3):
        for r in range(2):
            held[d, r] = along[d][r] * RETURN_LINK
    returned = pltpu.make_async_copy(held, slopes, semaphores.at[4])
    returned.start()
    for i in range(4):
        fetch[i]
    moved = [[fields[d, r] - fields[3, r] * along[d][r] for r in range(2)] for d in range(3)]
    along_y = left(yb_ref, jnp.concatenate(moved[1], axis=1))
    scale = X_SCALE * MIDDLE_LINK
    steep, along_z, along_y = [
        to_components(x_ref, jnp.concatenate(lines, axis=0)) * scale
        for lines in (moved[0], moved[2], (along_y[:, :NX], along_y[:, NX:]))
    ]
    across = jnp.concatenate(times(steep[:HALF], steep[HALF:], behind[0], behind[1]), axis=0)
    for field, part in enumerate((across + along_y, along_z)):
        for r in range(2):
            for side in range(2):
                out[pl.ds(4 * r + 2 * field + side, 256, stride=8), :] = part[
                    :, NY * r + HALF * side : NY * r + HALF * (side + 1)
                ]
    returned.wait()


def filter_back_kernel(where, data, tables, numbers, out):
    y_ref, z_from_ref, z_to_ref = (tables[:, 512 * i : 512 * (i + 1)] for i in range(3))
    arrived = [
        jnp.concatenate(
            [
                jnp.concatenate(
                    [data[pl.ds(4 * r + 2 * field + side, 256, stride=8), :] for side in range(2)],
                    axis=1,
                )
                for r in range(2)
            ],
            axis=0,
        )
        for field in range(2)
    ]
    def coefficient(i):
        return numbers[:HALF, i : i + 1]

    across, along = forward_z(z_from_ref, coefficient, arrived)
    waves = [x + z for x, z in zip(across, derivative_z(coefficient, 9, along))]
    scale = DIVERGENCE_LINK / MIDDLE_LINK / (NZ * NY)
    waves = filtered_rows(waves, y_ref, where[0] % HALF, scale)
    plane = inverse_z(z_to_ref, coefficient, [waves])
    early = first_half()
    for pair in range(4):
        for side in range(2):
            rows = slice(64 * pair, 64 * (pair + 1))
            even = plane[rows, HALF * side : HALF * (side + 1)]
            odd = plane[rows, NY + HALF * side : NY + HALF * (side + 1)]
            out[pl.ds(8 * side + pair, 64, stride=16), :] = jnp.where(
                early, even, pltpu.roll(odd, ROWS, 1)
            )
            out[pl.ds(8 * side + 4 + pair, 64, stride=16), :] = jnp.where(
                early, pltpu.roll(even, ROWS, 1), odd
            )


def new_pressure_kernel(data, x_ref, bulk, own, passed, out, held, semaphores):
    row = lax.broadcasted_iota(jnp.int32, (256, HALF), 0)
    weight = jnp.where((row & (HALF - 1)) == 0, 1.0, 2.0) * (X_SCALE / DIVERGENCE_LINK)
    components = [(data[pl.ds(i, 256, stride=4), :] * weight).T for i in range(4)]
    lines = right(jnp.concatenate(components, axis=0), x_ref).reshape(SLAB, ROWS, NX)
    sent = []
    for i in range(4):
        planes = pl.ds(2 * i, 2)
        held[planes] = own[planes] - bulk[planes] * lines[2 * i : 2 * i + 2]
        held[planes, :TILE] += passed[planes].astype(f32)
        sent.append(pltpu.make_async_copy(held.at[planes], out.at[planes], semaphores.at[i]))
        sent[i].start()
    for copy in sent:
        copy.wait()


def source_kernel(where, lives, c0, c1, c2, t0, t1, t2, pressure, own, passed, l0, l1, l2):
    blank = jnp.zeros((SLAB, 256, NX), bf16)
    l0[:SLAB] = blank
    l2[SLAB:] = blank
    corners = (c0, c1, c2)

    def place(slot, carry):
        rows = pl.ds(pl.multiple_of(slot * TILE, TILE), TILE)
        lane = lax.broadcasted_iota(jnp.int32, (HALF, NX), 1)
        line = lax.broadcasted_iota(jnp.int32, (HALF, NX), 0) & (TILE - 1)
        quarter = lax.broadcasted_iota(jnp.int32, (SLAB, 8, HALF), 2) // TILE
        for reach, (tiles, placed) in enumerate(((t0, l0), (t1, l1), (t2, l2))):
            offset = corners[reach][slot, 0] & (SLAB - 1)
            hot = ((lane - line - corners[reach][slot, 2]) & (NX - 1)) == 0
            hot = jnp.where(hot, 1.0, 0.0).astype(bf16)
            first = SLAB - offset if reach == 1 else 0
            to = 0 if reach == 1 else offset
            block = tiles[slot, pl.ds(first, SLAB)].astype(f32)
            block = jnp.stack([jnp.where(quarter == i, block, 0.0) for i in range(4)], axis=1)
            block = block.reshape(SLAB * TILE, HALF).astype(bf16)
            across = jnp.dot(block, hot, preferred_element_type=f32).astype(bf16)
            placed[pl.ds(to, SLAB), rows, :] = across.reshape(SLAB, TILE, NX)
        return carry

    lax.fori_loop(0, SLOTS_HERE, place, 0)
    line = lax.broadcasted_iota(jnp.int32, (ROWS + TILE, 256), 0)
    lane = lax.broadcasted_iota(jnp.int32, (ROWS + TILE, 256), 1)
    hots = []
    for reach in range(3):
        sender = ((where[0] + PEERS_Z - reach) % PEERS_Z) * PEERS_Y + where[1]
        start = jnp.full((ROWS + TILE, 256), -2 * TILE, jnp.int32)
        for slot in range(SLOTS_HERE):
            row = corners[reach][slot, 1] - where[1] * ROWS
            row = jnp.where(slot < lives[sender], row, -2 * NX)
            within = 4 * (lane & 7) + ((lane // 8) & 3)
            start = jnp.where(lane // TILE == slot, within + row, start)
        hots.append(jnp.where(line == start, 1.0, 0.0).astype(bf16))
    for z in range(SLAB):
        window = jnp.dot(hots[0], l0[z], preferred_element_type=f32)
        window += jnp.dot(hots[1], l1[z], preferred_element_type=f32)
        window += jnp.dot(hots[2], l2[SLAB + z], preferred_element_type=f32)
        own[z] = pressure[z] + window[:ROWS]
        passed[z] = window[ROWS:].astype(bf16)


VMEM = pl.BlockSpec(memory_space=pltpu.VMEM)
SMEM = pl.BlockSpec(memory_space=pltpu.SMEM)
FAR = pl.BlockSpec(memory_space=pltpu.HBM)


def call(kernel, name, specs, arrays, shapes, outs, scratch=(), semaphores=0, limit=20):
    scratch = [pltpu.VMEM(shape, kind) for shape, kind in scratch]
    if semaphores:
        scratch.append(pltpu.SemaphoreType.DMA((semaphores,)))
    return pl.pallas_call(
        kernel,
        out_shape=[jax.ShapeDtypeStruct(shape, kind) for shape, kind in shapes],
        in_specs=specs,
        out_specs=outs,
        scratch_shapes=scratch,
        compiler_params=pltpu.CompilerParams(vmem_limit_bytes=limit << 20),
        cost_estimate=pl.CostEstimate(flops=int(4e8), bytes_accessed=1 << 20, transcendentals=0),
        name=name,
    )(*arrays)


def from_behind(x, axis, by):
    peers = lax.axis_size(axis)
    return lax.ppermute(x, axis, [(i, (i + by) % peers) for i in range(peers)])


def to_rows(slopes, row_block):
    blocks = [
        lax.dynamic_slice_in_dim(slopes, ROWS * ((row_block + ahead) % PEERS_Y), ROWS, 2)
        for ahead in range(PEERS_Y)
    ]
    arrived = [blocks[0]] + [from_behind(blocks[ahead], "gy", ahead) for ahead in range(1, PEERS_Y)]
    ordered = [
        lax.select_n((row_block - device) % PEERS_Y, *arrived) for device in range(PEERS_Y)
    ]
    return jnp.concatenate(ordered, 1).astype(f32)


def exchange(columns, rows):
    blocks = columns.astype(f16).reshape(256, rows, HALF)
    return lax.all_to_all(blocks, ("gz", "gy"), 0, 0, tiled=True)


def arrived(moved):
    return moved.reshape(-1, HALF).astype(f32)


def local(pressure, velocity, bulk, buoyancy, tiles, tile_corner, live_count):
    slab_index = lax.axis_index("gz")
    row_block = lax.axis_index("gy")
    here = row_block.reshape(1).astype(jnp.int32)
    device = (slab_index * PEERS_Y + row_block).astype(jnp.int32)
    place = jnp.stack([slab_index, row_block]).astype(jnp.int32)
    table = {key: jnp.asarray(value) for key, value in TABLES.items()}

    components = jnp.einsum(
        "cx,abx->cab",
        table["x_lines"],
        pressure.reshape(4, HALF, NX),
        precision=lax.Precision.HIGH,
    )
    velocity_later, buoyancy_later, tiles, slab_later, components = lax.optimization_barrier(
        (velocity, buoyancy, tiles, slab_index, components)
    )
    fields = jnp.concatenate([velocity_later, buoyancy_later[None]])
    sent = [
        (
            lax.dynamic_slice_in_dim(fields, 2 * ((row_block + ahead) % PEERS_Y), 2, 1) * FIELD_LINK
        ).astype(f16)
        for ahead in range(1, PEERS_Y)
    ]
    own = lax.dynamic_slice_in_dim(fields, 2 * row_block, 2, 1) * FIELD_LINK
    first, third = from_behind(sent[0], "gy", 1), from_behind(sent[2], "gy", 3)
    packed = tiles.reshape(SLOTS_HERE, 2 * SLAB, 8, HALF)
    moved, second, packed, packed_end = lax.optimization_barrier(
        (exchange(components, 4), sent[1], packed, packed[:, SLAB:])
    )
    (filtered,) = call(
        filter_out_kernel,
        "filter_out",
        [SMEM] + [VMEM] * 3,
        [
            device.reshape(1),
            arrived(moved),
            table["filter_out"],
            table["numbers"],
        ],
        [((2048, HALF), f32)],
        [VMEM],
        [((NZ, NY), f32)],
    )
    filtered, own, first, second, third, packed, packed_end = lax.optimization_barrier(
        (filtered, own, first, second, third, packed, packed_end)
    )
    second = from_behind(second, "gy", 2)
    tiles_before, tiles_second = from_behind(packed, "gz", 1), from_behind(packed_end, "gz", 2)
    corners = [
        lax.dynamic_slice_in_dim(
            tile_corner,
            ((slab_later - reach) % PEERS_Z * PEERS_Y + row_block) * SLOTS_HERE,
            SLOTS_HERE,
            0,
        )
        for reach in range(3)
    ]
    moved, *corners = lax.optimization_barrier((exchange(filtered, 8), *corners))
    slopes, middle = call(
        middle_kernel,
        "middle",
        [SMEM] + [VMEM] * 3 + [FAR] * 2,
        [
            here,
            arrived(moved),
            table["middle"],
            table["numbers"],
            jnp.stack([own, first.astype(f32), third.astype(f32)]) * (1.0 / FIELD_LINK),
            second.astype(f32) * (1.0 / FIELD_LINK),
        ],
        [((3, 2, NY, NX), f32), ((2048, HALF), f32)],
        [FAR, VMEM],
        [((3, 2, NY, NX), f32), ((4, 2, NY, NX), f32)],
        5,
    )
    middle, slopes, tiles_before, tiles_second = lax.optimization_barrier(
        (middle, slopes.astype(f16), tiles_before, tiles_second)
    )
    slopes = to_rows(slopes, row_block)
    new_velocity = (velocity * RETURN_LINK - buoyancy[None] * slopes) * (1.0 / RETURN_LINK)
    own, passed = call(
        source_kernel,
        "source",
        [SMEM] * 5 + [VMEM] * 4,
        [
            place,
            live_count,
            *corners,
            packed,
            tiles_before,
            tiles_second,
            pressure,
        ],
        [((SLAB, ROWS, NX), f32), ((SLAB, TILE, NX), bf16)],
        [VMEM] * 2,
        [((2 * SLAB, 256, NX), bf16), ((SLAB, 256, NX), bf16), ((2 * SLAB, 256, NX), bf16)],
    )
    (filtered_back,) = call(
        filter_back_kernel,
        "filter_back",
        [SMEM] + [VMEM] * 3,
        [
            device.reshape(1),
            arrived(exchange(middle, 8)),
            table["filter_back"],
            table["numbers"],
        ],
        [((1024, HALF), f32)],
        [VMEM],
    )
    passed = from_behind(passed, "gy", 1)
    filtered_back, own = lax.optimization_barrier((filtered_back, own))
    moved, new_velocity = lax.optimization_barrier((exchange(filtered_back, 4), new_velocity))
    (new_pressure,) = call(
        new_pressure_kernel,
        "new_pressure",
        [VMEM] * 5,
        [arrived(moved), table["x_waves"], bulk, own, passed],
        [((SLAB, ROWS, NX), f32)],
        [FAR],
        [((SLAB, ROWS, NX), f32)],
        4,
    )
    return (new_pressure, new_velocity)


def solution(mesh):
    in_specs = (
        P("gz", "gy", None),
        P(None, "gz", "gy", None),
        P("gz", "gy", None),
        P("gz", "gy", None),
        P(("gz", "gy"), None, None, None),
        P(),
        P(),
    )
    out_specs = (P("gz", "gy", None), P(None, "gz", "gy", None))
    return jax.shard_map(local, mesh=mesh, in_specs=in_specs, out_specs=out_specs, check_vma=False)
```
